32 devices in a mesh: dp: 8 (over z, y), mp: 4 (over x, core).
Axes of the slice: x: 2, y: 2, z: 4, core: 2. Of those that a mesh axis runs over, the one named last changes fastest.
Arguments:
- images: bfloat16 [4, 24, 16, 16, 1024], P(None, 'dp'), may hold values from -6 to 6
- image_size: int32 [4, 24, 2], P(None, 'dp'), may hold values from 8 to 16, as said below
- entry_weight: bfloat16 [1024, 512], P('dp', 'mp'), may hold values from -0.1875 to 0.1875
- entry_gain: float32 [512], P('mp'), may hold values from 0.25 to 1.75
- entry_shift: float32 [512], P('mp'), may hold values from -3 to 3
- stride_weight: bfloat16 [3, 3, 512, 512], P(None, None, 'dp', 'mp'), may hold values from -0.09375 to 0.09375
- stride_gain: float32 [512], P('mp'), may hold values from 0.25 to 1.75
- stride_shift: float32 [512], P('mp'), may hold values from -3 to 3
- expand_weight: bfloat16 [512, 2048], P('mp', 'dp'), may hold values from -0.25 to 0.25
- expand_gain: float32 [2048], P('mp'), may hold values from 0.25 to 1.75
- expand_shift: float32 [2048], P('mp'), may hold values from -3 to 3
- project_weight: bfloat16 [1024, 2048], P('dp', 'mp'), may hold values from -0.1875 to 0.1875
- project_gain: float32 [2048], P('mp'), may hold values from 0.25 to 1.75
- project_shift: float32 [2048], P('mp'), may hold values from -3 to 3
- squeeze_weight: bfloat16 [2048, 128], P('mp', 'dp'), may hold values from -0.5 to 0.5
- squeeze_bias: float32 [128], replicated, may hold values from -3 to 3
- excite_weight: bfloat16 [128, 2048], P('dp', 'mp'), may hold values from -0.5 to 0.5
- excite_bias: float32 [2048], P('mp'), may hold values from -3 to 3
- reduce_weight: bfloat16 [2048, 512], P('dp', 'mp'), may hold values from -0.125 to 0.125
- reduce_gain: float32 [512], P('mp'), may hold values from 0.25 to 1.75
- reduce_shift: float32 [512], P('mp'), may hold values from -3 to 3
- spatial_weight: bfloat16 [3, 3, 512, 512], P(None, None, 'dp', 'mp'), may hold values from -0.09375 to 0.09375
- spatial_gain: float32 [512], P('mp'), may hold values from 0.25 to 1.75
- spatial_shift: float32 [512], P('mp'), may hold values from -3 to 3
- widen_weight: bfloat16 [512, 2048], P('mp', 'dp'), may hold values from -0.25 to 0.25
- widen_gain: float32 [2048], P('mp'), may hold values from 0.25 to 1.75
- widen_shift: float32 [2048], P('mp'), may hold values from -3 to 3
- shrink_weight: bfloat16 [2048, 128], P('mp', 'dp'), may hold values from -0.5 to 0.5
- shrink_bias: float32 [128], replicated, may hold values from -3 to 3
- gating_weight: bfloat16 [128, 2048], P('dp', 'mp'), may hold values from -0.5 to 0.5
- gating_bias: float32 [2048], P('mp'), may hold values from -3 to 3
- cotangent: bfloat16 [4, 24, 8, 8, 2048], P(None, 'dp', None, None, 'mp'), may hold values from -6 to 6
Outputs:
- result: bfloat16 [4, 24, 8, 8, 2048], P(None, 'dp', None, None, 'mp')
- images_grad: float32 [4, 24, 16, 16, 1024], P(None, 'dp', None, None, 'mp')
- entry_weight_grad: float32 [1024, 512], P('dp', 'mp')
- entry_gain_grad: float32 [512], P('mp')
- entry_shift_grad: float32 [512], P('mp')
- stride_weight_grad: float32 [3, 3, 512, 512], P(None, None, 'dp', 'mp')
- stride_gain_grad: float32 [512], P('mp')
- stride_shift_grad: float32 [512], P('mp')
- expand_weight_grad: float32 [512, 2048], P('mp', 'dp')
- expand_gain_grad: float32 [2048], P('mp')
- expand_shift_grad: float32 [2048], P('mp')
- project_weight_grad: float32 [1024, 2048], P('dp', 'mp')
- project_gain_grad: float32 [2048], P('mp')
- project_shift_grad: float32 [2048], P('mp')
- squeeze_weight_grad: float32 [2048, 128], P('mp', 'dp')
- squeeze_bias_grad: float32 [128], replicated
- excite_weight_grad: float32 [128, 2048], P('dp', 'mp')
- excite_bias_grad: float32 [2048], P('mp')
- reduce_weight_grad: float32 [2048, 512], P('dp', 'mp')
- reduce_gain_grad: float32 [512], P('mp')
- reduce_shift_grad: float32 [512], P('mp')
- spatial_weight_grad: float32 [3, 3, 512, 512], P(None, None, 'dp', 'mp')
- spatial_gain_grad: float32 [512], P('mp')
- spatial_shift_grad: float32 [512], P('mp')
- widen_weight_grad: float32 [512, 2048], P('mp', 'dp')
- widen_gain_grad: float32 [2048], P('mp')
- widen_shift_grad: float32 [2048], P('mp')
- shrink_weight_grad: float32 [2048, 128], P('mp', 'dp')
- shrink_bias_grad: float32 [128], replicated
- gating_weight_grad: float32 [128, 2048], P('dp', 'mp')
- gating_bias_grad: float32 [2048], P('mp')
The draws below stay inside these ranges and needn't reach their ends.
Inputs may be any that keep to these rules, and one draw needn't show every extreme that they name: `image_size`: each image's content fills its top left corner of height by width pixels; the rest is padding. In every micro-batch one image is 16 by 16 and another is 8 by 8.
All inputs are finite; a program needn't handle non-finite values.
Results may differ from the reference program's by a relative error of at most 0.025.
Values may be sent and summed in bfloat16 or wider, within the bound.
A program may use at most 192 MiB of HBM per device.

```python
import jax
import jax.numpy as jnp
from jax import lax

CIN = 1024
BOT = 512
COUT = 2048
SEH = 128
SIDE = 16
MICRO = 4
IMAGES = 24
HALF = 8


def draw_image_size(key, part):
    key = jax.random.fold_in(key, 11)
    first_key, second_key, third_key = jax.random.split(key, 3)
    sides = jax.random.randint(first_key, (MICRO, IMAGES, 2), SIDE // 2, SIDE + 1, dtype=jnp.int32)
    largest = jax.random.randint(second_key, (MICRO,), 0, IMAGES, dtype=jnp.int32)
    smallest = (largest + 1 + jax.random.randint(third_key, (MICRO,), 0, IMAGES - 1, dtype=jnp.int32)) % IMAGES
    order = jnp.arange(IMAGES, dtype=jnp.int32)
    sides = jnp.where((order[None, :] == largest[:, None])[..., None], SIDE, sides)
    sides = jnp.where((order[None, :] == smallest[:, None])[..., None], SIDE // 2, sides)
    return sides.astype(jnp.int32)


def spiked(values, key, source, target, blocks, factor):
    def block_of(dim):
        return (jnp.arange(values.shape[dim]) // (values.shape[dim] // blocks)).reshape((-1,) + (1,) * (values.ndim - 1 - dim))

    first = jax.random.permutation(key, blocks)[block_of(target)]
    far = (block_of(target) + blocks // 2) % blocks
    return jnp.where((block_of(source) == first) | (block_of(source) == far), factor * values, values)


def steps_of(key, dims, shards, low, top_value):
    def one(position, parts):
        heights = jax.random.uniform(jax.random.fold_in(jax.random.fold_in(key, 6), position), (parts,), jnp.float32, low / len(shards), top_value / len(shards))
        return jnp.repeat(jnp.exp(heights), dims[position] // parts).reshape((-1,) + (1,) * (len(dims) - position - 1))

    loudness = one(*shards[0])
    for cut in shards[1:]:
        loudness = loudness * one(*cut)
    return loudness


def bell_draw(own_key, extent, spread, most, cuts=(), held_as=jnp.bfloat16):
    values = jax.random.normal(own_key, extent, jnp.float32) * spread
    if len(cuts) > 0:
        values = steps_of(own_key, extent, cuts, -0.22, 0.18) * values
    return jnp.clip(values, min=-most, max=most).astype(held_as)


def noise_with(own_key, shape, deviation, most, cuts, heavy, kind=jnp.bfloat16):
    result = deviation * jax.random.normal(own_key, shape, jnp.float32)
    if cuts:
        result = result * steps_of(own_key, shape, cuts, -0.22, 0.18)
    return jnp.clip(spiked(result, jax.random.fold_in(own_key, 3), *heavy), -most, most).astype(kind)


def setup_inputs(seed: int = 0) -> dict:
    keys = jax.random.split(jax.random.key(seed), 33)
    images = bell_draw(keys[0], (MICRO, IMAGES, SIDE, SIDE, CIN), 1.0, 6.0, ((1, 8),))
    image_size = draw_image_size(jax.random.fold_in(keys[32], 71), 0)
    entry_weight = bell_draw(keys[2], (CIN, BOT), CIN ** -0.5, 0.1875, ((0, 8), (1, 4)))
    entry_gain = jnp.clip(1.0 + 0.15 * jax.random.normal(keys[3], (BOT,), jnp.float32), 0.25, 1.75)
    entry_shift = bell_draw(keys[4], (BOT,), 0.5, 3.0, ((0, 4),), jnp.float32)
    stride_weight = bell_draw(keys[5], (3, 3, BOT, BOT), (9 * BOT) ** -0.5, 0.09375, ((2, 8), (3, 4)))
    stride_gain = jnp.clip(1.0 + 0.15 * jax.random.normal(keys[6], (BOT,), jnp.float32), 0.25, 1.75)
    stride_shift = bell_draw(keys[7], (BOT,), 0.5, 3.0, ((0, 4),), jnp.float32)
    expand_weight = bell_draw(keys[8], (BOT, COUT), BOT ** -0.5, 0.25, ((0, 4), (1, 8)))
    expand_gain = jnp.clip(1.0 + 0.15 * jax.random.normal(keys[9], (COUT,), jnp.float32), 0.25, 1.75)
    expand_shift = bell_draw(keys[10], (COUT,), 0.5, 3.0, ((0, 4),), jnp.float32)
    project_weight = bell_draw(keys[11], (CIN, COUT), CIN ** -0.5, 0.1875, ((0, 8), (1, 4)))
    project_gain = jnp.clip(1.0 + 0.15 * jax.random.normal(keys[12], (COUT,), jnp.float32), 0.25, 1.75)
    project_shift = bell_draw(keys[13], (COUT,), 0.5, 3.0, ((0, 4),), jnp.float32)
    squeeze_weight = bell_draw(keys[14], (COUT, SEH), (COUT // 16) ** -0.5, 0.5, ((0, 4), (1, 8)))
    squeeze_bias = bell_draw(keys[15], (SEH,), 0.5, 3.0, (), jnp.float32)
    excite_weight = bell_draw(keys[16], (SEH, COUT), SEH ** -0.5, 0.5, ((0, 8), (1, 4)))
    excite_bias = bell_draw(keys[17], (COUT,), 0.5, 3.0, ((0, 4),), jnp.float32)
    reduce_weight = bell_draw(keys[18], (COUT, BOT), COUT ** -0.5, 0.125, ((0, 8), (1, 4)))
    reduce_gain = jnp.clip(1.0 + 0.15 * jax.random.normal(keys[19], (BOT,), jnp.float32), 0.25, 1.75)
    reduce_shift = bell_draw(keys[20], (BOT,), 0.5, 3.0, ((0, 4),), jnp.float32)
    spatial_weight = bell_draw(keys[21], (3, 3, BOT, BOT), (9 * BOT) ** -0.5, 0.09375, ((2, 8), (3, 4)))
    spatial_gain = jnp.clip(1.0 + 0.15 * jax.random.normal(keys[22], (BOT,), jnp.float32), 0.25, 1.75)
    spatial_shift = bell_draw(keys[23], (BOT,), 0.5, 3.0, ((0, 4),), jnp.float32)
    widen_weight = bell_draw(keys[24], (BOT, COUT), BOT ** -0.5, 0.25, ((0, 4), (1, 8)))
    widen_gain = jnp.clip(1.0 + 0.15 * jax.random.normal(keys[25], (COUT,), jnp.float32), 0.25, 1.75)
    widen_shift = bell_draw(keys[26], (COUT,), 0.5, 3.0, ((0, 4),), jnp.float32)
    shrink_weight = bell_draw(keys[27], (COUT, SEH), (COUT // 16) ** -0.5, 0.5, ((0, 4), (1, 8)))
    shrink_bias = bell_draw(keys[28], (SEH,), 0.5, 3.0, (), jnp.float32)
    gating_weight = bell_draw(keys[29], (SEH, COUT), SEH ** -0.5, 0.5, ((0, 8), (1, 4)))
    gating_bias = bell_draw(keys[30], (COUT,), 0.5, 3.0, ((0, 4),), jnp.float32)
    cotangent = noise_with(keys[31], (MICRO, IMAGES, HALF, HALF, COUT), 1.0, 6.0, ((1, 8), (4, 4)), (1, 4, 8, 2.0))
    return dict(images=images, image_size=image_size, entry_weight=entry_weight, entry_gain=entry_gain, entry_shift=entry_shift, stride_weight=stride_weight, stride_gain=stride_gain, stride_shift=stride_shift, expand_weight=expand_weight, expand_gain=expand_gain, expand_shift=expand_shift, project_weight=project_weight, project_gain=project_gain, project_shift=project_shift, squeeze_weight=squeeze_weight, squeeze_bias=squeeze_bias, excite_weight=excite_weight, excite_bias=excite_bias, reduce_weight=reduce_weight, reduce_gain=reduce_gain, reduce_shift=reduce_shift, spatial_weight=spatial_weight, spatial_gain=spatial_gain, spatial_shift=spatial_shift, widen_weight=widen_weight, widen_gain=widen_gain, widen_shift=widen_shift, shrink_weight=shrink_weight, shrink_bias=shrink_bias, gating_weight=gating_weight, gating_bias=gating_bias, cotangent=cotangent)


eps_norm = 1e-05
highest = lax.Precision.HIGHEST

@jax.custom_vjp
def low(v):
    return lax.optimization_barrier(v.astype(jnp.bfloat16)).astype(jnp.float32)

@jax.custom_vjp
def low_back(v):
    return v

def low_keep(v):
    return (low(v), None)

def low_pass(kept, grad):
    return (grad,)

def back_keep(v):
    return (v, None)

def back_low(kept, grad):
    return (low(grad),)
low.defvjp(low_keep, low_pass)
low_back.defvjp(back_keep, back_low)

def pixel_masks(sizes, side):
    half = side // 2
    height = sizes[:, 0]
    breadth = sizes[:, 1]
    places = jnp.arange(side, dtype=jnp.int32)
    inside = ((places[None, :, None] < height[:, None, None]) & (places[None, None, :] < breadth[:, None, None])).astype(jnp.float32)
    halves = jnp.arange(half, dtype=jnp.int32)
    reduced = ((halves[None, :, None] < ((height + 1) // 2)[:, None, None]) & (halves[None, None, :] < ((breadth + 1) // 2)[:, None, None])).astype(jnp.float32)
    return (inside, reduced)

def spatial_taps(field, stride):
    count, side, channels = (field.shape[0], field.shape[1], field.shape[3])
    reach = stride * (side // stride - 1) + 1
    padded = jnp.pad(field, ((0, 0), (1, 1), (1, 1), (0, 0)))
    pieces = []
    for row in range(3):
        for column in range(3):
            pieces.append(lax.slice(padded, (0, row, column, 0), (count, row + reach, column + reach, channels), (1, stride, stride, 1)))
    return jnp.concatenate(pieces, axis=3)

def convolve(field, kernel):
    flat = jnp.dot(field.reshape(-1, field.shape[-1]), kernel, precision=highest)
    return flat.reshape(field.shape[:-1] + (kernel.shape[1],))

def spatial(field, kernel, stride):
    return convolve(spatial_taps(field, stride), kernel.reshape(-1, kernel.shape[3]))

def normalize(field, mask, gain, shift):
    weights = mask[..., None]
    total = jnp.sum(mask)
    mean = lax.optimization_barrier(jnp.sum(field * weights, axis=(0, 1, 2))) / total
    second = lax.optimization_barrier(jnp.sum(field * field * weights, axis=(0, 1, 2))) / total
    return (field - mean) * lax.rsqrt(second - mean * mean + eps_norm) * gain + shift

def excitation(field, mask, squeeze, squeeze_bias, excite, excite_bias):
    pixels = lax.optimization_barrier(jnp.sum(mask, axis=(1, 2)))
    pooled = lax.optimization_barrier(jnp.sum(field * mask[..., None], axis=(1, 2))) / pixels[:, None]
    hidden = jax.nn.silu(jnp.dot(pooled, squeeze, precision=highest) + squeeze_bias)
    scale = jax.nn.sigmoid(jnp.dot(hidden, excite, precision=highest) + excite_bias)
    return field * scale[:, None, None, :]

def first_block(picture, inside, reduced, weights):
    entry_weight, entry_gain, entry_shift, stride_weight, stride_gain, stride_shift, expand_weight, expand_gain, expand_shift, project_weight, project_gain, project_shift, squeeze_weight, squeeze_bias, excite_weight, excite_bias = weights
    entry = low_back(convolve(picture, entry_weight))
    entry_act = low(jax.nn.silu(normalize(entry, inside, entry_gain, entry_shift)) * inside[..., None])
    strided = low_back(spatial(entry_act, stride_weight, 2))
    stride_act = low(jax.nn.silu(normalize(strided, reduced, stride_gain, stride_shift)) * reduced[..., None])
    expanded = low_back(convolve(stride_act, expand_weight))
    branch = excitation(normalize(expanded, reduced, expand_gain, expand_shift), reduced, squeeze_weight, squeeze_bias, excite_weight, excite_bias)
    projected = low_back(convolve(picture[:, ::2, ::2, :], project_weight))
    shortcut = normalize(projected, reduced, project_gain, project_shift)
    return low(jax.nn.silu(branch + shortcut) * reduced[..., None])

def second_block(first, reduced, weights):
    reduce_weight, reduce_gain, reduce_shift, spatial_weight, spatial_gain, spatial_shift, widen_weight, widen_gain, widen_shift, shrink_weight, shrink_bias, gating_weight, gating_bias = weights
    narrowed = low_back(convolve(first, reduce_weight))
    reduce_act = low(jax.nn.silu(normalize(narrowed, reduced, reduce_gain, reduce_shift)) * reduced[..., None])
    mixed = low_back(spatial(reduce_act, spatial_weight, 1))
    spatial_act = low(jax.nn.silu(normalize(mixed, reduced, spatial_gain, spatial_shift)) * reduced[..., None])
    widened = low_back(convolve(spatial_act, widen_weight))
    branch = excitation(normalize(widened, reduced, widen_gain, widen_shift), reduced, shrink_weight, shrink_bias, gating_weight, gating_bias)
    return jax.nn.silu(branch + first) * reduced[..., None]

def reference(images, image_size, entry_weight, entry_gain, entry_shift, stride_weight, stride_gain, stride_shift, expand_weight, expand_gain, expand_shift, project_weight, project_gain, project_shift, squeeze_weight, squeeze_bias, excite_weight, excite_bias, reduce_weight, reduce_gain, reduce_shift, spatial_weight, spatial_gain, spatial_shift, widen_weight, widen_gain, widen_shift, shrink_weight, shrink_bias, gating_weight, gating_bias, cotangent):
    params = tuple((value.astype(jnp.float32) for value in (entry_weight, entry_gain, entry_shift, stride_weight, stride_gain, stride_shift, expand_weight, expand_gain, expand_shift, project_weight, project_gain, project_shift, squeeze_weight, squeeze_bias, excite_weight, excite_bias, reduce_weight, reduce_gain, reduce_shift, spatial_weight, spatial_gain, spatial_shift, widen_weight, widen_gain, widen_shift, shrink_weight, shrink_bias, gating_weight, gating_bias)))

    def micro_step(carry, batch):
        picture, sizes, seed_grad = batch
        inside, reduced = pixel_masks(sizes, SIDE)

        def network(weights, picture_value):
            first = first_block(picture_value, inside, reduced, weights[:16])
            return second_block(first, reduced, weights[16:])
        output, pullback = jax.vjp(network, params, picture.astype(jnp.float32))
        weight_grads, picture_grad = pullback(seed_grad.astype(jnp.float32))
        carry = jax.tree.map(jnp.add, carry, weight_grads)
        return (carry, (output.astype(jnp.bfloat16), picture_grad))
    zeros = jax.tree.map(jnp.zeros_like, params)
    totals, (outputs, picture_grads) = lax.scan(micro_step, zeros, (images, image_size, cotangent))
    return (outputs, picture_grads, totals[0], totals[1], totals[2], totals[3], totals[4], totals[5], totals[6], totals[7], totals[8], totals[9], totals[10], totals[11], totals[12], totals[13], totals[14], totals[15], totals[16], totals[17], totals[18], totals[19], totals[20], totals[21], totals[22], totals[23], totals[24], totals[25], totals[26], totals[27], totals[28])
```

```python
import jax
import jax.numpy as jnp
from jax import lax
from jax.sharding import PartitionSpec as P

eps_norm = 1e-05
highest = lax.Precision.HIGHEST


def matmul(left, right):
    return jnp.dot(left, right, preferred_element_type=jnp.float32)


def contract_rows(left, right):
    return lax.dot_general(
        left, right, (((0,), (0,)), ((), ())), preferred_element_type=jnp.float32
    )


def contract_cols(left, right):
    return lax.dot_general(
        left, right, (((1,), (1,)), ((), ())), preferred_element_type=jnp.float32
    )


def swish_slope(value):
    sigma = jax.nn.sigmoid(value)
    return sigma * (1.0 + value * (1.0 - sigma))


def pixel_masks(sizes, side):
    half = side // 2
    height = sizes[:, 0]
    breadth = sizes[:, 1]
    places = jnp.arange(side, dtype=jnp.int32)
    inside = (
        (places[None, :, None] < height[:, None, None])
        & (places[None, None, :] < breadth[:, None, None])
    ).astype(jnp.float32)
    halves = jnp.arange(half, dtype=jnp.int32)
    reduced = (
        (halves[None, :, None] < ((height + 1) // 2)[:, None, None])
        & (halves[None, None, :] < ((breadth + 1) // 2)[:, None, None])
    ).astype(jnp.float32)
    return (inside, reduced)


def spatial_taps(field, stride):
    count, side, channels = (field.shape[0], field.shape[1], field.shape[3])
    reach = stride * (side // stride - 1) + 1
    padded = jnp.pad(field, ((0, 0), (1, 1), (1, 1), (0, 0)))
    pieces = []
    for row in range(3):
        for column in range(3):
            pieces.append(
                lax.slice(
                    padded,
                    (0, row, column, 0),
                    (count, row + reach, column + reach, channels),
                    (1, stride, stride, 1),
                )
            )
    return jnp.concatenate(pieces, axis=3)


def untap(grads, stride, side):
    count, out_side = (grads.shape[0], grads.shape[1])
    channels = grads.shape[3] // 9
    reach = stride * (out_side - 1) + 1
    total = jnp.zeros((count, side + 2, side + 2, channels), jnp.float32)
    for row in range(3):
        for column in range(3):
            first = (row * 3 + column) * channels
            piece = grads[:, :, :, first : first + channels]
            total = total + lax.pad(
                piece,
                jnp.float32(0.0),
                (
                    (0, 0, 0),
                    (row, side + 2 - row - reach, stride - 1),
                    (column, side + 2 - column - reach, stride - 1),
                    (0, 0, 0),
                ),
            )
    return total[:, 1 : side + 1, 1 : side + 1, :]


def batch_statistics(fields, mask):
    weights = mask[..., None]
    terms = []
    for field in fields:
        terms.append(jnp.sum(field * weights, axis=(0, 1, 2)))
        terms.append(jnp.sum(field * field * weights, axis=(0, 1, 2)))
    packed, total_vector = lax.psum((jnp.concatenate(terms), jnp.sum(mask).reshape(1)), "dp")
    total = total_vector[0]
    result = []
    offset = 0
    for field in fields:
        breadth = field.shape[3]
        mean = packed[offset : offset + breadth] / total
        second = packed[offset + breadth : offset + 2 * breadth] / total
        result.append((mean, lax.rsqrt(second - mean * mean + eps_norm)))
        offset = offset + 2 * breadth
    return (result, total)


def standardize(raw, statistics, gain, shift):
    mean, scale = statistics
    normed = (raw - mean) * scale
    return (normed, normed * gain + shift)


def batch_backward(grads, normeds, scales, gains, mask, total, extras):
    terms = []
    for grad, normed in zip(grads, normeds):
        terms.append(jnp.sum(grad * normed, axis=(0, 1, 2)))
        terms.append(jnp.sum(grad, axis=(0, 1, 2)))
    for extra in extras:
        terms.append(extra)
    packed = lax.psum(jnp.concatenate(terms), "dp")
    results = []
    pairs = []
    offset = 0
    for grad, normed, scale, gain in zip(grads, normeds, scales, gains):
        breadth = grad.shape[3]
        gain_grad = packed[offset : offset + breadth]
        shift_grad = packed[offset + breadth : offset + 2 * breadth]
        offset = offset + 2 * breadth
        results.append(
            scale * gain * (grad - mask[..., None] * (shift_grad + normed * gain_grad) / total)
        )
        pairs.append((gain_grad, shift_grad))
    rest = []
    for extra in extras:
        rest.append(packed[offset : offset + extra.shape[0]])
        offset = offset + extra.shape[0]
    return (results, pairs, rest)


def excite_forward(field, mask, pixels, squeeze_full, squeeze_bias, excite_full, excite_bias):
    pooled = jnp.sum(field * mask[..., None], axis=(1, 2)) / pixels[:, None]
    inner_pre = (
        jnp.dot(pooled, squeeze_full.astype(jnp.float32), precision=highest) + squeeze_bias
    )
    hidden = jax.nn.silu(inner_pre)
    scale = jax.nn.sigmoid(
        jnp.dot(hidden, excite_full.astype(jnp.float32), precision=highest) + excite_bias
    )
    return (pooled, inner_pre, hidden, scale)


def excite_backward(grad_branch, field, mask, pixels, saved, squeeze_full, excite_full):
    pooled, inner_pre, hidden, scale = saved
    grad_scale = jnp.sum(grad_branch * field, axis=(1, 2))
    grad_gate = grad_scale * scale * (1.0 - scale)
    excite_grad = jnp.dot(hidden.T, grad_gate, precision=highest)
    grad_hidden = jnp.dot(grad_gate, excite_full.astype(jnp.float32).T, precision=highest)
    grad_inner = grad_hidden * swish_slope(inner_pre)
    squeeze_grad = jnp.dot(pooled.T, grad_inner, precision=highest)
    grad_pooled = jnp.dot(grad_inner, squeeze_full.astype(jnp.float32).T, precision=highest)
    grad_field = (
        grad_branch * scale[:, None, None, :]
        + grad_pooled[:, None, None, :] * mask[..., None] / pixels[:, None, None, None]
    )
    return (
        grad_field,
        squeeze_grad,
        excite_grad,
        jnp.sum(grad_inner, axis=0),
        jnp.sum(grad_gate, axis=0),
    )


def whole_vector(value):
    return lax.all_gather(value, "mp", axis=0, tiled=True)


def whole_matrix(value, dp_axis, mp_axis):
    value = lax.all_gather(value, "dp", axis=dp_axis, tiled=True)
    return lax.all_gather(value, "mp", axis=mp_axis, tiled=True)


def own_part(value, dp_axis, mp_axis):
    value = lax.psum_scatter(
        value.astype(jnp.bfloat16), "mp", scatter_dimension=mp_axis, tiled=True
    )
    return lax.psum_scatter(value, "dp", scatter_dimension=dp_axis, tiled=True).astype(
        jnp.float32
    )


def shards(
    images,
    image_size,
    entry_weight,
    entry_gain,
    entry_shift,
    stride_weight,
    stride_gain,
    stride_shift,
    expand_weight,
    expand_gain,
    expand_shift,
    project_weight,
    project_gain,
    project_shift,
    squeeze_weight,
    squeeze_bias,
    excite_weight,
    excite_bias,
    reduce_weight,
    reduce_gain,
    reduce_shift,
    spatial_weight,
    spatial_gain,
    spatial_shift,
    widen_weight,
    widen_gain,
    widen_shift,
    shrink_weight,
    shrink_bias,
    gating_weight,
    gating_bias,
    cotangent,
):
    place = lax.axis_index("mp")
    count, side = (images.shape[1], images.shape[2])
    half = side // 2
    channels_in = images.shape[4]
    entry_full = whole_matrix(entry_weight, 0, 1)
    stride_full = whole_matrix(stride_weight, 2, 3)
    expand_full = whole_matrix(expand_weight, 1, 0)
    project_full = whole_matrix(project_weight, 0, 1)
    squeeze_full = whole_matrix(squeeze_weight, 1, 0)
    excite_full = whole_matrix(excite_weight, 0, 1)
    reduce_full = whole_matrix(reduce_weight, 0, 1)
    spatial_full = whole_matrix(spatial_weight, 2, 3)
    widen_full = whole_matrix(widen_weight, 1, 0)
    shrink_full = whole_matrix(shrink_weight, 1, 0)
    gating_full = whole_matrix(gating_weight, 0, 1)
    entry_gain, entry_shift = whole_vector(entry_gain), whole_vector(entry_shift)
    stride_gain, stride_shift = whole_vector(stride_gain), whole_vector(stride_shift)
    expand_gain, expand_shift = whole_vector(expand_gain), whole_vector(expand_shift)
    project_gain, project_shift = whole_vector(project_gain), whole_vector(project_shift)
    reduce_gain, reduce_shift = whole_vector(reduce_gain), whole_vector(reduce_shift)
    spatial_gain, spatial_shift = whole_vector(spatial_gain), whole_vector(spatial_shift)
    widen_gain, widen_shift = whole_vector(widen_gain), whole_vector(widen_shift)
    excite_bias, gating_bias = whole_vector(excite_bias), whole_vector(gating_bias)
    seed_grad = lax.all_to_all(cotangent, "mp", split_axis=0, concat_axis=4, tiled=True)[0]
    picture = lax.dynamic_index_in_dim(images, place, 0, keepdims=False)
    sizes = lax.dynamic_index_in_dim(image_size, place, 0, keepdims=False)
    inside, reduced = pixel_masks(sizes, side)
    pixels = jnp.sum(reduced, axis=(1, 2))
    reduced_mask = reduced[..., None]
    entry_raw = matmul(picture.reshape(-1, channels_in), entry_full).reshape(
        count, side, side, -1
    )
    stats, inside_total = batch_statistics([entry_raw], inside)
    entry_stats = stats[0]
    entry_normed, entry_pre = standardize(entry_raw, entry_stats, entry_gain, entry_shift)
    entry_act = (jax.nn.silu(entry_pre) * inside[..., None]).astype(jnp.bfloat16)
    entry_wide = entry_act
    bottleneck = entry_wide.shape[3]
    stride_taps = spatial_taps(entry_wide, 2).reshape(-1, 9 * bottleneck)
    stride_raw = matmul(stride_taps, stride_full.reshape(9 * bottleneck, -1)).reshape(
        count, half, half, -1
    )
    stats, reduced_total = batch_statistics([stride_raw], reduced)
    stride_stats = stats[0]
    stride_normed, stride_pre = standardize(stride_raw, stride_stats, stride_gain, stride_shift)
    stride_act = (jax.nn.silu(stride_pre) * reduced_mask).astype(jnp.bfloat16)
    local_bottleneck = stride_act.shape[3]
    stride_flat = stride_act.reshape(-1, local_bottleneck)
    expand_raw = matmul(stride_flat, expand_full).reshape(count, half, half, -1)
    strided_flat = picture[:, ::2, ::2, :].reshape(-1, channels_in)
    project_raw = matmul(strided_flat, project_full).reshape(count, half, half, -1)
    stats, reduced_total = batch_statistics([expand_raw, project_raw], reduced)
    expand_stats, project_stats = (stats[0], stats[1])
    expand_normed, expand_pre = standardize(expand_raw, expand_stats, expand_gain, expand_shift)
    project_normed, project_pre = standardize(
        project_raw, project_stats, project_gain, project_shift
    )
    first_saved = excite_forward(
        expand_pre, reduced, pixels, squeeze_full, squeeze_bias, excite_full, excite_bias
    )
    first_sum = expand_pre * first_saved[3][:, None, None, :] + project_pre
    first_out = (jax.nn.silu(first_sum) * reduced_mask).astype(jnp.bfloat16)
    block_wide = first_out
    block_flat = block_wide.reshape(-1, block_wide.shape[3])
    reduce_raw = matmul(block_flat, reduce_full).reshape(count, half, half, -1)
    stats, reduced_total = batch_statistics([reduce_raw], reduced)
    reduce_stats = stats[0]
    reduce_normed, reduce_pre = standardize(reduce_raw, reduce_stats, reduce_gain, reduce_shift)
    reduce_act = (jax.nn.silu(reduce_pre) * reduced_mask).astype(jnp.bfloat16)
    reduce_wide = reduce_act
    second_taps = spatial_taps(reduce_wide, 1).reshape(-1, 9 * bottleneck)
    spatial_raw = matmul(second_taps, spatial_full.reshape(9 * bottleneck, -1)).reshape(
        count, half, half, -1
    )
    stats, reduced_total = batch_statistics([spatial_raw], reduced)
    spatial_stats = stats[0]
    spatial_normed, spatial_pre = standardize(
        spatial_raw, spatial_stats, spatial_gain, spatial_shift
    )
    spatial_act = (jax.nn.silu(spatial_pre) * reduced_mask).astype(jnp.bfloat16)
    spatial_flat = spatial_act.reshape(-1, local_bottleneck)
    widen_raw = matmul(spatial_flat, widen_full).reshape(count, half, half, -1)
    stats, reduced_total = batch_statistics([widen_raw], reduced)
    widen_stats = stats[0]
    widen_normed, widen_pre = standardize(widen_raw, widen_stats, widen_gain, widen_shift)
    second_saved = excite_forward(
        widen_pre, reduced, pixels, shrink_full, shrink_bias, gating_full, gating_bias
    )
    second_sum = widen_pre * second_saved[3][:, None, None, :] + first_out.astype(jnp.float32)
    output = (jax.nn.silu(second_sum) * reduced_mask).astype(jnp.bfloat16)
    second_grad = seed_grad.astype(jnp.float32) * reduced_mask * swish_slope(second_sum)
    widen_grad, shrink_grad, gating_grad, shrink_bias_grad, gating_bias_grad = excite_backward(
        second_grad, widen_pre, reduced, pixels, second_saved, shrink_full, gating_full
    )
    grads, widen_pair, extras = batch_backward(
        [widen_grad],
        [widen_normed],
        [widen_stats[1]],
        [widen_gain],
        reduced,
        reduced_total,
        (shrink_bias_grad, gating_bias_grad),
    )
    widen_pair = widen_pair[0]
    shrink_bias_total, gating_bias_total = (extras[0], extras[1])
    widen_local = grads[0].astype(jnp.bfloat16)
    widen_low = widen_local
    widen_flat = widen_low.reshape(-1, widen_low.shape[3])
    widen_weight_grad = contract_rows(spatial_flat, widen_flat)
    spatial_act_grad = contract_cols(widen_flat, widen_full).reshape(count, half, half, -1)
    spatial_grad = spatial_act_grad * reduced_mask * swish_slope(spatial_pre)
    grads, spatial_pair, extras = batch_backward(
        [spatial_grad],
        [spatial_normed],
        [spatial_stats[1]],
        [spatial_gain],
        reduced,
        reduced_total,
        (),
    )
    spatial_pair = spatial_pair[0]
    spatial_low = grads[0].astype(jnp.bfloat16).reshape(-1, local_bottleneck)
    spatial_weight_grad = contract_rows(second_taps, spatial_low).reshape(
        3, 3, bottleneck, local_bottleneck
    )
    second_tap_grad = contract_cols(spatial_low, spatial_full.reshape(9 * bottleneck, -1))
    reduce_act_grad = untap(second_tap_grad.reshape(count, half, half, -1), 1, half)
    reduce_grad = reduce_act_grad * reduced_mask * swish_slope(reduce_pre)
    grads, reduce_pair, extras = batch_backward(
        [reduce_grad],
        [reduce_normed],
        [reduce_stats[1]],
        [reduce_gain],
        reduced,
        reduced_total,
        (),
    )
    reduce_pair = reduce_pair[0]
    reduce_low = grads[0].astype(jnp.bfloat16).reshape(-1, local_bottleneck)
    reduce_weight_grad = contract_rows(block_flat, reduce_low)
    first_partial = contract_cols(reduce_low, reduce_full).reshape(count, half, half, -1)
    first_out_grad = first_partial + second_grad
    first_grad = first_out_grad * reduced_mask * swish_slope(first_sum)
    expand_grad, squeeze_grad, excite_grad, squeeze_bias_grad, excite_bias_grad = (
        excite_backward(
            first_grad, expand_pre, reduced, pixels, first_saved, squeeze_full, excite_full
        )
    )
    grads, pairs, extras = batch_backward(
        [expand_grad, first_grad],
        [expand_normed, project_normed],
        [expand_stats[1], project_stats[1]],
        [expand_gain, project_gain],
        reduced,
        reduced_total,
        (squeeze_bias_grad, excite_bias_grad),
    )
    expand_pair, project_pair = (pairs[0], pairs[1])
    squeeze_bias_total, excite_bias_total = (extras[0], extras[1])
    expand_local = grads[0].astype(jnp.bfloat16)
    expand_low = expand_local
    expand_flat = expand_low.reshape(-1, expand_low.shape[3])
    expand_weight_grad = contract_rows(stride_flat, expand_flat)
    stride_act_grad = contract_cols(expand_flat, expand_full).reshape(count, half, half, -1)
    project_low = grads[1].astype(jnp.bfloat16).reshape(-1, grads[1].shape[3])
    project_weight_grad = contract_rows(strided_flat, project_low)
    strided_grad = contract_cols(project_low, project_full).reshape(
        count, half, half, channels_in
    )
    stride_grad = stride_act_grad * reduced_mask * swish_slope(stride_pre)
    grads, stride_pair, extras = batch_backward(
        [stride_grad],
        [stride_normed],
        [stride_stats[1]],
        [stride_gain],
        reduced,
        reduced_total,
        (),
    )
    stride_pair = stride_pair[0]
    stride_low = grads[0].astype(jnp.bfloat16).reshape(-1, local_bottleneck)
    stride_weight_grad = contract_rows(stride_taps, stride_low).reshape(
        3, 3, bottleneck, local_bottleneck
    )
    first_tap_grad = contract_cols(stride_low, stride_full.reshape(9 * bottleneck, -1))
    entry_act_grad = untap(first_tap_grad.reshape(count, half, half, -1), 2, side)
    entry_grad = entry_act_grad * inside[..., None] * swish_slope(entry_pre)
    grads, entry_pair, extras = batch_backward(
        [entry_grad], [entry_normed], [entry_stats[1]], [entry_gain], inside, inside_total, ()
    )
    entry_pair = entry_pair[0]
    entry_low = grads[0].astype(jnp.bfloat16).reshape(-1, local_bottleneck)
    entry_weight_grad = contract_rows(picture.reshape(-1, channels_in), entry_low)
    picture_partial = contract_cols(entry_low, entry_full).reshape(
        count, side, side, channels_in
    )
    picture_partial = picture_partial + lax.pad(
        strided_grad, jnp.float32(0.0), ((0, 0, 0), (0, 1, 1), (0, 1, 1), (0, 0, 0))
    )

    def own_vector(value):
        return lax.psum_scatter(value, "mp", scatter_dimension=0, tiled=True)

    picture_grad = lax.all_to_all(
        picture_partial.astype(jnp.bfloat16)[None], "mp", split_axis=4, concat_axis=0, tiled=True
    ).astype(jnp.float32)
    result = lax.all_to_all(output[None], "mp", split_axis=4, concat_axis=0, tiled=True)
    return (
        result,
        picture_grad,
        own_part(entry_weight_grad, 0, 1),
        own_vector(entry_pair[0]),
        own_vector(entry_pair[1]),
        own_part(stride_weight_grad, 2, 3),
        own_vector(stride_pair[0]),
        own_vector(stride_pair[1]),
        own_part(expand_weight_grad, 1, 0),
        own_vector(expand_pair[0]),
        own_vector(expand_pair[1]),
        own_part(project_weight_grad, 0, 1),
        own_vector(project_pair[0]),
        own_vector(project_pair[1]),
        own_part(squeeze_grad, 1, 0),
        lax.psum(squeeze_bias_total, "mp"),
        own_part(excite_grad, 0, 1),
        own_vector(excite_bias_total),
        own_part(reduce_weight_grad, 0, 1),
        own_vector(reduce_pair[0]),
        own_vector(reduce_pair[1]),
        own_part(spatial_weight_grad, 2, 3),
        own_vector(spatial_pair[0]),
        own_vector(spatial_pair[1]),
        own_part(widen_weight_grad, 1, 0),
        own_vector(widen_pair[0]),
        own_vector(widen_pair[1]),
        own_part(shrink_grad, 1, 0),
        lax.psum(shrink_bias_total, "mp"),
        own_part(gating_grad, 0, 1),
        own_vector(gating_bias_total),
    )


def solution(mesh):
    in_specs = (
        P(None, "dp", None, None, None),
        P(None, "dp", None),
        P("dp", "mp"),
        P("mp"),
        P("mp"),
        P(None, None, "dp", "mp"),
        P("mp"),
        P("mp"),
        P("mp", "dp"),
        P("mp"),
        P("mp"),
        P("dp", "mp"),
        P("mp"),
        P("mp"),
        P("mp", "dp"),
        P(),
        P("dp", "mp"),
        P("mp"),
        P("dp", "mp"),
        P("mp"),
        P("mp"),
        P(None, None, "dp", "mp"),
        P("mp"),
        P("mp"),
        P("mp", "dp"),
        P("mp"),
        P("mp"),
        P("mp", "dp"),
        P(),
        P("dp", "mp"),
        P("mp"),
        P(None, "dp", None, None, "mp"),
    )
    out_specs = (
        P(None, "dp", None, None, "mp"),
        P(None, "dp", None, None, "mp"),
        P("dp", "mp"),
        P("mp"),
        P("mp"),
        P(None, None, "dp", "mp"),
        P("mp"),
        P("mp"),
        P("mp", "dp"),
        P("mp"),
        P("mp"),
        P("dp", "mp"),
        P("mp"),
        P("mp"),
        P("mp", "dp"),
        P(),
        P("dp", "mp"),
        P("mp"),
        P("dp", "mp"),
        P("mp"),
        P("mp"),
        P(None, None, "dp", "mp"),
        P("mp"),
        P("mp"),
        P("mp", "dp"),
        P("mp"),
        P("mp"),
        P("mp", "dp"),
        P(),
        P("dp", "mp"),
        P("mp"),
    )
    return jax.shard_map(shards, mesh=mesh, in_specs=in_specs, out_specs=out_specs, check_vma=False)
```

```python
import functools

import jax
import jax.numpy as jnp
from jax import lax
from jax.experimental import pallas as pl
from jax.experimental.pallas import tpu as pltpu
from jax.sharding import PartitionSpec as P

eps_norm = 1e-05
highest = lax.Precision.HIGHEST
BF = jnp.bfloat16
F32 = jnp.float32
MESH = pl.DeviceIdType.MESH

TENSORS = {
    "E": (128, 512, 1, "E"),
    "P": (128, 2048, 1, "P"),
    "S": (576, 512, 1, "S"),
    "X": (512, 256, 0, "X"),
    "A": (32, 2048, 1, "A"),
    "R": (256, 512, 1, "R"),
    "T": (576, 512, 1, "S"),
    "V": (512, 256, 0, "X"),
    "B": (32, 2048, 1, "A"),
}
NAMES = list(TENSORS)
INDEX = {n: i for i, n in enumerate(NAMES)}
CLASSES = {"E": (128, 128), "P": (128, 512), "S": (576, 128), "X": (128, 256), "A": (32, 512), "R": (256, 128)}
Q = 192
VMEM_LIMIT = 64 * 2**20
WIDE = 2048
EXCHANGES = {
    "entry": (4, 512), "stride": (2, 512), "xp": (4, 2048), "reduce": (2, 512), "spatial": (2, 512), "widen": (2, 2048),
    "widen_b": (4, 2048), "spatial_b": (2, 512), "reduce_b": (2, 512), "xp_b": (4, 2048), "bias_b": (2, 2048),
    "stride_b": (2, 512), "entry_b": (2, 512),
}
EX = {n: i for i, n in enumerate(EXCHANGES)}
ROW = {"entry": 0, "stride": 2, "reduce": 4, "spatial": 6, "expand": 8, "project": 16, "widen": 24, "excite": 32, "gating": 36,
       "squeeze": 40, "shrink": 41}
SMALL = 48
NORM512 = {"entry": 0, "stride": 1, "reduce": 2, "spatial": 3}
NORM2048 = {"expand": 0, "project": 1, "widen": 2}


def sigmoid(v):
    return 0.5 + 0.5 * jnp.tanh(0.5 * v)


def dot(a, b):
    return jnp.dot(a, b, preferred_element_type=F32)


def dot_cols(a, b):
    return lax.dot_general(a, b, (((1,), (1,)), ((), ())), preferred_element_type=F32)


def dot_rows(a, b):
    return lax.dot_general(a, b, (((0,), (0,)), ((), ())), preferred_element_type=F32)


def halves(v):
    high = v.astype(BF)
    return high, (v - high.astype(F32)).astype(BF)


def exact(fn, v, w):
    high, low = halves(v)
    return fn(high, w) + fn(low, w)


def outer(a, b):
    ah, al = halves(a)
    bh, bl = halves(b)
    af, alf, bf, blf = ah.astype(F32), al.astype(F32), bh.astype(F32), bl.astype(F32)
    left = jnp.concatenate([af, af, alf, jnp.zeros_like(af)], axis=0).astype(BF)
    right = jnp.concatenate([bf, blf, bf, jnp.zeros_like(bf)], axis=0).astype(BF)
    return dot_rows(left, right)


def lanes(v, times):
    return jnp.concatenate([v] * times, axis=1) if times > 1 else v


def scratch_list():
    s = {}
    for n, (r, c, _, _) in TENSORS.items():
        s["W" + n] = pltpu.VMEM((4, 2, r, c), BF)
    for k, (r, c) in CLASSES.items():
        s["RC" + k] = pltpu.VMEM((2, 4, 2, r, c), BF)
        s["R1" + k] = pltpu.VMEM((2, 2, r, c), BF)
        s["R2" + k] = pltpu.VMEM((2, 4, r, c), BF)
        s["RZ" + k] = pltpu.VMEM((3, r, c), BF)
    for n, (r, c) in EXCHANGES.items():
        s["X_" + n] = pltpu.VMEM((8, r, c), F32)
    s["picT"] = pltpu.VMEM((768, 1024), BF)
    s["stage"] = pltpu.VMEM((768, 1024), BF)
    s["taps1"] = pltpu.VMEM((Q, 4608), BF)
    s["taps2"] = pltpu.VMEM((Q, 4608), BF)
    s["act_e"] = pltpu.VMEM((Q, WIDE), BF)
    s["act_s"] = pltpu.VMEM((Q, 512), BF)
    s["act_p"] = pltpu.VMEM((Q, 512), BF)
    s["first"] = pltpu.VMEM((Q, WIDE), BF)
    s["cotb"] = pltpu.VMEM((Q, WIDE), BF)
    s["g1"] = pltpu.VMEM((Q, WIDE), BF)
    s["g2"] = pltpu.VMEM((Q, WIDE), BF)
    s["gs"] = pltpu.VMEM((Q, 512), BF)
    s["shift"] = pltpu.VMEM((9, Q, Q), BF)
    s["perm"] = pltpu.VMEM((256, 256), BF)
    for n in ("e_raw", "x_raw", "j_raw", "w_raw", "sg"):
        s[n] = pltpu.VMEM((Q, WIDE), F32)
    for n in ("s_raw", "r_raw", "p_raw", "gq", "acc"):
        s[n] = pltpu.VMEM((Q, 512), F32)
    s["sgrad"] = pltpu.VMEM((Q, 1024), F32)
    s["insm"] = pltpu.VMEM((768, 128), F32)
    s["redm"] = pltpu.VMEM((Q, 128), F32)
    s["pix"] = pltpu.VMEM((8, 128), F32)
    s["cnt"] = pltpu.VMEM((8, 512), F32)
    s["gv5"] = pltpu.VMEM((8, 512), F32)
    s["gv20"] = pltpu.VMEM((8, WIDE), F32)
    s["nv5"] = pltpu.VMEM((4, 8, 512), F32)
    s["nv20"] = pltpu.VMEM((3, 8, WIDE), F32)
    for n in ("isum1", "isum2", "pool1", "pool2", "scale1", "scale2", "pg", "G0", "G1", "gate"):
        s[n] = pltpu.VMEM((8, WIDE), F32)
    for n in ("inner1", "inner2", "ing"):
        s[n] = pltpu.VMEM((8, 128), F32)
    s["PR"] = pltpu.VMEM((4, SMALL, 128), F32)
    s["FS"] = pltpu.VMEM((4, SMALL, 128), F32)
    s["FR"] = pltpu.VMEM((4, SMALL, 128), F32)
    dma = pltpu.SemaphoreType.DMA
    s["ag_s"] = dma((9, 9))
    s["ag_r"] = dma((9, 9))
    s["loc"] = dma((16,))
    s["rs_s"] = dma((9, 9))
    s["rs_r"] = dma((9, 9))
    s["st_s"] = dma((13, 7))
    s["st_r"] = dma((13, 8))
    s["mp_s"] = dma((5, 4))
    s["mp_r"] = dma((5, 4))
    s["free"] = pltpu.SemaphoreType.REGULAR((3,))
    return s


IN_NAMES = ["images", "sizes", "cot_in", "params"] + ["in" + n for n in NAMES]
OUT_NAMES = ["result", "igrad"] + ["out" + n for n in NAMES] + ["small"]


def body(*refs):
    names = IN_NAMES + OUT_NAMES + list(scratch_list())
    g = dict(zip(names, refs))

    class NS:
        def __getattr__(self, k):
            return g[k]

    s = NS()
    d = lax.axis_index("dp")
    m = lax.axis_index("mp")
    z, y = d // 2, lax.rem(d, 2)
    x, c = m // 2, lax.rem(m, 2)
    mx = (1 - x) * 2 + c
    mc = x * 2 + (1 - c)
    whole = slice(None)
    xdev, ydev, cdev = (d, mx), (z * 2 + (1 - y), m), (d, mc)

    def zdev(k):
        return (lax.rem(z + k, 4) * 2 + y, m)

    def mdev(k):
        return (d, lax.rem(m + k, 4))

    def col(j, w):
        return pl.ds(pl.multiple_of(j * w, w), w)

    def rcopy(src, dst, ss, rs, dev):
        return pltpu.make_async_remote_copy(
            src_ref=src, dst_ref=dst, send_sem=ss, recv_sem=rs, device_id=dev, device_id_type=MESH
        )

    partners = [(lax.rem(z + k // 2, 4) * 2 + lax.rem(y + k % 2, 2), m) for k in range(1, 8)]
    partners += [mdev(k) for k in range(1, 4)]
    barrier = pltpu.get_barrier_semaphore()
    for dev in partners:
        pl.semaphore_signal(barrier, inc=1, device_id=dev, device_id_type=MESH)
    pl.semaphore_wait(barrier, len(partners))

    def part(n, zs, ys, mi):
        rows, columns, dim, _ = TENSORS[n]
        if dim == 1:
            return g["W" + n].at[zs, ys, :, col(mi, columns // 4)]
        return g["W" + n].at[zs, ys, col(mi, rows // 4), :]

    def ag(n, slot, region, dev, src=None):
        i = INDEX[n]
        return rcopy(region if src is None else src, region, s.ag_s.at[i, slot], s.ag_r.at[i, slot], dev)

    def ag_z(n):
        own = part(n, z, y, m)
        pltpu.make_async_copy(g["in" + n], own, s.loc.at[INDEX[n]]).start()
        for k in range(1, 4):
            ag(n, k - 1, own, zdev(k), g["in" + n]).start()

    def ag_1(n):
        pltpu.make_async_copy(g["in" + n], part(n, z, y, m), s.loc.at[INDEX[n]]).wait()
        for k in range(1, 4):
            ag(n, k - 1, part(n, lax.rem(z + 4 - k, 4), y, m), zdev(k)).wait_recv()
        ag(n, 3, part(n, whole, y, m), xdev).start()
        ag(n, 4, part(n, whole, y, m), ydev).start()

    def ag_2(n):
        ag(n, 3, part(n, whole, y, mx), xdev).wait_recv()
        ag(n, 4, part(n, whole, 1 - y, m), ydev).wait_recv()
        ag(n, 5, part(n, pl.ds(0, 2), y, mx), ydev).start()
        ag(n, 6, part(n, pl.ds(2, 2), 1 - y, m), xdev).start()

    def ag_c(n):
        ag(n, 5, part(n, pl.ds(0, 2), 1 - y, mx), ydev).wait_recv()
        ag(n, 6, part(n, pl.ds(2, 2), 1 - y, mx), xdev).wait_recv()
        for xx in range(2):
            ag(n, 7 + xx, part(n, whole, whole, xx * 2 + c), cdev).start()

    def ag_done(n):
        for xx in range(2):
            ag(n, 7 + xx, part(n, whole, whole, xx * 2 + (1 - c)), cdev).wait_recv()

    def ag_drain(n):
        own = part(n, z, y, m)
        for k in range(1, 4):
            ag(n, k - 1, own, zdev(k), g["in" + n]).wait_send()
        ag(n, 3, part(n, whole, y, m), xdev).wait_send()
        ag(n, 4, part(n, whole, y, m), ydev).wait_send()
        ag(n, 5, part(n, pl.ds(0, 2), y, mx), ydev).wait_send()
        ag(n, 6, part(n, pl.ds(2, 2), 1 - y, m), xdev).wait_send()
        for xx in range(2):
            ag(n, 7 + xx, part(n, whole, whole, xx * 2 + c), cdev).wait_send()

    ticks = {"k": 0}

    def tick():
        k = ticks["k"]
        ticks["k"] = k + 1
        if 0 <= k - 2 < 9:
            ag_c(NAMES[k - 2])
        if 0 <= k - 1 < 9:
            ag_2(NAMES[k - 1])
        if k < 9:
            ag_1(NAMES[k])
        if k + 2 < 9:
            ag_z(NAMES[k + 2])

    def loop(count, fn, unroll=1):
        def step(j, carry):
            fn(j)
            return carry

        lax.fori_loop(0, count, step, 0, unroll=unroll)

    def rs(n, slot, region, landing, dev):
        i = INDEX[n]
        return rcopy(region, landing, s.rs_s.at[i, slot], s.rs_r.at[i, slot], dev)

    credits = {"T": 0, "V": 1, "B": 2}
    takes = {"S": 0, "X": 1, "A": 2}

    def rs_partners():
        return [xdev, ydev, cdev] + [zdev(k) for k in range(1, 4)]

    def rs_copies(n):
        k = TENSORS[n][3]
        rc, r1, r2, rz = g["RC" + k], g["R1" + k], g["R2" + k], g["RZ" + k]
        out = {"c": [rs(n, xx, part(n, whole, whole, xx * 2 + (1 - c)), rc.at[xx], cdev) for xx in range(2)]}
        out["1"] = [
            rs(n, 2, part(n, pl.ds(0, 2), 1 - y, mx), r1.at[0], xdev),
            rs(n, 3, part(n, pl.ds(2, 2), 1 - y, mx), r1.at[1], ydev),
        ]
        out["2"] = [
            rs(n, 4, part(n, whole, y, mx), r2.at[0], xdev),
            rs(n, 5, part(n, whole, 1 - y, m), r2.at[1], ydev),
        ]
        out["z"] = [rs(n, 5 + k, part(n, lax.rem(z + k, 4), y, m), rz.at[k - 1], zdev(k)) for k in range(1, 4)]
        return out, rc, r1, r2, rz

    def bump(region, extra):
        region[...] = region[...] + extra

    def reduce_scatter(n):
        cp, rc, r1, r2, rz = rs_copies(n)
        if n in takes:
            pl.semaphore_wait(s.free.at[takes[n]], 6)
        for t in cp["c"]:
            t.start()
        yield
        for t in cp["c"]:
            t.wait_recv()

        def add_c(j):
            zz, yy = j // 2, lax.rem(j, 2)
            for xx in range(2):
                bump(part(n, zz, yy, xx * 2 + c), rc[xx, zz, yy])

        loop(8, add_c)
        for t in cp["1"]:
            t.start()
        yield
        for t in cp["1"]:
            t.wait_recv()
        for h in range(2):
            bump(part(n, h, 1 - y, m), r1[0, h])
            bump(part(n, 2 + h, y, mx), r1[1, h])
        for t in cp["2"]:
            t.start()
        yield
        for t in cp["2"]:
            t.wait_recv()

        def add_2(zz):
            bump(part(n, zz, y, m), (r2[0, zz].astype(F32) + r2[1, zz].astype(F32)).astype(BF))

        loop(4, add_2)
        for t in cp["z"]:
            t.start()
        yield
        for t in cp["z"]:
            t.wait_recv()
        total = part(n, z, y, m)[...].astype(F32)
        for k in range(3):
            total = total + rz[k].astype(F32)
        g["out" + n][...] = total
        if n in credits:
            for dev in rs_partners():
                pl.semaphore_signal(s.free.at[credits[n]], inc=1, device_id=dev, device_id_type=MESH)
        for stage in cp.values():
            for t in stage:
                t.wait_send()

    active = []

    def pump():
        for gen in list(active):
            try:
                next(gen)
            except StopIteration:
                active.remove(gen)

    def begin(n):
        gen = reduce_scatter(n)
        active.append(gen)
        next(gen)

    def st_peers():
        return [lax.rem(z + k // 2, 4) * 2 + lax.rem(y + k % 2, 2) for k in range(1, 8)]

    def send_stats(e):
        buf, i = g["X_" + e], EX[e]
        for k, dd in enumerate(st_peers()):
            rcopy(buf.at[d], buf.at[d], s.st_s.at[i, k], s.st_r.at[i, d], (dd, m)).start()

    def get_stats(e):
        buf, i = g["X_" + e], EX[e]
        for k, dd in enumerate(st_peers()):
            rcopy(buf.at[dd], buf.at[dd], s.st_s.at[i, k], s.st_r.at[i, dd], (dd, m)).wait_recv()
        for k, dd in enumerate(st_peers()):
            rcopy(buf.at[d], buf.at[d], s.st_s.at[i, k], s.st_r.at[i, d], (dd, m)).wait_send()
        total = buf[0]
        for k in range(1, 8):
            total = total + buf[k]
        return total

    def mp_copies(i, src, dst):
        return [rcopy(src(lax.rem(m + k, 4)), dst(m), s.mp_s.at[i, k], s.mp_r.at[i, k], mdev(k)) for k in range(1, 4)]

    def mp_wait(i, src, dst, recv=True, send=True):
        for k in range(1, 4):
            if recv:
                rcopy(src(m), dst(lax.rem(m + 4 - k, 4)), s.mp_s.at[i, k], s.mp_r.at[i, k], mdev(k)).wait_recv()
            if send:
                rcopy(src(lax.rem(m + k, 4)), dst(m), s.mp_s.at[i, k], s.mp_r.at[i, k], mdev(k)).wait_send()

    cot_src, cot_dst = (lambda j: s.cot_in.at[j]), (lambda j: s.cotb.at[:, col(j, 512)])
    par_src, par_dst = (lambda j: s.params), (lambda j: s.PR.at[j])
    res_src, res_dst = (lambda j: s.g2.at[:, col(j, 512)]), (lambda j: s.result.at[j])
    img_src, img_dst = (lambda j: s.stage.at[:, col(j, 256)]), (lambda j: s.igrad.at[j])
    fin_src, fin_dst = (lambda j: s.FS.at[j]), (lambda j: s.FR.at[j])

    ag_z("E")
    for t in mp_copies(1, par_src, par_dst):
        t.start()
    own_pic = pltpu.make_async_copy(s.images.at[m], s.stage, s.loc.at[9])
    own_pic.start()
    ag_z("P")
    s.PR[m] = s.params[...]

    r64 = lax.broadcasted_iota(jnp.int32, (64, 128), 0)
    p64, q64 = r64 >> 3, r64 & 7
    s.pix[...] = jnp.ones((8, 128), F32)
    for i in range(3):
        high, wide = s.sizes[m, i, 0], s.sizes[m, i, 1]
        for pa in range(2):
            for pb in range(2):
                ok = (2 * p64 + pa < high) & (2 * q64 + pb < wide)
                s.insm[(pa * 2 + pb) * Q + i * 64 : (pa * 2 + pb) * Q + i * 64 + 64, :] = jnp.where(ok, 1.0, 0.0).astype(F32)
        ok = (2 * p64 < high) & (2 * q64 < wide)
        mask = jnp.where(ok, 1.0, 0.0).astype(F32)
        s.redm[i * 64 : i * 64 + 64, :] = mask
        s.pix[i : i + 1, :] = jnp.sum(mask, axis=0, keepdims=True)
    r8 = lax.broadcasted_iota(jnp.int32, (8, 128), 0)
    real = jnp.where(r8 < 3, 1.0, 0.0).astype(F32)

    rr = lax.broadcasted_iota(jnp.int32, (Q, Q), 0)
    cc = lax.broadcasted_iota(jnp.int32, (Q, Q), 1)
    pp, qq = (rr >> 3) & 7, rr & 7
    for t in range(9):
        da, db = t // 3 - 1, t % 3 - 1
        ok = (cc == rr + (da * 8 + db)) & (qq + db >= 0) & (qq + db < 8) & (pp + da >= 0) & (pp + da < 8)
        s.shift[t] = jnp.where(ok, 1.0, 0.0).astype(BF)
    rp = lax.broadcasted_iota(jnp.int32, (256, 256), 0)
    cp_ = lax.broadcasted_iota(jnp.int32, (256, 256), 1)
    source = ((rp >> 3) & 7) * 32 + (rp >> 7) * 16 + (rp & 7) * 2 + ((rp >> 6) & 1)
    s.perm[...] = jnp.where(cp_ == source, 1.0, 0.0).astype(BF)

    own_pic.wait()
    for i in range(3):
        def permute(j, i=i):
            v = dot(s.perm[...], s.stage[i * 256 : (i + 1) * 256, col(j, 256)]).astype(BF)
            for pl_ in range(4):
                s.picT[pl_ * Q + i * 64 : pl_ * Q + i * 64 + 64, col(j, 256)] = v[pl_ * 64 : pl_ * 64 + 64]

        loop(4, permute)

    tick()
    tick()
    mp_wait(1, par_src, par_dst)
    for n, r in ROW.items():
        if n in NORM512:
            for k in range(2):
                row = NORM512[n] * 2 + k
                for j in range(4):
                    s.gv5[row : row + 1, j * 128 : j * 128 + 128] = s.PR[j, r + k : r + k + 1, :]
        elif n in NORM2048 or n in ("excite", "gating"):
            first_row = NORM2048[n] * 2 if n in NORM2048 else (6 if n == "excite" else 7)
            for k in range(2 if n in NORM2048 else 1):
                for j in range(4):
                    for h in range(4):
                        b = (j * 4 + h) * 128
                        s.gv20[first_row + k : first_row + k + 1, b : b + 128] = s.PR[j, r + k * 4 + h : r + k * 4 + h + 1, :]
    tick()

    def put(e, row, columns, value):
        g["X_" + e][d, row : row + 1, columns] = value

    def colsum(v):
        return jnp.sum(v, axis=0, keepdims=True)

    def norm_vectors(nv, index, total, square, count, gv, grow):
        mean = total / count
        rstd = lax.rsqrt(square / count - mean * mean + eps_norm)
        a = gv[grow : grow + 1, :] * rstd
        nv[index, 0:1, :] = a
        nv[index, 1:2, :] = gv[grow + 1 : grow + 2, :] - mean * a
        nv[index, 2:3, :] = mean
        nv[index, 3:4, :] = rstd

    def norm_back_vectors(nv, index, gain_grad, shift_grad, count):
        a, mean, rstd = nv[index, 0:1, :], nv[index, 2:3, :], nv[index, 3:4, :]
        w = a * rstd * gain_grad / count
        nv[index, 4:5, :] = a * shift_grad / count - mean * w
        nv[index, 5:6, :] = w

    def activate(raw, index, out):
        for j in range(4):
            b = slice(j * 128, j * 128 + 128)
            pre = raw[:, b] * s.nv5[index, 0:1, b] + s.nv5[index, 1:2, b]
            out[:, b] = (pre * sigmoid(pre) * s.redm[...]).astype(BF)

    def sums_512(e, columns, value, mask, row=0):
        vm = value * mask
        put(e, row, columns, colsum(vm))
        put(e, row + 1, columns, colsum(vm * value))

    def sums_wide(e, columns, value, isum, row):
        total = 0.0
        square = 0.0
        for i in range(3):
            v = value[i * 64 : i * 64 + 64]
            vm = v * lanes(s.redm[i * 64 : i * 64 + 64, :], v.shape[1] // 128)
            si = colsum(vm)
            if isum is not None:
                isum[i : i + 1, columns] = si
            total = total + si
            square = square + colsum(vm * v)
        put(e, row, columns, total)
        put(e, row + 1, columns, square)

    tick()
    ag_done("E")

    def entry_step(n):
        b = col(n, 256)
        v = dot(s.picT[...], s.WE[:, :, :, b].reshape(1024, 256))
        total = 0.0
        square = 0.0
        for k in range(4):
            vk = v[k * Q : k * Q + Q]
            s.e_raw[:, pl.ds(pl.multiple_of(k * 512 + n * 256, 256), 256)] = vk
            vm = vk * lanes(s.insm[k * Q : k * Q + Q, :], 2)
            total = total + colsum(vm)
            square = square + colsum(vm * vk)
        put("entry", 0, b, total)
        put("entry", 1, b, square)

    loop(2, entry_step)
    put("entry", 2, slice(0, 512), lanes(colsum(s.insm[...]), 4))
    put("entry", 3, slice(0, 512), lanes(colsum(s.redm[...]), 4))
    send_stats("entry")

    tick()
    ag_done("P")

    def project_step(n):
        b = col(n, 256)
        v = dot(s.picT[0:Q, :], s.WP[:, :, :, b].reshape(1024, 256))
        s.j_raw[:, b] = v
        sums_wide("xp", b, v, None, 2)

    loop(8, project_step)
    tot = get_stats("entry")
    s.cnt[0:2, :] = tot[2:4]
    norm_vectors(s.nv5, 0, tot[0:1], tot[1:2], tot[2:3], s.gv5, 0)

    def entry_act_step(j):
        pcol = col(lax.rem(j, 4), 128)
        mask = s.insm[pl.ds(pl.multiple_of((j // 4) * Q, Q), Q), :]
        pre = s.e_raw[:, col(j, 128)] * s.nv5[0, 0:1, pcol] + s.nv5[0, 1:2, pcol]
        s.act_e[:, col(j, 128)] = (pre * sigmoid(pre) * mask).astype(BF)

    loop(16, entry_act_step, 2)
    for a in range(3):
        for b in range(3):
            t = a * 3 + b
            plane = (2 if a != 1 else 0) + (1 if b != 1 else 0)
            which = (0 if a == 0 else 1) * 3 + (0 if b == 0 else 1)
            v = s.act_e[:, plane * 512 : plane * 512 + 512]
            if which != 4:
                v = dot(s.shift[which], v).astype(BF)
            s.taps1[:, t * 512 : t * 512 + 512] = v

    def conv3(taps, w, raw, e):
        def step(n):
            b = col(n, 256)
            v = dot(taps[:, 0:512], w[:, :, 0:64, b].reshape(512, 256))
            for t in range(1, 9):
                v = v + dot(taps[:, t * 512 : t * 512 + 512], w[:, :, t * 64 : t * 64 + 64, b].reshape(512, 256))
            raw[:, b] = v
            sums_512(e, b, v, lanes(s.redm[...], 2))

        loop(2, step)

    tick()
    ag_done("S")
    conv3(s.taps1, s.WS, s.s_raw, "stride")
    send_stats("stride")
    for t in mp_copies(0, cot_src, cot_dst):
        t.start()
    own_cot = pltpu.make_async_copy(cot_src(m), cot_dst(m), s.loc.at[10])
    own_cot.start()
    tick()
    ag_done("X")
    tot = get_stats("stride")
    count5 = s.cnt[1:2, :]
    norm_vectors(s.nv5, 1, tot[0:1], tot[1:2], count5, s.gv5, 2)
    activate(s.s_raw, 1, s.act_s)

    for n in ("isum1", "isum2", "G0", "G1"):
        g[n][...] = jnp.zeros((8, WIDE), F32)

    def widening(act, w, raw, e, isum):
        def step(k):
            b = col(k, 256)
            v = dot(act[...], w[k // 2, lax.rem(k, 2)])
            raw[:, b] = v
            sums_wide(e, b, v, isum, 0)

        loop(8, step)

    widening(s.act_s, s.WX, s.x_raw, "xp", s.isum1)
    send_stats("xp")
    tick()
    ag_done("A")
    count20 = lanes(s.cnt[1:2, :], 4)
    tot = get_stats("xp")
    norm_vectors(s.nv20, 0, tot[0:1], tot[1:2], count20, s.gv20, 0)
    norm_vectors(s.nv20, 1, tot[2:3], tot[3:4], count20, s.gv20, 2)

    def squeeze_excite(index, isum, w, bias, gate_row, pool, inner, scale):
        pooled = (s.nv20[index, 0:1, :] * isum[...] / lanes(s.pix[...], 16) + s.nv20[index, 1:2, :]) * lanes(real, 16)
        pool[...] = pooled
        pre = exact(dot_cols, pooled, w[:, :, 0:16, :].reshape(128, WIDE)) + bias
        inner[...] = pre
        gate = exact(dot, pre * sigmoid(pre), w[:, :, 16:32, :].reshape(128, WIDE)) + s.gv20[gate_row : gate_row + 1, :]
        scale[...] = sigmoid(gate)

    squeeze_excite(0, s.isum1, s.WA, s.PR[0, 40:41, :], 6, s.pool1, s.inner1, s.scale1)

    def first_sum(j, i):
        b, rows = col(j, 128), slice(i * 64, i * 64 + 64)
        pre = s.x_raw[rows, b] * s.nv20[0, 0:1, b] + s.nv20[0, 1:2, b]
        return pre * s.scale1[i : i + 1, b] + (s.j_raw[rows, b] * s.nv20[1, 0:1, b] + s.nv20[1, 1:2, b])

    def first_step(j):
        for i in range(3):
            rows = slice(i * 64, i * 64 + 64)
            v = first_sum(j, i)
            s.first[rows, col(j, 128)] = (v * sigmoid(v) * s.redm[rows, :]).astype(BF)

    loop(16, first_step, 2)

    tick()
    ag_done("R")

    def reduce_step(n):
        b = col(n, 256)
        v = dot(s.first[...], s.WR[:, :, :, b].reshape(WIDE, 256))
        s.r_raw[:, b] = v
        sums_512("reduce", b, v, lanes(s.redm[...], 2))

    loop(2, reduce_step)
    send_stats("reduce")
    tick()
    tot = get_stats("reduce")
    norm_vectors(s.nv5, 2, tot[0:1], tot[1:2], count5, s.gv5, 4)
    activate(s.r_raw, 2, s.act_p)
    for t in range(9):
        v = s.act_p[...]
        if t != 4:
            v = dot(s.shift[t], v).astype(BF)
        s.taps2[:, t * 512 : t * 512 + 512] = v
    ag_done("T")
    conv3(s.taps2, s.WT, s.p_raw, "spatial")
    send_stats("spatial")
    tick()
    ag_done("V")
    tot = get_stats("spatial")
    norm_vectors(s.nv5, 3, tot[0:1], tot[1:2], count5, s.gv5, 6)
    activate(s.p_raw, 3, s.act_p)
    widening(s.act_p, s.WV, s.w_raw, "widen", s.isum2)
    send_stats("widen")
    ag_done("B")
    own_cot.wait()
    mp_wait(0, cot_src, cot_dst)
    tot = get_stats("widen")
    norm_vectors(s.nv20, 2, tot[0:1], tot[1:2], count20, s.gv20, 4)
    squeeze_excite(2, s.isum2, s.WB, s.PR[0, 41:42, :], 7, s.pool2, s.inner2, s.scale2)

    def result_step(j):
        b = col(j, 128)
        for i in range(3):
            rows = slice(i * 64, i * 64 + 64)
            raw = s.w_raw[rows, b]
            pre = raw * s.nv20[2, 0:1, b] + s.nv20[2, 1:2, b]
            v = pre * s.scale2[i : i + 1, b] + s.first[rows, b].astype(F32)
            sg = sigmoid(v)
            mask = s.redm[rows, :]
            s.g2[rows, b] = (v * sg * mask).astype(BF)
            grad = s.cotb[rows, b].astype(F32) * mask * (sg * (1.0 + v * (1.0 - sg)))
            s.sg[rows, b] = grad
            s.G0[i : i + 1, b] = colsum(grad)
            s.G1[i : i + 1, b] = colsum(grad * ((raw - s.nv20[2, 2:3, b]) * s.nv20[2, 3:4, b]))

    loop(16, result_step, 2)
    for t in mp_copies(2, res_src, res_dst):
        t.start()
    own_res = pltpu.make_async_copy(res_src(m), res_dst(m), s.loc.at[11])
    own_res.start()

    def keep512(n, k, v):
        for j in range(4):
            s.FS[j, ROW[n] + k : ROW[n] + k + 1, :] = v[:, j * 128 : j * 128 + 128]

    def keep2048(row, v):
        for j in range(4):
            for h in range(4):
                b = (j * 4 + h) * 128
                s.FS[j, row + h : row + h + 1, :] = v[:, b : b + 128]

    def excite_back(index, isum, w, inner, scale):
        scl = scale[...]
        gate_grad = (s.gv20[index * 2 : index * 2 + 1, :] * s.G1[...] + s.gv20[index * 2 + 1 : index * 2 + 2, :] * s.G0[...]) * (
            scl * (1.0 - scl)
        )
        s.gate[...] = gate_grad
        pre = inner[...]
        sg = sigmoid(pre)
        ing = exact(dot_cols, gate_grad, w[:, :, 16:32, :].reshape(128, WIDE)) * (sg * (1.0 + pre * (1.0 - sg)))
        s.ing[...] = ing
        pix = lanes(s.pix[...], 16)
        pg = exact(dot, ing, w[:, :, 0:16, :].reshape(128, WIDE)) / pix
        s.pg[...] = pg
        spread = (isum[...] - s.nv20[index, 2:3, :] * pix) * s.nv20[index, 3:4, :]
        return (colsum(scl * s.G1[...] + pg * spread), colsum(scl * s.G0[...] + pg * pix), colsum(gate_grad), colsum(ing))

    def excite_weights(n, pool, inner):
        pre = inner[...]
        hidden = pre * sigmoid(pre)
        w = g["W" + n]

        def step(j):
            b = col(j, 512)
            w[:, :, 0:16, b] = outer(s.ing[...], pool[:, b]).astype(BF).reshape(4, 2, 16, 512)
            w[:, :, 16:32, b] = outer(hidden, s.gate[:, b]).astype(BF).reshape(4, 2, 16, 512)

        loop(4, step)

    def wide_grad(index, raw, out, scale):
        def step(j):
            b = col(j, 128)
            for i in range(3):
                rows = slice(i * 64, i * 64 + 64)
                grad, mask = s.sg[rows, b], s.redm[rows, :]
                if scale is not None:
                    grad = grad * scale[i : i + 1, b] + mask * s.pg[i : i + 1, b]
                v = s.nv20[index, 0:1, b] * grad - mask * (s.nv20[index, 4:5, b] + s.nv20[index, 5:6, b] * raw[rows, b])
                out[rows, b] = v.astype(BF)

        loop(16, step, 2)

    def back_sums(e, index, b, grad, raw, mask):
        out = []
        pre = raw * s.nv5[index, 0:1, b] + s.nv5[index, 1:2, b]
        sg = sigmoid(pre)
        grad = grad * mask * (sg * (1.0 + pre * (1.0 - sg)))
        put(e, 0, b, colsum(grad * ((raw - s.nv5[index, 2:3, b]) * s.nv5[index, 3:4, b])))
        put(e, 1, b, colsum(grad))
        return grad

    def narrow_back(e, index, acc, raw):
        for j in range(4):
            b = slice(j * 128, j * 128 + 128)
            s.gq[:, b] = back_sums(e, index, b, acc[:, b], raw[:, b], s.redm[...])

    def narrow_grad(index, raw):
        for j in range(4):
            b = slice(j * 128, j * 128 + 128)
            v = s.nv5[index, 0:1, b] * s.gq[:, b] - s.redm[...] * (s.nv5[index, 4:5, b] + s.nv5[index, 5:6, b] * raw[:, b])
            s.gs[:, b] = v.astype(BF)

    def narrow_stats(e, n):
        tot = get_stats(e)
        keep512(n, 0, tot[0:1])
        keep512(n, 1, tot[1:2])
        norm_back_vectors(s.nv5, NORM512[n], tot[0:1], tot[1:2], s.cnt[0:1, :] if n == "entry" else count5)

    def widening_back(grads, w):
        def step(n):
            rows = col(n, 256)
            v = dot_cols(grads[:, 0:256], w[0, 0, rows, :])
            for k in range(1, 8):
                v = v + dot_cols(grads[:, k * 256 : k * 256 + 256], w[k // 2, k % 2, rows, :])
            s.acc[:, rows] = v

        loop(2, step)

    def widening_weights(n, act, grads):
        ag_drain(n)
        w = g["W" + n]

        def step(k):
            w[k // 2, lax.rem(k, 2)] = dot_rows(act[...], grads[:, col(k, 256)]).astype(BF)

        loop(8, step)
        begin(n)

    def conv3_weights(n, taps):
        ag_drain(n)
        w = g["W" + n]

        def step(t):
            for h in range(2):
                b = slice(h * 256, h * 256 + 256)
                v = dot_rows(taps[:, col(t, 512)], s.gs[:, b]).astype(BF)
                w[:, :, col(t, 64), b] = v.reshape(4, 2, 64, 256)

        loop(9, step)
        begin(n)

    sums = excite_back(2, s.isum2, s.WB, s.inner2, s.scale2)
    for k in range(3):
        put("widen_b", k, slice(0, WIDE), sums[k])
    put("widen_b", 3, slice(0, WIDE), lanes(sums[3], 16))
    send_stats("widen_b")
    ag_drain("B")
    excite_weights("B", s.pool2, s.inner2)
    begin("B")
    tot = get_stats("widen_b")
    keep2048(ROW["widen"], tot[0:1])
    keep2048(ROW["widen"] + 4, tot[1:2])
    keep2048(ROW["gating"], tot[2:3])
    for j in range(4):
        s.FS[j, ROW["shrink"] : ROW["shrink"] + 1, :] = tot[3:4, 0:128]
    norm_back_vectors(s.nv20, 2, tot[0:1], tot[1:2], count20)
    wide_grad(2, s.w_raw, s.g1, s.scale2)
    widening_back(s.g1, s.WV)
    narrow_back("spatial_b", 3, s.acc, s.p_raw)
    send_stats("spatial_b")
    pump()
    widening_weights("V", s.act_p, s.g1)
    narrow_stats("spatial_b", "spatial")
    narrow_grad(3, s.p_raw)
    pump()
    s.acc[...] = jnp.zeros((Q, 512), F32)

    def spatial_back(t):
        v = dot(s.shift[8 - t], s.gs[...]).astype(BF)
        s.acc[...] += dot_cols(v, s.WT[:, :, col(t, 64), :].reshape(512, 512))

    loop(9, spatial_back)
    narrow_back("reduce_b", 2, s.acc, s.r_raw)
    send_stats("reduce_b")
    pump()
    conv3_weights("T", s.taps2)
    narrow_stats("reduce_b", "reduce")
    narrow_grad(2, s.r_raw)
    pump()

    def reduce_back(k):
        v = dot_cols(s.gs[...], s.WR[k // 2, lax.rem(k, 2)])
        for h in range(2):
            j = k * 2 + h
            b = col(j, 128)
            project_sum = 0.0
            shift_sum = 0.0
            for i in range(3):
                rows = slice(i * 64, i * 64 + 64)
                fs = first_sum(j, i)
                sg = sigmoid(fs)
                grad = (v[rows, h * 128 : h * 128 + 128] + s.sg[rows, b]) * s.redm[rows, :] * (sg * (1.0 + fs * (1.0 - sg)))
                s.sg[rows, b] = grad
                total = colsum(grad)
                s.G0[i : i + 1, b] = total
                s.G1[i : i + 1, b] = colsum(grad * ((s.x_raw[rows, b] - s.nv20[0, 2:3, b]) * s.nv20[0, 3:4, b]))
                shift_sum = shift_sum + total
                project_sum = project_sum + colsum(grad * ((s.j_raw[rows, b] - s.nv20[1, 2:3, b]) * s.nv20[1, 3:4, b]))
            put("xp_b", 2, b, project_sum)
            put("xp_b", 3, b, shift_sum)

    loop(8, reduce_back)
    sums = excite_back(0, s.isum1, s.WA, s.inner1, s.scale1)
    put("xp_b", 0, slice(0, WIDE), sums[0])
    put("xp_b", 1, slice(0, WIDE), sums[1])
    send_stats("xp_b")
    put("bias_b", 0, slice(0, WIDE), sums[2])
    put("bias_b", 1, slice(0, WIDE), lanes(sums[3], 16))
    send_stats("bias_b")
    pump()
    ag_drain("R")

    def reduce_weights(k):
        s.WR[k // 2, lax.rem(k, 2)] = dot_rows(s.first[:, col(k, 256)], s.gs[...]).astype(BF)

    loop(8, reduce_weights)
    begin("R")
    ag_drain("A")
    excite_weights("A", s.pool1, s.inner1)
    begin("A")
    tot = get_stats("xp_b")
    for k, n in enumerate(("expand", "project")):
        keep2048(ROW[n], tot[2 * k : 2 * k + 1])
        keep2048(ROW[n] + 4, tot[2 * k + 1 : 2 * k + 2])
        norm_back_vectors(s.nv20, k, tot[2 * k : 2 * k + 1], tot[2 * k + 1 : 2 * k + 2], count20)
    wide_grad(0, s.x_raw, s.g1, s.scale1)
    widening_back(s.g1, s.WX)
    narrow_back("stride_b", 1, s.acc, s.s_raw)
    send_stats("stride_b")
    pump()
    own_res.wait()
    mp_wait(2, res_src, res_dst)
    wide_grad(1, s.j_raw, s.g2, None)

    def project_back(zz):
        w = s.WP[zz].reshape(256, WIDE)
        s.sgrad[:, col(zz, 256)] = dot_cols(s.g2[...], w)

    loop(4, project_back)
    widening_weights("X", s.act_s, s.g1)
    ag_drain("P")

    def project_weights(n):
        b = col(n, 256)
        for h in range(2):
            v = dot_rows(s.picT[0:Q, h * 512 : h * 512 + 512], s.g2[:, b]).astype(BF)
            s.WP[2 * h : 2 * h + 2, :, :, b] = v.reshape(2, 2, 128, 256)

    loop(8, project_weights)
    begin("P")
    narrow_stats("stride_b", "stride")
    narrow_grad(1, s.s_raw)
    pump()

    for k in range(4):
        pa, pb = k // 2, k % 2
        columns = slice(k * 512, k * 512 + 512)
        first_tap = True
        for a in (0, 2) if pa else (1,):
            for b in (0, 2) if pb else (1,):
                t = a * 3 + b
                which = (0 if a == 0 else 1) * 3 + (0 if b == 0 else 1)
                v = s.gs[...]
                if which != 4:
                    v = dot(s.shift[8 - which], v).astype(BF)
                v = dot_cols(v, s.WS[:, :, t * 64 : t * 64 + 64, :].reshape(512, 512))
                if first_tap:
                    s.w_raw[:, columns] = v
                else:
                    s.w_raw[:, columns] += v
                first_tap = False

    def entry_back(n):
        b = col(n, 128)
        gain_sum = 0.0
        shift_sum = 0.0
        for k in range(4):
            kb = pl.ds(pl.multiple_of(k * 512 + n * 128, 128), 128)
            raw = s.e_raw[:, kb]
            pre = raw * s.nv5[0, 0:1, b] + s.nv5[0, 1:2, b]
            sg = sigmoid(pre)
            grad = s.w_raw[:, kb] * s.insm[k * Q : k * Q + Q, :] * (sg * (1.0 + pre * (1.0 - sg)))
            s.w_raw[:, kb] = grad
            gain_sum = gain_sum + colsum(grad * ((raw - s.nv5[0, 2:3, b]) * s.nv5[0, 3:4, b]))
            shift_sum = shift_sum + colsum(grad)
        put("entry_b", 0, b, gain_sum)
        put("entry_b", 1, b, shift_sum)

    loop(4, entry_back)
    send_stats("entry_b")
    pump()
    conv3_weights("S", s.taps1)
    narrow_stats("entry_b", "entry")

    def entry_grad(j):
        pcol = col(lax.rem(j, 4), 128)
        mask = s.insm[pl.ds(pl.multiple_of((j // 4) * Q, Q), Q), :]
        b = col(j, 128)
        v = s.nv5[0, 0:1, pcol] * s.w_raw[:, b] - mask * (s.nv5[0, 4:5, pcol] + s.nv5[0, 5:6, pcol] * s.e_raw[:, b])
        s.act_e[:, b] = v.astype(BF)

    loop(16, entry_grad, 2)
    tot = get_stats("bias_b")
    keep2048(ROW["excite"], tot[0:1])
    for j in range(4):
        s.FS[j, ROW["squeeze"] : ROW["squeeze"] + 1, :] = tot[1:2, 0:128]
        for r in range(42, SMALL, 2):
            s.FS[j, r : r + 2, :] = jnp.zeros((2, 128), F32)
    s.FR[m] = s.FS[m]
    for t in mp_copies(4, fin_src, fin_dst):
        t.start()

    def image_grad(zz):
        w = s.WE[zz].reshape(256, 512)
        for k in range(4):
            v = dot_cols(s.act_e[:, k * 512 : k * 512 + 512], w)
            if k == 0:
                v = v + s.sgrad[:, col(zz, 256)]
            s.taps1[:, pl.ds(pl.multiple_of(k * 1024 + zz * 256, 256), 256)] = v.astype(BF)

    loop(4, image_grad)
    for i in range(3):
        def unpermute(j, i=i):
            v = jnp.concatenate(
                [s.taps1[i * 64 : i * 64 + 64, pl.ds(pl.multiple_of(k * 1024 + j * 256, 256), 256)] for k in range(4)], axis=0
            )
            s.stage[i * 256 : i * 256 + 256, col(j, 256)] = dot_rows(s.perm[...], v).astype(BF)

        loop(4, unpermute)
    for t in mp_copies(3, img_src, img_dst):
        t.start()
    own_img = pltpu.make_async_copy(img_src(m), img_dst(m), s.loc.at[12])
    own_img.start()
    ag_drain("E")

    def entry_weights(zz):
        v = dot_rows(s.picT[0:Q, col(zz, 256)], s.act_e[:, 0:512])
        for k in range(1, 4):
            v = v + dot_rows(s.picT[k * Q : k * Q + Q, col(zz, 256)], s.act_e[:, k * 512 : k * 512 + 512])
        s.WE[zz] = v.astype(BF).reshape(2, 128, 512)

    loop(4, entry_weights)
    begin("E")
    while active:
        pump()
    mp_wait(4, fin_src, fin_dst)
    s.small[...] = ((s.FR[0] + s.FR[1]) + s.FR[2]) + s.FR[3]
    own_img.wait()
    mp_wait(3, img_src, img_dst)

def fused_shards(*arrays):
    (images, image_size, entry_weight, entry_gain, entry_shift, stride_weight, stride_gain, stride_shift, expand_weight,
     expand_gain, expand_shift, project_weight, project_gain, project_shift, squeeze_weight, squeeze_bias, excite_weight,
     excite_bias, reduce_weight, reduce_gain, reduce_shift, spatial_weight, spatial_gain, spatial_shift, widen_weight,
     widen_gain, widen_shift, shrink_weight, shrink_bias, gating_weight, gating_bias, cotangent) = arrays
    small = [entry_gain, entry_shift, stride_gain, stride_shift, reduce_gain, reduce_shift, spatial_gain, spatial_shift,
             expand_gain, expand_shift, project_gain, project_shift, widen_gain, widen_shift, excite_bias, gating_bias,
             squeeze_bias, shrink_bias]
    params = jnp.concatenate([v.reshape(-1, 128) for v in small] + [jnp.zeros((SMALL - 42, 128), F32)], axis=0)
    shards = {
        "E": entry_weight,
        "P": project_weight,
        "S": stride_weight.reshape(576, 128),
        "X": expand_weight,
        "A": jnp.concatenate([squeeze_weight.T, excite_weight], axis=0),
        "R": reduce_weight,
        "T": spatial_weight.reshape(576, 128),
        "V": widen_weight,
        "B": jnp.concatenate([shrink_weight.T, gating_weight], axis=0),
    }
    outs = [jax.ShapeDtypeStruct((4, Q, 512), BF), jax.ShapeDtypeStruct((4, 768, 256), BF)]
    outs += [jax.ShapeDtypeStruct(CLASSES[TENSORS[n][3]], F32) for n in NAMES]
    outs += [jax.ShapeDtypeStruct((SMALL, 128), F32)]
    hbm, vmem = pl.BlockSpec(memory_space=pl.ANY), pl.BlockSpec(memory_space=pltpu.VMEM)
    got = pl.pallas_call(
        body,
        out_shape=outs,
        in_specs=[hbm, pl.BlockSpec(memory_space=pltpu.SMEM), hbm, vmem] + [hbm] * len(NAMES),
        out_specs=[hbm, hbm] + [vmem] * (len(NAMES) + 1),
        scratch_shapes=list(scratch_list().values()),
        compiler_params=pltpu.CompilerParams(
            collective_id=0, has_side_effects=True, vmem_limit_bytes=VMEM_LIMIT
        ),
        cost_estimate=pl.CostEstimate(flops=14_000_000_000, bytes_accessed=30_000_000, transcendentals=10_000_000),
    )(images.reshape(4, 768, 1024), image_size, cotangent.reshape(4, Q, 512), params, *[shards[n] for n in NAMES])
    result, igrad, weights, rows = got[0], got[1], dict(zip(NAMES, got[2:-1])), got[-1]

    def vector(first, count):
        return rows[first : first + count].reshape(-1)

    def pair(n):
        k = 1 if n in NORM512 else 4
        return vector(ROW[n], k), vector(ROW[n] + k, k)

    return (
        result.reshape(cotangent.shape),
        igrad.reshape(4, 3, 16, 16, 256).astype(F32),
        weights["E"], *pair("entry"),
        weights["S"].reshape(stride_weight.shape), *pair("stride"),
        weights["X"], *pair("expand"),
        weights["P"], *pair("project"),
        weights["A"][:16].T, vector(ROW["squeeze"], 1), weights["A"][16:], vector(ROW["excite"], 4),
        weights["R"], *pair("reduce"),
        weights["T"].reshape(spatial_weight.shape), *pair("spatial"),
        weights["V"], *pair("widen"),
        weights["B"][:16].T, vector(ROW["shrink"], 1), weights["B"][16:], vector(ROW["gating"], 4),
    )


def matmul(left, right):
    return jnp.dot(left, right, preferred_element_type=jnp.float32)


def contract_rows(left, right):
    return lax.dot_general(
        left, right, (((0,), (0,)), ((), ())), preferred_element_type=jnp.float32
    )


def contract_cols(left, right):
    return lax.dot_general(
        left, right, (((1,), (1,)), ((), ())), preferred_element_type=jnp.float32
    )


def swish_slope(value):
    sigma = jax.nn.sigmoid(value)
    return sigma * (1.0 + value * (1.0 - sigma))


def pixel_masks(sizes, side):
    half = side // 2
    height = sizes[:, 0]
    breadth = sizes[:, 1]
    places = jnp.arange(side, dtype=jnp.int32)
    inside = (
        (places[None, :, None] < height[:, None, None])
        & (places[None, None, :] < breadth[:, None, None])
    ).astype(jnp.float32)
    halves = jnp.arange(half, dtype=jnp.int32)
    reduced = (
        (halves[None, :, None] < ((height + 1) // 2)[:, None, None])
        & (halves[None, None, :] < ((breadth + 1) // 2)[:, None, None])
    ).astype(jnp.float32)
    return (inside, reduced)


def spatial_taps(field, stride):
    count, side, channels = (field.shape[0], field.shape[1], field.shape[3])
    reach = stride * (side // stride - 1) + 1
    padded = jnp.pad(field, ((0, 0), (1, 1), (1, 1), (0, 0)))
    pieces = []
    for row in range(3):
        for column in range(3):
            pieces.append(
                lax.slice(
                    padded,
                    (0, row, column, 0),
                    (count, row + reach, column + reach, channels),
                    (1, stride, stride, 1),
                )
            )
    return jnp.concatenate(pieces, axis=3)


def untap(grads, stride, side):
    count, out_side = (grads.shape[0], grads.shape[1])
    channels = grads.shape[3] // 9
    reach = stride * (out_side - 1) + 1
    total = jnp.zeros((count, side + 2, side + 2, channels), jnp.float32)
    for row in range(3):
        for column in range(3):
            first = (row * 3 + column) * channels
            piece = grads[:, :, :, first : first + channels]
            total = total + lax.pad(
                piece,
                jnp.float32(0.0),
                (
                    (0, 0, 0),
                    (row, side + 2 - row - reach, stride - 1),
                    (column, side + 2 - column - reach, stride - 1),
                    (0, 0, 0),
                ),
            )
    return total[:, 1 : side + 1, 1 : side + 1, :]


def batch_statistics(fields, mask):
    weights = mask[..., None]
    terms = []
    for field in fields:
        terms.append(jnp.sum(field * weights, axis=(0, 1, 2)))
        terms.append(jnp.sum(field * field * weights, axis=(0, 1, 2)))
    packed, total_vector = lax.psum((jnp.concatenate(terms), jnp.sum(mask).reshape(1)), "dp")
    total = total_vector[0]
    result = []
    offset = 0
    for field in fields:
        breadth = field.shape[3]
        mean = packed[offset : offset + breadth] / total
        second = packed[offset + breadth : offset + 2 * breadth] / total
        result.append((mean, lax.rsqrt(second - mean * mean + eps_norm)))
        offset = offset + 2 * breadth
    return (result, total)


def standardize(raw, statistics, gain, shift):
    mean, scale = statistics
    normed = (raw - mean) * scale
    return (normed, normed * gain + shift)


def batch_backward(grads, normeds, scales, gains, mask, total, extras):
    terms = []
    for grad, normed in zip(grads, normeds):
        terms.append(jnp.sum(grad * normed, axis=(0, 1, 2)))
        terms.append(jnp.sum(grad, axis=(0, 1, 2)))
    for extra in extras:
        terms.append(extra)
    packed = lax.psum(jnp.concatenate(terms), "dp")
    results = []
    pairs = []
    offset = 0
    for grad, normed, scale, gain in zip(grads, normeds, scales, gains):
        breadth = grad.shape[3]
        gain_grad = packed[offset : offset + breadth]
        shift_grad = packed[offset + breadth : offset + 2 * breadth]
        offset = offset + 2 * breadth
        results.append(
            scale * gain * (grad - mask[..., None] * (shift_grad + normed * gain_grad) / total)
        )
        pairs.append((gain_grad, shift_grad))
    rest = []
    for extra in extras:
        rest.append(packed[offset : offset + extra.shape[0]])
        offset = offset + extra.shape[0]
    return (results, pairs, rest)


def excite_forward(field, mask, pixels, squeeze_full, squeeze_bias, excite_full, excite_bias):
    pooled = jnp.sum(field * mask[..., None], axis=(1, 2)) / pixels[:, None]
    inner_pre = (
        jnp.dot(pooled, squeeze_full.astype(jnp.float32), precision=highest) + squeeze_bias
    )
    hidden = jax.nn.silu(inner_pre)
    scale = jax.nn.sigmoid(
        jnp.dot(hidden, excite_full.astype(jnp.float32), precision=highest) + excite_bias
    )
    return (pooled, inner_pre, hidden, scale)


def excite_backward(grad_branch, field, mask, pixels, saved, squeeze_full, excite_full):
    pooled, inner_pre, hidden, scale = saved
    grad_scale = jnp.sum(grad_branch * field, axis=(1, 2))
    grad_gate = grad_scale * scale * (1.0 - scale)
    excite_grad = jnp.dot(hidden.T, grad_gate, precision=highest)
    grad_hidden = jnp.dot(grad_gate, excite_full.astype(jnp.float32).T, precision=highest)
    grad_inner = grad_hidden * swish_slope(inner_pre)
    squeeze_grad = jnp.dot(pooled.T, grad_inner, precision=highest)
    grad_pooled = jnp.dot(grad_inner, squeeze_full.astype(jnp.float32).T, precision=highest)
    grad_field = (
        grad_branch * scale[:, None, None, :]
        + grad_pooled[:, None, None, :] * mask[..., None] / pixels[:, None, None, None]
    )
    return (
        grad_field,
        squeeze_grad,
        excite_grad,
        jnp.sum(grad_inner, axis=0),
        jnp.sum(grad_gate, axis=0),
    )


def whole_vector(value):
    return lax.all_gather(value, "mp", axis=0, tiled=True)


def whole_matrix(value, dp_axis, mp_axis):
    value = lax.all_gather(value, "dp", axis=dp_axis, tiled=True)
    return lax.all_gather(value, "mp", axis=mp_axis, tiled=True)


def own_part(value, dp_axis, mp_axis):
    value = lax.psum_scatter(
        value.astype(jnp.bfloat16), "mp", scatter_dimension=mp_axis, tiled=True
    )
    return lax.psum_scatter(value, "dp", scatter_dimension=dp_axis, tiled=True).astype(
        jnp.float32
    )


def plain_shards(
    images,
    image_size,
    entry_weight,
    entry_gain,
    entry_shift,
    stride_weight,
    stride_gain,
    stride_shift,
    expand_weight,
    expand_gain,
    expand_shift,
    project_weight,
    project_gain,
    project_shift,
    squeeze_weight,
    squeeze_bias,
    excite_weight,
    excite_bias,
    reduce_weight,
    reduce_gain,
    reduce_shift,
    spatial_weight,
    spatial_gain,
    spatial_shift,
    widen_weight,
    widen_gain,
    widen_shift,
    shrink_weight,
    shrink_bias,
    gating_weight,
    gating_bias,
    cotangent,
):
    place = lax.axis_index("mp")
    count, side = (images.shape[1], images.shape[2])
    half = side // 2
    channels_in = images.shape[4]
    entry_full = whole_matrix(entry_weight, 0, 1)
    stride_full = whole_matrix(stride_weight, 2, 3)
    expand_full = whole_matrix(expand_weight, 1, 0)
    project_full = whole_matrix(project_weight, 0, 1)
    squeeze_full = whole_matrix(squeeze_weight, 1, 0)
    excite_full = whole_matrix(excite_weight, 0, 1)
    reduce_full = whole_matrix(reduce_weight, 0, 1)
    spatial_full = whole_matrix(spatial_weight, 2, 3)
    widen_full = whole_matrix(widen_weight, 1, 0)
    shrink_full = whole_matrix(shrink_weight, 1, 0)
    gating_full = whole_matrix(gating_weight, 0, 1)
    entry_gain, entry_shift = whole_vector(entry_gain), whole_vector(entry_shift)
    stride_gain, stride_shift = whole_vector(stride_gain), whole_vector(stride_shift)
    expand_gain, expand_shift = whole_vector(expand_gain), whole_vector(expand_shift)
    project_gain, project_shift = whole_vector(project_gain), whole_vector(project_shift)
    reduce_gain, reduce_shift = whole_vector(reduce_gain), whole_vector(reduce_shift)
    spatial_gain, spatial_shift = whole_vector(spatial_gain), whole_vector(spatial_shift)
    widen_gain, widen_shift = whole_vector(widen_gain), whole_vector(widen_shift)
    excite_bias, gating_bias = whole_vector(excite_bias), whole_vector(gating_bias)
    seed_grad = lax.all_to_all(cotangent, "mp", split_axis=0, concat_axis=4, tiled=True)[0]
    picture = lax.dynamic_index_in_dim(images, place, 0, keepdims=False)
    sizes = lax.dynamic_index_in_dim(image_size, place, 0, keepdims=False)
    inside, reduced = pixel_masks(sizes, side)
    pixels = jnp.sum(reduced, axis=(1, 2))
    reduced_mask = reduced[..., None]
    entry_raw = matmul(picture.reshape(-1, channels_in), entry_full).reshape(
        count, side, side, -1
    )
    stats, inside_total = batch_statistics([entry_raw], inside)
    entry_stats = stats[0]
    entry_normed, entry_pre = standardize(entry_raw, entry_stats, entry_gain, entry_shift)
    entry_act = (jax.nn.silu(entry_pre) * inside[..., None]).astype(jnp.bfloat16)
    entry_wide = entry_act
    bottleneck = entry_wide.shape[3]
    stride_taps = spatial_taps(entry_wide, 2).reshape(-1, 9 * bottleneck)
    stride_raw = matmul(stride_taps, stride_full.reshape(9 * bottleneck, -1)).reshape(
        count, half, half, -1
    )
    stats, reduced_total = batch_statistics([stride_raw], reduced)
    stride_stats = stats[0]
    stride_normed, stride_pre = standardize(stride_raw, stride_stats, stride_gain, stride_shift)
    stride_act = (jax.nn.silu(stride_pre) * reduced_mask).astype(jnp.bfloat16)
    local_bottleneck = stride_act.shape[3]
    stride_flat = stride_act.reshape(-1, local_bottleneck)
    expand_raw = matmul(stride_flat, expand_full).reshape(count, half, half, -1)
    strided_flat = picture[:, ::2, ::2, :].reshape(-1, channels_in)
    project_raw = matmul(strided_flat, project_full).reshape(count, half, half, -1)
    stats, reduced_total = batch_statistics([expand_raw, project_raw], reduced)
    expand_stats, project_stats = (stats[0], stats[1])
    expand_normed, expand_pre = standardize(expand_raw, expand_stats, expand_gain, expand_shift)
    project_normed, project_pre = standardize(
        project_raw, project_stats, project_gain, project_shift
    )
    first_saved = excite_forward(
        expand_pre, reduced, pixels, squeeze_full, squeeze_bias, excite_full, excite_bias
    )
    first_sum = expand_pre * first_saved[3][:, None, None, :] + project_pre
    first_out = (jax.nn.silu(first_sum) * reduced_mask).astype(jnp.bfloat16)
    block_wide = first_out
    block_flat = block_wide.reshape(-1, block_wide.shape[3])
    reduce_raw = matmul(block_flat, reduce_full).reshape(count, half, half, -1)
    stats, reduced_total = batch_statistics([reduce_raw], reduced)
    reduce_stats = stats[0]
    reduce_normed, reduce_pre = standardize(reduce_raw, reduce_stats, reduce_gain, reduce_shift)
    reduce_act = (jax.nn.silu(reduce_pre) * reduced_mask).astype(jnp.bfloat16)
    reduce_wide = reduce_act
    second_taps = spatial_taps(reduce_wide, 1).reshape(-1, 9 * bottleneck)
    spatial_raw = matmul(second_taps, spatial_full.reshape(9 * bottleneck, -1)).reshape(
        count, half, half, -1
    )
    stats, reduced_total = batch_statistics([spatial_raw], reduced)
    spatial_stats = stats[0]
    spatial_normed, spatial_pre = standardize(
        spatial_raw, spatial_stats, spatial_gain, spatial_shift
    )
    spatial_act = (jax.nn.silu(spatial_pre) * reduced_mask).astype(jnp.bfloat16)
    spatial_flat = spatial_act.reshape(-1, local_bottleneck)
    widen_raw = matmul(spatial_flat, widen_full).reshape(count, half, half, -1)
    stats, reduced_total = batch_statistics([widen_raw], reduced)
    widen_stats = stats[0]
    widen_normed, widen_pre = standardize(widen_raw, widen_stats, widen_gain, widen_shift)
    second_saved = excite_forward(
        widen_pre, reduced, pixels, shrink_full, shrink_bias, gating_full, gating_bias
    )
    second_sum = widen_pre * second_saved[3][:, None, None, :] + first_out.astype(jnp.float32)
    output = (jax.nn.silu(second_sum) * reduced_mask).astype(jnp.bfloat16)
    second_grad = seed_grad.astype(jnp.float32) * reduced_mask * swish_slope(second_sum)
    widen_grad, shrink_grad, gating_grad, shrink_bias_grad, gating_bias_grad = excite_backward(
        second_grad, widen_pre, reduced, pixels, second_saved, shrink_full, gating_full
    )
    grads, widen_pair, extras = batch_backward(
        [widen_grad],
        [widen_normed],
        [widen_stats[1]],
        [widen_gain],
        reduced,
        reduced_total,
        (shrink_bias_grad, gating_bias_grad),
    )
    widen_pair = widen_pair[0]
    shrink_bias_total, gating_bias_total = (extras[0], extras[1])
    widen_local = grads[0].astype(jnp.bfloat16)
    widen_low = widen_local
    widen_flat = widen_low.reshape(-1, widen_low.shape[3])
    widen_weight_grad = contract_rows(spatial_flat, widen_flat)
    spatial_act_grad = contract_cols(widen_flat, widen_full).reshape(count, half, half, -1)
    spatial_grad = spatial_act_grad * reduced_mask * swish_slope(spatial_pre)
    grads, spatial_pair, extras = batch_backward(
        [spatial_grad],
        [spatial_normed],
        [spatial_stats[1]],
        [spatial_gain],
        reduced,
        reduced_total,
        (),
    )
    spatial_pair = spatial_pair[0]
    spatial_low = grads[0].astype(jnp.bfloat16).reshape(-1, local_bottleneck)
    spatial_weight_grad = contract_rows(second_taps, spatial_low).reshape(
        3, 3, bottleneck, local_bottleneck
    )
    second_tap_grad = contract_cols(spatial_low, spatial_full.reshape(9 * bottleneck, -1))
    reduce_act_grad = untap(second_tap_grad.reshape(count, half, half, -1), 1, half)
    reduce_grad = reduce_act_grad * reduced_mask * swish_slope(reduce_pre)
    grads, reduce_pair, extras = batch_backward(
        [reduce_grad],
        [reduce_normed],
        [reduce_stats[1]],
        [reduce_gain],
        reduced,
        reduced_total,
        (),
    )
    reduce_pair = reduce_pair[0]
    reduce_low = grads[0].astype(jnp.bfloat16).reshape(-1, local_bottleneck)
    reduce_weight_grad = contract_rows(block_flat, reduce_low)
    first_partial = contract_cols(reduce_low, reduce_full).reshape(count, half, half, -1)
    first_out_grad = first_partial + second_grad
    first_grad = first_out_grad * reduced_mask * swish_slope(first_sum)
    expand_grad, squeeze_grad, excite_grad, squeeze_bias_grad, excite_bias_grad = (
        excite_backward(
            first_grad, expand_pre, reduced, pixels, first_saved, squeeze_full, excite_full
        )
    )
    grads, pairs, extras = batch_backward(
        [expand_grad, first_grad],
        [expand_normed, project_normed],
        [expand_stats[1], project_stats[1]],
        [expand_gain, project_gain],
        reduced,
        reduced_total,
        (squeeze_bias_grad, excite_bias_grad),
    )
    expand_pair, project_pair = (pairs[0], pairs[1])
    squeeze_bias_total, excite_bias_total = (extras[0], extras[1])
    expand_local = grads[0].astype(jnp.bfloat16)
    expand_low = expand_local
    expand_flat = expand_low.reshape(-1, expand_low.shape[3])
    expand_weight_grad = contract_rows(stride_flat, expand_flat)
    stride_act_grad = contract_cols(expand_flat, expand_full).reshape(count, half, half, -1)
    project_low = grads[1].astype(jnp.bfloat16).reshape(-1, grads[1].shape[3])
    project_weight_grad = contract_rows(strided_flat, project_low)
    strided_grad = contract_cols(project_low, project_full).reshape(
        count, half, half, channels_in
    )
    stride_grad = stride_act_grad * reduced_mask * swish_slope(stride_pre)
    grads, stride_pair, extras = batch_backward(
        [stride_grad],
        [stride_normed],
        [stride_stats[1]],
        [stride_gain],
        reduced,
        reduced_total,
        (),
    )
    stride_pair = stride_pair[0]
    stride_low = grads[0].astype(jnp.bfloat16).reshape(-1, local_bottleneck)
    stride_weight_grad = contract_rows(stride_taps, stride_low).reshape(
        3, 3, bottleneck, local_bottleneck
    )
    first_tap_grad = contract_cols(stride_low, stride_full.reshape(9 * bottleneck, -1))
    entry_act_grad = untap(first_tap_grad.reshape(count, half, half, -1), 2, side)
    entry_grad = entry_act_grad * inside[..., None] * swish_slope(entry_pre)
    grads, entry_pair, extras = batch_backward(
        [entry_grad], [entry_normed], [entry_stats[1]], [entry_gain], inside, inside_total, ()
    )
    entry_pair = entry_pair[0]
    entry_low = grads[0].astype(jnp.bfloat16).reshape(-1, local_bottleneck)
    entry_weight_grad = contract_rows(picture.reshape(-1, channels_in), entry_low)
    picture_partial = contract_cols(entry_low, entry_full).reshape(
        count, side, side, channels_in
    )
    picture_partial = picture_partial + lax.pad(
        strided_grad, jnp.float32(0.0), ((0, 0, 0), (0, 1, 1), (0, 1, 1), (0, 0, 0))
    )

    def own_vector(value):
        return lax.psum_scatter(value, "mp", scatter_dimension=0, tiled=True)

    picture_grad = lax.all_to_all(
        picture_partial.astype(jnp.bfloat16)[None], "mp", split_axis=4, concat_axis=0, tiled=True
    ).astype(jnp.float32)
    result = lax.all_to_all(output[None], "mp", split_axis=4, concat_axis=0, tiled=True)
    return (
        result,
        picture_grad,
        own_part(entry_weight_grad, 0, 1),
        own_vector(entry_pair[0]),
        own_vector(entry_pair[1]),
        own_part(stride_weight_grad, 2, 3),
        own_vector(stride_pair[0]),
        own_vector(stride_pair[1]),
        own_part(expand_weight_grad, 1, 0),
        own_vector(expand_pair[0]),
        own_vector(expand_pair[1]),
        own_part(project_weight_grad, 0, 1),
        own_vector(project_pair[0]),
        own_vector(project_pair[1]),
        own_part(squeeze_grad, 1, 0),
        lax.psum(squeeze_bias_total, "mp"),
        own_part(excite_grad, 0, 1),
        own_vector(excite_bias_total),
        own_part(reduce_weight_grad, 0, 1),
        own_vector(reduce_pair[0]),
        own_vector(reduce_pair[1]),
        own_part(spatial_weight_grad, 2, 3),
        own_vector(spatial_pair[0]),
        own_vector(spatial_pair[1]),
        own_part(widen_weight_grad, 1, 0),
        own_vector(widen_pair[0]),
        own_vector(widen_pair[1]),
        own_part(shrink_grad, 1, 0),
        lax.psum(shrink_bias_total, "mp"),
        own_part(gating_grad, 0, 1),
        own_vector(gating_bias_total),
    )


def solution(mesh):
    in_specs = (
        P(None, "dp", None, None, None),
        P(None, "dp", None),
        P("dp", "mp"),
        P("mp"),
        P("mp"),
        P(None, None, "dp", "mp"),
        P("mp"),
        P("mp"),
        P("mp", "dp"),
        P("mp"),
        P("mp"),
        P("dp", "mp"),
        P("mp"),
        P("mp"),
        P("mp", "dp"),
        P(),
        P("dp", "mp"),
        P("mp"),
        P("dp", "mp"),
        P("mp"),
        P("mp"),
        P(None, None, "dp", "mp"),
        P("mp"),
        P("mp"),
        P("mp", "dp"),
        P("mp"),
        P("mp"),
        P("mp", "dp"),
        P(),
        P("dp", "mp"),
        P("mp"),
        P(None, "dp", None, None, "mp"),
    )
    out_specs = (
        P(None, "dp", None, None, "mp"),
        P(None, "dp", None, None, "mp"),
        P("dp", "mp"),
        P("mp"),
        P("mp"),
        P(None, None, "dp", "mp"),
        P("mp"),
        P("mp"),
        P("mp", "dp"),
        P("mp"),
        P("mp"),
        P("dp", "mp"),
        P("mp"),
        P("mp"),
        P("mp", "dp"),
        P(),
        P("dp", "mp"),
        P("mp"),
        P("dp", "mp"),
        P("mp"),
        P("mp"),
        P(None, None, "dp", "mp"),
        P("mp"),
        P("mp"),
        P("mp", "dp"),
        P("mp"),
        P("mp"),
        P("mp", "dp"),
        P(),
        P("dp", "mp"),
        P("mp"),
    )
    shards = fused_shards if dict(mesh.shape) == {"dp": 8, "mp": 4} else plain_shards
    return jax.shard_map(shards, mesh=mesh, in_specs=in_specs, out_specs=out_specs, check_vma=False)
```

```python
import functools

import jax
import jax.numpy as jnp
from jax import lax
from jax.experimental import pallas as pl
from jax.experimental.pallas import tpu as pltpu
from jax.sharding import PartitionSpec as P

eps_norm = 1e-05
highest = lax.Precision.HIGHEST
BF = jnp.bfloat16
F32 = jnp.float32
MESH = pl.DeviceIdType.MESH

TENSORS = {
    "E": (128, 512, 1, "E"),
    "P": (128, 2048, 1, "P"),
    "S": (576, 512, 1, "S"),
    "X": (512, 256, 0, "X"),
    "A": (32, 2048, 1, "A"),
    "R": (256, 512, 1, "R"),
    "T": (576, 512, 1, "S"),
    "V": (512, 256, 0, "X"),
    "B": (32, 2048, 1, "A"),
}
NAMES = list(TENSORS)
PIECES = {
    "E": [(0, 128)],
    "P": [(0, 32), (32, 32), (64, 32), (96, 32)],
    "S": [(0, 128), (128, 128), (256, 128), (384, 192)],
    "X": [(0, 128), (128, 128)],
    "A": [(0, 32)],
    "R": [(0, 128), (128, 128)],
    "T": [(0, 128), (128, 128), (256, 128), (384, 192)],
    "V": [(0, 128), (128, 128)],
    "B": [(0, 32)],
}
ORDER = [(n, i) for n in NAMES for i in range(len(PIECES[n]))]
INDEX = {piece: i for i, piece in enumerate(ORDER)}
AG_Z_LAST = ()
RS_Z_LAST = ()
AG_MORE = {3: (), 4: ()}
RS_MORE = {3: (), 4: ()}
ZLAG = 5
SLOTS = (0, 1, 2, 6, 9, 10)
LAST = {n: INDEX[n, len(PIECES[n]) - 1] for n in NAMES}
COUNT = len(ORDER)
LEAD, LAG, RLAG = 3, 2, 3
OPT = ()
TICKS = "bch"
STARTS = 1
PUMPS = "ABCDEFGHIJKLMNOPQRSUVWXY"
CLASSES = {"E": (128, 128), "P": (128, 512), "S": (576, 128), "X": (128, 256), "A": (32, 512), "R": (256, 128)}
Q = 192
VMEM_LIMIT = 64 * 2**20
WIDE = 2048
EXCHANGES = {
    "entry": (4, 512), "stride": (2, 512), "xp": (4, 2048), "reduce": (2, 512), "spatial": (2, 512), "widen": (2, 2048),
    "widen_b": (4, 2048), "spatial_b": (2, 512), "reduce_b": (2, 512), "xp_b": (4, 2048), "bias_b": (2, 2048),
    "stride_b": (2, 512), "entry_b": (2, 512),
}
EX = {n: i % 2 for i, n in enumerate(n for n in EXCHANGES if n != "bias_b")}
EX["bias_b"] = 2
ROW = {"entry": 0, "stride": 2, "reduce": 4, "spatial": 6, "expand": 8, "project": 16, "widen": 24, "excite": 32, "gating": 36,
       "squeeze": 40, "shrink": 41}
SMALL = 48
NORM512 = {"entry": 0, "stride": 1, "reduce": 2, "spatial": 3}
NORM2048 = {"expand": 0, "project": 1, "widen": 2}


def sigmoid(v):
    return 0.5 + 0.5 * jnp.tanh(0.5 * v)


def dot(a, b):
    return jnp.dot(a, b, preferred_element_type=F32)


def dot_cols(a, b):
    return lax.dot_general(a, b, (((1,), (1,)), ((), ())), preferred_element_type=F32)


def dot_rows(a, b):
    return lax.dot_general(a, b, (((0,), (0,)), ((), ())), preferred_element_type=F32)


def halves(v):
    high = v.astype(BF)
    return high, (v - high.astype(F32)).astype(BF)


def exact(fn, v, w):
    high, low = halves(v)
    return fn(high, w) + fn(low, w)


def outer(a, b):
    ah, al = halves(a)
    bh, bl = halves(b)
    af, alf, bf, blf = ah.astype(F32), al.astype(F32), bh.astype(F32), bl.astype(F32)
    left = jnp.concatenate([af, af, alf, jnp.zeros_like(af)], axis=0).astype(BF)
    right = jnp.concatenate([bf, blf, bf, jnp.zeros_like(bf)], axis=0).astype(BF)
    return dot_rows(left, right)


def lanes(v, times):
    return jnp.concatenate([v] * times, axis=1) if times > 1 else v


def scratch_list():
    s = {}
    for n, (r, c, _, _) in TENSORS.items():
        s["W" + n] = pltpu.VMEM((4, 2, r, c), BF)
    for k, (r, c) in CLASSES.items():
        s["RC" + k] = pltpu.VMEM((2, 4, 2, r, c), BF)
        s["R1" + k] = pltpu.VMEM((4, r, c), BF)
        s["R2" + k] = pltpu.VMEM((2, 4, r, c), BF)
        s["RZ" + k] = pltpu.VMEM((3, r, c), BF)
    for n, (r, c) in EXCHANGES.items():
        s["X_" + n] = pltpu.VMEM((8, r, c), F32)
    s["picT"] = pltpu.VMEM((768, 1024), BF)
    s["stage"] = pltpu.VMEM((768, 1024), BF)
    s["taps1"] = pltpu.VMEM((Q, 4608), BF)
    s["taps2"] = pltpu.VMEM((Q, 4608), BF)
    s["act_e"] = pltpu.VMEM((Q, WIDE), BF)
    s["act_s"] = pltpu.VMEM((Q, 512), BF)
    s["act_p"] = pltpu.VMEM((Q, 512), BF)
    s["first"] = pltpu.VMEM((Q, WIDE), BF)
    s["cotb"] = pltpu.VMEM((Q, WIDE), BF)
    s["g1"] = pltpu.VMEM((Q, WIDE), BF)
    s["g2"] = pltpu.VMEM((Q, WIDE), BF)
    s["gs"] = pltpu.VMEM((Q, 512), BF)
    s["shift"] = pltpu.VMEM((9, Q, Q), BF)
    s["perm"] = pltpu.VMEM((256, 256), BF)
    for n in ("e_raw", "x_raw", "j_raw", "w_raw", "sg"):
        s[n] = pltpu.VMEM((Q, WIDE), F32)
    for n in ("s_raw", "r_raw", "p_raw", "gq", "acc"):
        s[n] = pltpu.VMEM((Q, 512), F32)
    s["sgrad"] = pltpu.VMEM((Q, 1024), F32)
    s["insm"] = pltpu.VMEM((768, 128), F32)
    s["redm"] = pltpu.VMEM((Q, 128), F32)
    s["pix"] = pltpu.VMEM((8, 128), F32)
    s["cnt"] = pltpu.VMEM((8, 512), F32)
    s["gv5"] = pltpu.VMEM((8, 512), F32)
    s["gv20"] = pltpu.VMEM((8, WIDE), F32)
    s["nv5"] = pltpu.VMEM((4, 8, 512), F32)
    s["nv20"] = pltpu.VMEM((3, 8, WIDE), F32)
    for n in ("isum1", "isum2", "pool1", "pool2", "scale1", "scale2", "pg", "G0", "G1", "gate"):
        s[n] = pltpu.VMEM((8, WIDE), F32)
    for n in ("inner1", "inner2", "ing"):
        s[n] = pltpu.VMEM((8, 128), F32)
    s["params"] = pltpu.VMEM((SMALL, 128), F32)
    for n, _, rows in VECTORS:
        s["v_" + n] = pltpu.VMEM((rows, 128), F32)
    for n in ("A", "B"):
        s["in" + n] = pltpu.VMEM((32, 512), BF)
    s["PR"] = pltpu.VMEM((4, SMALL, 128), F32)
    s["FS"] = pltpu.VMEM((4, SMALL, 128), F32)
    s["FR"] = pltpu.VMEM((4, SMALL, 128), F32)
    dma = pltpu.SemaphoreType.DMA
    s["ag_s"] = dma((COUNT, 11))
    s["ag_r"] = dma((COUNT, 11))
    s["loc"] = dma((COUNT + 4,))
    s["vec"] = dma((len(VECTORS) + 4,))
    s["rs_s"] = dma((COUNT, 11))
    s["rs_r"] = dma((COUNT, 11))
    s["st_s"] = dma((3, 7))
    s["st_r"] = dma((3, 8))
    s["mp_s"] = dma((5, 4))
    s["mp_r"] = dma((5, 4))
    s["free"] = pltpu.SemaphoreType.REGULAR((3,))
    return s


VECTORS = []
for _n in ("entry", "stride", "reduce", "spatial"):
    VECTORS += [(_n + "_gain", ROW[_n], 1), (_n + "_shift", ROW[_n] + 1, 1)]
for _n in ("expand", "project", "widen"):
    VECTORS += [(_n + "_gain", ROW[_n], 4), (_n + "_shift", ROW[_n] + 4, 4)]
VECTORS += [("excite_bias", ROW["excite"], 4), ("gating_bias", ROW["gating"], 4)]
VECTORS += [("squeeze_bias", ROW["squeeze"], 1), ("shrink_bias", ROW["shrink"], 1)]
PLAIN = [n for n in NAMES if n not in ("A", "B")]
IN_NAMES = ["images", "sizes", "cot_in"] + ["in" + n for n in PLAIN] + ["sqA", "exA", "sqB", "exB"] + [v[0] for v in VECTORS]
OUT_NAMES = ["result", "igrad"] + ["out" + n for n in NAMES] + ["small"]
LAST_IN = ["result", "igrad"] + ["out" + n for n in NAMES] + ["small"]
LAST_OUT = ["f_result", "f_igrad"] + ["f_" + n for n in PLAIN] + ["f_sqA", "f_exA", "f_sqB", "f_exB"] + [v[0] for v in VECTORS]


def last_body(*refs):
    g = dict(zip(LAST_IN + LAST_OUT, refs))
    step = pl.program_id(0)

    @pl.when(step == 0)
    def _():
        for n in PLAIN:
            g["f_" + n][...] = g["out" + n][...]
        for n in "AB":
            g["f_sq" + n][...] = g["out" + n][0:16, :]
            g["f_ex" + n][...] = g["out" + n][16:32, :]
        for n, row, rows in VECTORS:
            g[n][...] = g["small"][row : row + rows, :]

    g["f_igrad"][...] = g["igrad"][...].astype(F32)
    g["f_result"][...] = g["result"][...]


class Copy:
    def __init__(self, *given):
        self.given = given

    def made(self):
        src, dst, ss, rs, dev = self.given
        return pltpu.make_async_remote_copy(
            src_ref=src, dst_ref=dst, send_sem=ss, recv_sem=rs, device_id=dev, device_id_type=MESH
        )

    def start(self, priority=0):
        self.made().start(priority=priority)

    def wait_recv(self):
        self.made().wait_recv()

    def wait_send(self):
        self.made().wait_send()


def body(*refs):
    names = IN_NAMES + OUT_NAMES + list(scratch_list())
    g = dict(zip(names, refs))

    class NS:
        def __getattr__(self, k):
            return g[k]

    s = NS()
    d = lax.axis_index("dp")
    m = lax.axis_index("mp")
    z, y = d // 2, lax.rem(d, 2)
    x, c = m // 2, lax.rem(m, 2)
    mx = (1 - x) * 2 + c
    mc = x * 2 + (1 - c)
    whole = slice(None)
    xdev, ydev, cdev = (d, mx), (z * 2 + (1 - y), m), (d, mc)

    def zdev(k):
        return (lax.rem(z + k, 4) * 2 + y, m)

    def mdev(k):
        return (d, lax.rem(m + k, 4))

    def col(j, w):
        return pl.ds(pl.multiple_of(j * w, w), w)

    def rcopy(src, dst, ss, rs, dev):
        return Copy(src, dst, ss, rs, dev)

    partners = [(lax.rem(z + k // 2, 4) * 2 + lax.rem(y + k % 2, 2), m) for k in range(1, 8)]
    partners += [mdev(k) for k in range(1, 4)]
    vec = [pltpu.make_async_copy(g[v[0]], g["v_" + v[0]], s.vec.at[i]) for i, v in enumerate(VECTORS)]
    for i, n in enumerate("AB"):
        vec += [
            pltpu.make_async_copy(g["sq" + n], g["in" + n].at[pl.ds(0, 16)], s.vec.at[len(VECTORS) + 2 * i]),
            pltpu.make_async_copy(g["ex" + n], g["in" + n].at[pl.ds(16, 16)], s.vec.at[len(VECTORS) + 2 * i + 1]),
        ]
    own_pic = pltpu.make_async_copy(s.images.at[m], s.stage, s.loc.at[COUNT])
    own_pic.start()
    for t in vec:
        t.start()
    barrier = pltpu.get_barrier_semaphore()
    for dev in partners:
        pl.semaphore_signal(barrier, inc=1, device_id=dev, device_id_type=MESH)
    pl.semaphore_wait(barrier, len(partners))

    def part(piece, zs, ys, mi):
        n, i = piece
        rows, columns, dim, _ = TENSORS[n]
        start, size = PIECES[n][i]
        if dim == 1:
            return g["W" + n].at[zs, ys, pl.ds(start, size), col(mi, columns // 4)]
        return g["W" + n].at[zs, ys, col(mi, rows // 4), pl.ds(start, size)]

    def cut(piece):
        n, i = piece
        start, size = PIECES[n][i]
        return (pl.ds(start, size), whole) if TENSORS[n][2] == 1 else (whole, pl.ds(start, size))

    def shard(piece):
        return g["in" + piece[0]].at[cut(piece)]

    def ag(p, slot, region, dev, src=None):
        i = INDEX[p]
        return rcopy(region if src is None else src, region, s.ag_s.at[i, slot], s.ag_r.at[i, slot], dev)

    def place(p):
        return pltpu.make_async_copy(shard(p), part(p, z, y, m), s.loc.at[INDEX[p]])

    def ag_copies(p):
        own = part(p, z, y, m)
        out, here = {}, {}
        if p in AG_Z_LAST:
            out[0] = [ag(p, 3, own, xdev, shard(p)), ag(p, 4, own, ydev, shard(p))]
            here[0] = [(3, part(p, z, y, mx)), (4, part(p, z, 1 - y, m))]
            out[1] = [ag(p, 5, part(p, z, y, mx), ydev)]
            here[1] = [(5, part(p, z, 1 - y, mx))]
            out[2] = [ag(p, SLOTS[k - 1 + 3 * xx], part(p, z, whole, xx * 2 + c), zdev(k)) for k in range(1, 4) for xx in range(2)]
            here[2] = [
                (SLOTS[k - 1 + 3 * xx], part(p, lax.rem(z + 4 - k, 4), whole, xx * 2 + c)) for k in range(1, 4) for xx in range(2)
            ]
        else:
            share = 3 if INDEX[p] in AG_MORE[3] else 4 if INDEX[p] in AG_MORE[4] else 2
            low, high = pl.ds(0, share), pl.ds(share, 4 - share)
            out[0] = [ag(p, k - 1, own, zdev(k), shard(p)) for k in range(1, 4)]
            here[0] = [(k - 1, part(p, lax.rem(z + 4 - k, 4), y, m)) for k in range(1, 4)]
            out[1] = [ag(p, 3, part(p, whole, y, m), xdev), ag(p, 4, part(p, whole, y, m), ydev)]
            here[1] = [(3, part(p, whole, y, mx)), (4, part(p, whole, 1 - y, m))]
            out[2] = [ag(p, 5, part(p, low, y, mx), ydev)]
            here[2] = [(5, part(p, low, 1 - y, mx))]
            if share < 4:
                out[2] += [ag(p, 6, part(p, high, 1 - y, m), xdev)]
                here[2] += [(6, part(p, high, 1 - y, mx))]
        out[3] = [ag(p, 7 + xx, part(p, whole, whole, xx * 2 + c), cdev) for xx in range(2)]
        here[3] = [(7 + xx, part(p, whole, whole, xx * 2 + (1 - c))) for xx in range(2)]
        return out, here

    def landed(p, here):
        for slot, region in here:
            ag(p, slot, region, cdev).wait_recv()

    def ag_z(p):
        place(p).start()
        for t in ag_copies(p)[0][0]:
            t.start()

    def ag_1(p):
        out, here = ag_copies(p)
        place(p).wait()
        landed(p, here[0])
        for t in out[1]:
            t.start()

    def ag_2(p):
        out, here = ag_copies(p)
        landed(p, here[1])
        for t in out[2]:
            t.start()

    def ag_c(p):
        out, here = ag_copies(p)
        landed(p, here[2])
        for t in out[3]:
            t.start()

    def ag_drain(n):
        if "ag" in OPT:
            return
        for i in range(len(PIECES[n])):
            for copies in ag_copies((n, i))[0].values():
                for t in copies:
                    t.wait_send()

    def stop(t):
        pass

    ticks = {"k": 0}

    def tick():
        if "ag" in OPT:
            return
        k = ticks["k"]
        ticks["k"] = k + 1
        for stage, lags in ((ag_c, (2 * LAG, 2 * LAG)), (ag_2, (LAG, 0)), (ag_1, (0, -1)), (ag_z, (-LEAD, -LEAD))):
            for slow in range(2):
                j = k - lags[slow]
                if 0 <= j < COUNT and (ORDER[j] in AG_Z_LAST) == bool(slow):
                    stage(ORDER[j])

    def mark(tag):
        for t in TICKS:
            if t == tag:
                if ticks["k"] < COUNT + 2 * LAG:
                    tick()

    def need(n):
        if "ag" in OPT:
            return
        while ticks["k"] <= LAST[n] + 2 * LAG:
            tick()
        for i in range(len(PIECES[n])):
            landed((n, i), ag_copies((n, i))[1][3])

    def loop(count, fn, unroll=1):
        def step(j, carry):
            fn(j)
            return carry

        lax.fori_loop(0, count, step, 0, unroll=unroll)

    def rs(p, slot, region, landing, dev):
        i = INDEX[p]
        return rcopy(region, landing, s.rs_s.at[i, slot], s.rs_r.at[i, slot], dev)

    credits = {"T": 0, "V": 1, "B": 2}
    takes = {"S": ("T", 0), "X": ("V", 1), "A": ("B", 2)}
    active = []

    def bump(region, extra):
        region[...] = region[...] + extra

    def reduce_scatter(p):
        n, piece = p
        k = TENSORS[n][3]
        rc, r1, r2, rz = g["RC" + k], g["R1" + k], g["R2" + k], g["RZ" + k]
        c_ = cut(p)
        pair = (pl.ds(0, 2),)
        four = (pl.ds(0, 4),)
        swap = [
            rs(p, xx, part(p, whole, whole, xx * 2 + (1 - c)), rc.at[(xx, pl.ds(0, 4), pl.ds(0, 2)) + c_], cdev) for xx in range(2)
        ]
        z_last = p not in RS_Z_LAST
        first, second, third = [], [], []
        if z_last:
            share = 3 if INDEX[p] in RS_MORE[3] else 4 if INDEX[p] in RS_MORE[4] else 2
            low, high = pl.ds(0, 4 - share), pl.ds(4 - share, share)
            if share < 4:
                first += [rs(p, 2, part(p, low, 1 - y, mx), r1.at[(pl.ds(0, 4 - share),) + c_], xdev)]
            first += [rs(p, 3, part(p, high, 1 - y, mx), r1.at[(pl.ds(4 - share, share),) + c_], ydev)]
            second = [
                rs(p, 4, part(p, whole, y, mx), r2.at[(0, pl.ds(0, 4)) + c_], xdev),
                rs(p, 5, part(p, whole, 1 - y, m), r2.at[(1, pl.ds(0, 4)) + c_], ydev),
            ]
            third = [rs(p, 5 + k, part(p, lax.rem(z + k, 4), y, m), rz.at[(k - 1,) + c_], zdev(k)) for k in range(1, 4)]
        else:
            for k in range(1, 4):
                for xx in range(2):
                    landing = r2.at[(k - 1, pl.ds(xx * 2, 2)) + c_] if k < 3 else r1.at[(pl.ds(xx * 2, 2),) + c_]
                    first += [rs(p, SLOTS[k - 1 + 3 * xx], part(p, lax.rem(z + k, 4), whole, xx * 2 + c), landing, zdev(k))]
            second = [rs(p, 3, part(p, z, 1 - y, mx), rz.at[(0,) + c_], ydev)]
            third = [rs(p, 4, part(p, z, y, mx), rz.at[(1,) + c_], xdev), rs(p, 5, part(p, z, 1 - y, m), rz.at[(2,) + c_], ydev)]
        for t in swap:
            t.start()
        yield
        for t in swap:
            t.wait_recv()

        def add_c(j):
            zz, yy = j // 2, lax.rem(j, 2)
            for xx in range(2):
                bump(part(p, zz, yy, xx * 2 + c), rc[(xx, zz, yy) + c_])

        loop(8, add_c)
        for t in first:
            t.start()
        for _ in range(RLAG if z_last else ZLAG):
            yield
        for t in first:
            t.wait_recv()
        if z_last:
            for h in range(4 - share):
                bump(part(p, h, 1 - y, m), r1[(h,) + c_])
            for h in range(share):
                bump(part(p, 4 - share + h, y, mx), r1[(4 - share + h,) + c_])
        else:
            for yy in range(2):
                for xx in range(2):
                    got = [r2[(0, xx * 2 + yy) + c_], r2[(1, xx * 2 + yy) + c_], r1[(xx * 2 + yy,) + c_]]
                    bump(part(p, z, yy, xx * 2 + c), (got[0].astype(F32) + got[1].astype(F32) + got[2].astype(F32)).astype(BF))
        for t in second:
            t.start()
        for _ in range(RLAG if z_last else 1):
            yield
        for t in second:
            t.wait_recv()
        if z_last:

            def add_2(zz):
                bump(part(p, zz, y, m), (r2[(0, zz) + c_].astype(F32) + r2[(1, zz) + c_].astype(F32)).astype(BF))

            loop(4, add_2)
        else:
            bump(part(p, z, y, mx), rz[(0,) + c_])
        for t in third:
            t.start()
        for _ in range(RLAG if z_last else 1):
            yield
        for t in third:
            t.wait_recv()
        total = part(p, z, y, m)[...].astype(F32)
        for k in range(0 if z_last else 1, 3):
            total = total + rz[(k,) + c_].astype(F32)
        g["out" + n][c_] = total
        if n in credits and piece == len(PIECES[n]) - 1:
            for dev in [xdev, ydev, cdev] + [zdev(k) for k in range(1, 4)]:
                pl.semaphore_signal(s.free.at[credits[n]], inc=1, device_id=dev, device_id_type=MESH)
        for t in swap + first + second + third:
            t.wait_send()

    waiting = []

    def pump():
        for item in list(active):
            try:
                next(item[1])
            except StopIteration:
                active.remove(item)
        for _ in range(STARTS):
            if not waiting:
                return
            n, i = waiting[0]
            if n in takes and i == 0:
                if any(item[0][0] == takes[n][0] for item in active):
                    return
                pl.semaphore_wait(s.free.at[takes[n][1]], 6)
            gen = reduce_scatter(waiting.pop(0))
            active.append(((n, i), gen))
            next(gen)

    def pumps(tag):
        for t in PUMPS:
            if t == tag:
                pump()

    def begin(n, pieces=None):
        if "rs" in OPT or "no" + n in OPT:
            return
        for i in range(len(PIECES[n])) if pieces is None else pieces:
            waiting.append((n, i))

    def st_peers():
        return [lax.rem(z + k // 2, 4) * 2 + lax.rem(y + k % 2, 2) for k in range(1, 8)]

    def send_stats(e):
        buf, i = g["X_" + e], EX[e]
        if "stats" in OPT:
            return
        for k, dd in enumerate(st_peers()):
            rcopy(buf.at[d], buf.at[d], s.st_s.at[i, k], s.st_r.at[i, d], (dd, m)).start(priority=1 if 'prio' in OPT else 0)

    def get_stats(e):
        buf, i = g["X_" + e], EX[e]
        for k, dd in enumerate([] if "stats" in OPT else st_peers()):
            rcopy(buf.at[dd], buf.at[dd], s.st_s.at[i, k], s.st_r.at[i, dd], (dd, m)).wait_recv()
        for k, dd in enumerate([] if "stats" in OPT else st_peers()):
            rcopy(buf.at[d], buf.at[d], s.st_s.at[i, k], s.st_r.at[i, d], (dd, m)).wait_send()
        total = buf[0]
        for k in range(1, 8):
            total = total + buf[k]
        return total

    def mp_copies(i, src, dst):
        return [rcopy(src(lax.rem(m + k, 4)), dst(m), s.mp_s.at[i, k], s.mp_r.at[i, k], mdev(k)) for k in range(1, 4)]

    def mp_wait(i, src, dst, recv=True, send=True):
        for k in range(1, 4):
            if recv:
                rcopy(src(m), dst(lax.rem(m + 4 - k, 4)), s.mp_s.at[i, k], s.mp_r.at[i, k], mdev(k)).wait_recv()
            if send:
                rcopy(src(lax.rem(m + k, 4)), dst(m), s.mp_s.at[i, k], s.mp_r.at[i, k], mdev(k)).wait_send()

    cot_src, cot_dst = (lambda j: s.cot_in.at[j]), (lambda j: s.cotb.at[:, col(j, 512)])
    par_src, par_dst = (lambda j: s.params), (lambda j: s.PR.at[j])
    res_src, res_dst = (lambda j: s.g2.at[:, col(j, 512)]), (lambda j: s.result.at[j])
    img_src, img_dst = (lambda j: s.stage.at[:, col(j, 256)]), (lambda j: s.igrad.at[j])
    fin_src, fin_dst = (lambda j: s.FS.at[j]), (lambda j: s.FR.at[j])

    if "ag" not in OPT:
        for p in ORDER[:LEAD]:
            ag_z(p)
    for t in vec:
        t.wait()
    for n, row, rows in VECTORS:
        s.params[row : row + rows, :] = g["v_" + n][...]
    s.params[42:SMALL, :] = jnp.zeros((SMALL - 42, 128), F32)
    for t in mp_copies(1, par_src, par_dst):
        t.start()
    s.PR[m] = s.params[...]

    if "start0" in OPT:
        mp_wait(1, par_src, par_dst)
        own_pic.wait()
        return
    r64 = lax.broadcasted_iota(jnp.int32, (64, 128), 0)
    p64, q64 = r64 >> 3, r64 & 7
    s.pix[...] = jnp.ones((8, 128), F32)
    for i in range(3):
        high, wide = s.sizes[m, i, 0], s.sizes[m, i, 1]
        for pa in range(2):
            for pb in range(2):
                ok = (2 * p64 + pa < high) & (2 * q64 + pb < wide)
                s.insm[(pa * 2 + pb) * Q + i * 64 : (pa * 2 + pb) * Q + i * 64 + 64, :] = jnp.where(ok, 1.0, 0.0).astype(F32)
        ok = (2 * p64 < high) & (2 * q64 < wide)
        mask = jnp.where(ok, 1.0, 0.0).astype(F32)
        s.redm[i * 64 : i * 64 + 64, :] = mask
        s.pix[i : i + 1, :] = jnp.sum(mask, axis=0, keepdims=True)
    r8 = lax.broadcasted_iota(jnp.int32, (8, 128), 0)
    real = jnp.where(r8 < 3, 1.0, 0.0).astype(F32)

    rr = lax.broadcasted_iota(jnp.int32, (Q, Q), 0)
    cc = lax.broadcasted_iota(jnp.int32, (Q, Q), 1)
    pp, qq = (rr >> 3) & 7, rr & 7
    for t in range(9):
        da, db = t // 3 - 1, t % 3 - 1
        ok = (cc == rr + (da * 8 + db)) & (qq + db >= 0) & (qq + db < 8) & (pp + da >= 0) & (pp + da < 8)
        s.shift[t] = jnp.where(ok, 1.0, 0.0).astype(BF)
    rp = lax.broadcasted_iota(jnp.int32, (256, 256), 0)
    cp_ = lax.broadcasted_iota(jnp.int32, (256, 256), 1)
    source = ((rp >> 3) & 7) * 32 + (rp >> 7) * 16 + (rp & 7) * 2 + ((rp >> 6) & 1)
    s.perm[...] = jnp.where(cp_ == source, 1.0, 0.0).astype(BF)

    own_pic.wait()
    if "start1" in OPT:
        mp_wait(1, par_src, par_dst)
        return
    for i in range(3):
        def permute(j, i=i):
            v = dot(s.perm[...], s.stage[i * 256 : (i + 1) * 256, col(j, 256)]).astype(BF)
            for pl_ in range(4):
                s.picT[pl_ * Q + i * 64 : pl_ * Q + i * 64 + 64, col(j, 256)] = v[pl_ * 64 : pl_ * 64 + 64]

        loop(4, permute)

    tick()
    mp_wait(1, par_src, par_dst)
    for n, r in ROW.items():
        if n in NORM512:
            for k in range(2):
                row = NORM512[n] * 2 + k
                for j in range(4):
                    s.gv5[row : row + 1, j * 128 : j * 128 + 128] = s.PR[j, r + k : r + k + 1, :]
        elif n in NORM2048 or n in ("excite", "gating"):
            first_row = NORM2048[n] * 2 if n in NORM2048 else (6 if n == "excite" else 7)
            for k in range(2 if n in NORM2048 else 1):
                for j in range(4):
                    for h in range(4):
                        b = (j * 4 + h) * 128
                        s.gv20[first_row + k : first_row + k + 1, b : b + 128] = s.PR[j, r + k * 4 + h : r + k * 4 + h + 1, :]
    tick()

    def put(e, row, columns, value):
        g["X_" + e][d, row : row + 1, columns] = value

    def colsum(v):
        return jnp.sum(v, axis=0, keepdims=True)

    def norm_vectors(nv, index, total, square, count, gv, grow):
        mean = total / count
        rstd = lax.rsqrt(square / count - mean * mean + eps_norm)
        a = gv[grow : grow + 1, :] * rstd
        nv[index, 0:1, :] = a
        nv[index, 1:2, :] = gv[grow + 1 : grow + 2, :] - mean * a
        nv[index, 2:3, :] = mean
        nv[index, 3:4, :] = rstd

    def norm_back_vectors(nv, index, gain_grad, shift_grad, count):
        a, mean, rstd = nv[index, 0:1, :], nv[index, 2:3, :], nv[index, 3:4, :]
        w = a * rstd * gain_grad / count
        nv[index, 4:5, :] = a * shift_grad / count - mean * w
        nv[index, 5:6, :] = w

    def activate(raw, index, out):
        for j in range(4):
            b = slice(j * 128, j * 128 + 128)
            pre = raw[:, b] * s.nv5[index, 0:1, b] + s.nv5[index, 1:2, b]
            out[:, b] = (pre * sigmoid(pre) * s.redm[...]).astype(BF)

    def sums_512(e, columns, value, mask, row=0):
        vm = value * mask
        put(e, row, columns, colsum(vm))
        put(e, row + 1, columns, colsum(vm * value))

    def sums_wide(e, columns, value, isum, row):
        total = 0.0
        square = 0.0
        for i in range(3):
            v = value[i * 64 : i * 64 + 64]
            vm = v * lanes(s.redm[i * 64 : i * 64 + 64, :], v.shape[1] // 128)
            si = colsum(vm)
            if isum is not None:
                isum[i : i + 1, columns] = si
            total = total + si
            square = square + colsum(vm * v)
        put(e, row, columns, total)
        put(e, row + 1, columns, square)

    if "compute" in OPT:
        for n in NAMES:
            need(n)
        for n in NAMES:
            ag_drain(n)
        for n in ["B", "V", "T", "R", "A", "X", "P", "S", "E"]:
            for i in range(len(PIECES[n])):
                begin(n, [i])
                pump()
        while active or waiting:
            pump()
        return
    need("E")

    def entry_step(n):
        b = col(n, 256)
        v = dot(s.picT[...], s.WE[:, :, :, b].reshape(1024, 256))
        total = 0.0
        square = 0.0
        for k in range(4):
            vk = v[k * Q : k * Q + Q]
            s.e_raw[:, pl.ds(pl.multiple_of(k * 512 + n * 256, 256), 256)] = vk
            vm = vk * lanes(s.insm[k * Q : k * Q + Q, :], 2)
            total = total + colsum(vm)
            square = square + colsum(vm * vk)
        put("entry", 0, b, total)
        put("entry", 1, b, square)

    loop(2, entry_step)
    put("entry", 2, slice(0, 512), lanes(colsum(s.insm[...]), 4))
    put("entry", 3, slice(0, 512), lanes(colsum(s.redm[...]), 4))
    send_stats("entry")
    mark("a")

    need("P")

    def project_step(n):
        b = col(n, 256)
        v = dot(s.picT[0:Q, :], s.WP[:, :, :, b].reshape(1024, 256))
        s.j_raw[:, b] = v
        sums_wide("xp", b, v, None, 2)

    loop(8, project_step)
    mark("b")
    tot = get_stats("entry")
    s.cnt[0:2, :] = tot[2:4]
    norm_vectors(s.nv5, 0, tot[0:1], tot[1:2], tot[2:3], s.gv5, 0)

    def entry_act_step(j):
        pcol = col(lax.rem(j, 4), 128)
        mask = s.insm[pl.ds(pl.multiple_of((j // 4) * Q, Q), Q), :]
        pre = s.e_raw[:, col(j, 128)] * s.nv5[0, 0:1, pcol] + s.nv5[0, 1:2, pcol]
        s.act_e[:, col(j, 128)] = (pre * sigmoid(pre) * mask).astype(BF)

    loop(16, entry_act_step, 2)
    mark("c")
    for a in range(3):
        for b in range(3):
            t = a * 3 + b
            plane = (2 if a != 1 else 0) + (1 if b != 1 else 0)
            which = (0 if a == 0 else 1) * 3 + (0 if b == 0 else 1)
            v = s.act_e[:, plane * 512 : plane * 512 + 512]
            if which != 4:
                v = dot(s.shift[which], v).astype(BF)
            s.taps1[:, t * 512 : t * 512 + 512] = v

    mark("d")

    def conv3(taps, w, raw, e):
        def step(n):
            b = col(n, 256)
            v = dot(taps[:, 0:512], w[:, :, 0:64, b].reshape(512, 256))
            for t in range(1, 9):
                v = v + dot(taps[:, t * 512 : t * 512 + 512], w[:, :, t * 64 : t * 64 + 64, b].reshape(512, 256))
            raw[:, b] = v
            sums_512(e, b, v, lanes(s.redm[...], 2))

        loop(2, step)

    need("S")
    conv3(s.taps1, s.WS, s.s_raw, "stride")
    send_stats("stride")
    for t in mp_copies(0, cot_src, cot_dst):
        t.start()
    own_cot = pltpu.make_async_copy(cot_src(m), cot_dst(m), s.loc.at[COUNT + 1])
    own_cot.start()
    mark("e")
    need("X")
    tot = get_stats("stride")
    count5 = s.cnt[1:2, :]
    norm_vectors(s.nv5, 1, tot[0:1], tot[1:2], count5, s.gv5, 2)
    activate(s.s_raw, 1, s.act_s)
    mark("f")

    for n in ("isum1", "isum2", "G0", "G1"):
        g[n][...] = jnp.zeros((8, WIDE), F32)

    def widening(act, w, raw, e, isum):
        def step(k):
            b = col(k, 256)
            v = dot(act[...], w[k // 2, lax.rem(k, 2)])
            raw[:, b] = v
            sums_wide(e, b, v, isum, 0)

        loop(8, step)

    widening(s.act_s, s.WX, s.x_raw, "xp", s.isum1)
    send_stats("xp")
    mark("g")
    need("A")
    count20 = lanes(s.cnt[1:2, :], 4)
    tot = get_stats("xp")
    norm_vectors(s.nv20, 0, tot[0:1], tot[1:2], count20, s.gv20, 0)
    norm_vectors(s.nv20, 1, tot[2:3], tot[3:4], count20, s.gv20, 2)

    def squeeze_excite(index, isum, w, bias, gate_row, pool, inner, scale):
        pooled = (s.nv20[index, 0:1, :] * isum[...] / lanes(s.pix[...], 16) + s.nv20[index, 1:2, :]) * lanes(real, 16)
        pool[...] = pooled
        pre = exact(dot_cols, pooled, w[:, :, 0:16, :].reshape(128, WIDE)) + bias
        inner[...] = pre
        gate = exact(dot, pre * sigmoid(pre), w[:, :, 16:32, :].reshape(128, WIDE)) + s.gv20[gate_row : gate_row + 1, :]
        scale[...] = sigmoid(gate)

    squeeze_excite(0, s.isum1, s.WA, s.PR[0, 40:41, :], 6, s.pool1, s.inner1, s.scale1)
    mark("h")

    def first_sum(j, i):
        b, rows = col(j, 128), slice(i * 64, i * 64 + 64)
        pre = s.x_raw[rows, b] * s.nv20[0, 0:1, b] + s.nv20[0, 1:2, b]
        return pre * s.scale1[i : i + 1, b] + (s.j_raw[rows, b] * s.nv20[1, 0:1, b] + s.nv20[1, 1:2, b])

    def first_step(j):
        for i in range(3):
            rows = slice(i * 64, i * 64 + 64)
            v = first_sum(j, i)
            s.first[rows, col(j, 128)] = (v * sigmoid(v) * s.redm[rows, :]).astype(BF)

    loop(16, first_step, 2)
    mark("i")

    need("R")

    def reduce_step(n):
        b = col(n, 256)
        v = dot(s.first[...], s.WR[:, :, :, b].reshape(WIDE, 256))
        s.r_raw[:, b] = v
        sums_512("reduce", b, v, lanes(s.redm[...], 2))

    loop(2, reduce_step)
    send_stats("reduce")
    mark("j")
    tot = get_stats("reduce")
    norm_vectors(s.nv5, 2, tot[0:1], tot[1:2], count5, s.gv5, 4)
    activate(s.r_raw, 2, s.act_p)
    for t in range(9):
        v = s.act_p[...]
        if t != 4:
            v = dot(s.shift[t], v).astype(BF)
        s.taps2[:, t * 512 : t * 512 + 512] = v
    mark("k")
    need("T")
    conv3(s.taps2, s.WT, s.p_raw, "spatial")
    send_stats("spatial")
    mark("l")
    need("V")
    tot = get_stats("spatial")
    norm_vectors(s.nv5, 3, tot[0:1], tot[1:2], count5, s.gv5, 6)
    activate(s.p_raw, 3, s.act_p)
    mark("m")
    widening(s.act_p, s.WV, s.w_raw, "widen", s.isum2)
    send_stats("widen")
    need("B")
    own_cot.wait()
    mp_wait(0, cot_src, cot_dst)
    tot = get_stats("widen")
    norm_vectors(s.nv20, 2, tot[0:1], tot[1:2], count20, s.gv20, 4)
    squeeze_excite(2, s.isum2, s.WB, s.PR[0, 41:42, :], 7, s.pool2, s.inner2, s.scale2)

    def result_step(j):
        b = col(j, 128)
        for i in range(3):
            rows = slice(i * 64, i * 64 + 64)
            raw = s.w_raw[rows, b]
            pre = raw * s.nv20[2, 0:1, b] + s.nv20[2, 1:2, b]
            v = pre * s.scale2[i : i + 1, b] + s.first[rows, b].astype(F32)
            sg = sigmoid(v)
            mask = s.redm[rows, :]
            s.g2[rows, b] = (v * sg * mask).astype(BF)
            grad = s.cotb[rows, b].astype(F32) * mask * (sg * (1.0 + v * (1.0 - sg)))
            s.sg[rows, b] = grad
            s.G0[i : i + 1, b] = colsum(grad)
            s.G1[i : i + 1, b] = colsum(grad * ((raw - s.nv20[2, 2:3, b]) * s.nv20[2, 3:4, b]))

    loop(16, result_step, 2)
    for t in mp_copies(2, res_src, res_dst):
        t.start()
    own_res = pltpu.make_async_copy(res_src(m), res_dst(m), s.loc.at[COUNT + 2])
    own_res.start()

    if "fwd" in OPT:
        for n in NAMES:
            ag_drain(n)
        own_res.wait()
        mp_wait(2, res_src, res_dst)
        return
    def keep512(n, k, v):
        for j in range(4):
            s.FS[j, ROW[n] + k : ROW[n] + k + 1, :] = v[:, j * 128 : j * 128 + 128]

    def keep2048(row, v):
        for j in range(4):
            for h in range(4):
                b = (j * 4 + h) * 128
                s.FS[j, row + h : row + h + 1, :] = v[:, b : b + 128]

    def excite_back(index, isum, w, inner, scale):
        scl = scale[...]
        gate_grad = (s.gv20[index * 2 : index * 2 + 1, :] * s.G1[...] + s.gv20[index * 2 + 1 : index * 2 + 2, :] * s.G0[...]) * (
            scl * (1.0 - scl)
        )
        s.gate[...] = gate_grad
        pre = inner[...]
        sg = sigmoid(pre)
        ing = exact(dot_cols, gate_grad, w[:, :, 16:32, :].reshape(128, WIDE)) * (sg * (1.0 + pre * (1.0 - sg)))
        s.ing[...] = ing
        pix = lanes(s.pix[...], 16)
        pg = exact(dot, ing, w[:, :, 0:16, :].reshape(128, WIDE)) / pix
        s.pg[...] = pg
        spread = (isum[...] - s.nv20[index, 2:3, :] * pix) * s.nv20[index, 3:4, :]
        return (colsum(scl * s.G1[...] + pg * spread), colsum(scl * s.G0[...] + pg * pix), colsum(gate_grad), colsum(ing))

    def excite_weights(n, pool, inner):
        pre = inner[...]
        hidden = pre * sigmoid(pre)
        w = g["W" + n]

        def step(j):
            b = col(j, 512)
            w[:, :, 0:16, b] = outer(s.ing[...], pool[:, b]).astype(BF).reshape(4, 2, 16, 512)
            w[:, :, 16:32, b] = outer(hidden, s.gate[:, b]).astype(BF).reshape(4, 2, 16, 512)

        loop(4, step)

    def wide_grad(index, raw, out, scale):
        def step(j):
            b = col(j, 128)
            for i in range(3):
                rows = slice(i * 64, i * 64 + 64)
                grad, mask = s.sg[rows, b], s.redm[rows, :]
                if scale is not None:
                    grad = grad * scale[i : i + 1, b] + mask * s.pg[i : i + 1, b]
                v = s.nv20[index, 0:1, b] * grad - mask * (s.nv20[index, 4:5, b] + s.nv20[index, 5:6, b] * raw[rows, b])
                out[rows, b] = v.astype(BF)

        loop(16, step, 2)

    def back_sums(e, index, b, grad, raw, mask):
        out = []
        pre = raw * s.nv5[index, 0:1, b] + s.nv5[index, 1:2, b]
        sg = sigmoid(pre)
        grad = grad * mask * (sg * (1.0 + pre * (1.0 - sg)))
        put(e, 0, b, colsum(grad * ((raw - s.nv5[index, 2:3, b]) * s.nv5[index, 3:4, b])))
        put(e, 1, b, colsum(grad))
        return grad

    def narrow_back(e, index, acc, raw):
        for j in range(4):
            b = slice(j * 128, j * 128 + 128)
            s.gq[:, b] = back_sums(e, index, b, acc[:, b], raw[:, b], s.redm[...])

    def narrow_grad(index, raw):
        for j in range(4):
            b = slice(j * 128, j * 128 + 128)
            v = s.nv5[index, 0:1, b] * s.gq[:, b] - s.redm[...] * (s.nv5[index, 4:5, b] + s.nv5[index, 5:6, b] * raw[:, b])
            s.gs[:, b] = v.astype(BF)

    def narrow_stats(e, n):
        tot = get_stats(e)
        keep512(n, 0, tot[0:1])
        keep512(n, 1, tot[1:2])
        norm_back_vectors(s.nv5, NORM512[n], tot[0:1], tot[1:2], s.cnt[0:1, :] if n == "entry" else count5)

    def widening_back(grads, w):
        def step(n):
            rows = col(n, 256)
            v = dot_cols(grads[:, 0:256], w[0, 0, rows, :])
            for k in range(1, 8):
                v = v + dot_cols(grads[:, k * 256 : k * 256 + 256], w[k // 2, k % 2, rows, :])
            s.acc[:, rows] = v

        loop(2, step)

    def widening_weights(n, act, grads):
        ag_drain(n)
        w = g["W" + n]

        def step(k):
            w[k // 2, lax.rem(k, 2)] = dot_rows(act[...], grads[:, col(k, 256)]).astype(BF)

        loop(8, step)
        begin(n)

    def conv3_weights(n, taps):
        ag_drain(n)
        w = g["W" + n]

        def step(t):
            for h in range(2):
                b = slice(h * 256, h * 256 + 256)
                v = dot_rows(taps[:, col(t, 512)], s.gs[:, b]).astype(BF)
                w[:, :, col(t, 64), b] = v.reshape(4, 2, 64, 256)

        loop(9, step)
        begin(n)

    sums = excite_back(2, s.isum2, s.WB, s.inner2, s.scale2)
    for k in range(3):
        put("widen_b", k, slice(0, WIDE), sums[k])
    put("widen_b", 3, slice(0, WIDE), lanes(sums[3], 16))
    send_stats("widen_b")
    ag_drain("B")
    excite_weights("B", s.pool2, s.inner2)
    begin("B")
    tot = get_stats("widen_b")
    pumps("A")
    keep2048(ROW["widen"], tot[0:1])
    keep2048(ROW["widen"] + 4, tot[1:2])
    keep2048(ROW["gating"], tot[2:3])
    for j in range(4):
        s.FS[j, ROW["shrink"] : ROW["shrink"] + 1, :] = tot[3:4, 0:128]
    norm_back_vectors(s.nv20, 2, tot[0:1], tot[1:2], count20)
    wide_grad(2, s.w_raw, s.g1, s.scale2)
    pumps("B")
    widening_back(s.g1, s.WV)
    narrow_back("spatial_b", 3, s.acc, s.p_raw)
    send_stats("spatial_b")
    pumps("C")
    widening_weights("V", s.act_p, s.g1)
    pumps("D")
    narrow_stats("spatial_b", "spatial")
    narrow_grad(3, s.p_raw)
    pumps("E")
    s.acc[...] = jnp.zeros((Q, 512), F32)

    def spatial_back(t):
        v = dot(s.shift[8 - t], s.gs[...]).astype(BF)
        s.acc[...] += dot_cols(v, s.WT[:, :, col(t, 64), :].reshape(512, 512))

    loop(9, spatial_back)
    pumps("F")
    narrow_back("reduce_b", 2, s.acc, s.r_raw)
    send_stats("reduce_b")
    pumps("G")
    conv3_weights("T", s.taps2)
    pumps("H")
    narrow_stats("reduce_b", "reduce")
    narrow_grad(2, s.r_raw)
    pumps("I")

    def reduce_back(k):
        v = dot_cols(s.gs[...], s.WR[k // 2, lax.rem(k, 2)])
        for h in range(2):
            j = k * 2 + h
            b = col(j, 128)
            project_sum = 0.0
            shift_sum = 0.0
            for i in range(3):
                rows = slice(i * 64, i * 64 + 64)
                fs = first_sum(j, i)
                sg = sigmoid(fs)
                grad = (v[rows, h * 128 : h * 128 + 128] + s.sg[rows, b]) * s.redm[rows, :] * (sg * (1.0 + fs * (1.0 - sg)))
                s.sg[rows, b] = grad
                total = colsum(grad)
                s.G0[i : i + 1, b] = total
                s.G1[i : i + 1, b] = colsum(grad * ((s.x_raw[rows, b] - s.nv20[0, 2:3, b]) * s.nv20[0, 3:4, b]))
                shift_sum = shift_sum + total
                project_sum = project_sum + colsum(grad * ((s.j_raw[rows, b] - s.nv20[1, 2:3, b]) * s.nv20[1, 3:4, b]))
            put("xp_b", 2, b, project_sum)
            put("xp_b", 3, b, shift_sum)

    loop(8, reduce_back)
    pumps("J")
    sums = excite_back(0, s.isum1, s.WA, s.inner1, s.scale1)
    put("xp_b", 0, slice(0, WIDE), sums[0])
    put("xp_b", 1, slice(0, WIDE), sums[1])
    send_stats("xp_b")
    put("bias_b", 0, slice(0, WIDE), sums[2])
    put("bias_b", 1, slice(0, WIDE), lanes(sums[3], 16))
    send_stats("bias_b")
    pumps("K")
    ag_drain("R")

    def reduce_weights(k):
        s.WR[k // 2, lax.rem(k, 2)] = dot_rows(s.first[:, col(k, 256)], s.gs[...]).astype(BF)

    loop(8, reduce_weights)
    begin("R")
    pumps("L")
    ag_drain("A")
    excite_weights("A", s.pool1, s.inner1)
    begin("A")
    pumps("M")
    tot = get_stats("xp_b")
    for k, n in enumerate(("expand", "project")):
        keep2048(ROW[n], tot[2 * k : 2 * k + 1])
        keep2048(ROW[n] + 4, tot[2 * k + 1 : 2 * k + 2])
        norm_back_vectors(s.nv20, k, tot[2 * k : 2 * k + 1], tot[2 * k + 1 : 2 * k + 2], count20)
    wide_grad(0, s.x_raw, s.g1, s.scale1)
    pumps("N")
    widening_back(s.g1, s.WX)
    narrow_back("stride_b", 1, s.acc, s.s_raw)
    send_stats("stride_b")
    pumps("O")
    own_res.wait()
    mp_wait(2, res_src, res_dst)
    wide_grad(1, s.j_raw, s.g2, None)

    def project_back(zz):
        w = s.WP[zz].reshape(256, WIDE)
        s.sgrad[:, col(zz, 256)] = dot_cols(s.g2[...], w)

    loop(4, project_back)
    pumps("P")
    widening_weights("X", s.act_s, s.g1)
    pumps("Q")
    ag_drain("P")

    def project_weights(n):
        b = col(n, 256)
        for h in range(2):
            v = dot_rows(s.picT[0:Q, h * 512 : h * 512 + 512], s.g2[:, b]).astype(BF)
            s.WP[2 * h : 2 * h + 2, :, :, b] = v.reshape(2, 2, 128, 256)

    loop(8, project_weights)
    begin("P")
    pumps("R")
    narrow_stats("stride_b", "stride")
    narrow_grad(1, s.s_raw)
    pumps("S")

    for k in range(4):
        pa, pb = k // 2, k % 2
        columns = slice(k * 512, k * 512 + 512)
        first_tap = True
        for a in (0, 2) if pa else (1,):
            for b in (0, 2) if pb else (1,):
                t = a * 3 + b
                which = (0 if a == 0 else 1) * 3 + (0 if b == 0 else 1)
                v = s.gs[...]
                if which != 4:
                    v = dot(s.shift[8 - which], v).astype(BF)
                v = dot_cols(v, s.WS[:, :, t * 64 : t * 64 + 64, :].reshape(512, 512))
                if first_tap:
                    s.w_raw[:, columns] = v
                else:
                    s.w_raw[:, columns] += v
                first_tap = False

    def entry_back(n):
        b = col(n, 128)
        gain_sum = 0.0
        shift_sum = 0.0
        for k in range(4):
            kb = pl.ds(pl.multiple_of(k * 512 + n * 128, 128), 128)
            raw = s.e_raw[:, kb]
            pre = raw * s.nv5[0, 0:1, b] + s.nv5[0, 1:2, b]
            sg = sigmoid(pre)
            grad = s.w_raw[:, kb] * s.insm[k * Q : k * Q + Q, :] * (sg * (1.0 + pre * (1.0 - sg)))
            s.w_raw[:, kb] = grad
            gain_sum = gain_sum + colsum(grad * ((raw - s.nv5[0, 2:3, b]) * s.nv5[0, 3:4, b]))
            shift_sum = shift_sum + colsum(grad)
        put("entry_b", 0, b, gain_sum)
        put("entry_b", 1, b, shift_sum)

    loop(4, entry_back)
    send_stats("entry_b")
    pumps("U")
    conv3_weights("S", s.taps1)
    pumps("V")
    narrow_stats("entry_b", "entry")

    def entry_grad(j):
        pcol = col(lax.rem(j, 4), 128)
        mask = s.insm[pl.ds(pl.multiple_of((j // 4) * Q, Q), Q), :]
        b = col(j, 128)
        v = s.nv5[0, 0:1, pcol] * s.w_raw[:, b] - mask * (s.nv5[0, 4:5, pcol] + s.nv5[0, 5:6, pcol] * s.e_raw[:, b])
        s.act_e[:, b] = v.astype(BF)

    loop(16, entry_grad, 2)
    pumps("W")
    tot = get_stats("bias_b")
    keep2048(ROW["excite"], tot[0:1])
    for j in range(4):
        s.FS[j, ROW["squeeze"] : ROW["squeeze"] + 1, :] = tot[1:2, 0:128]
        for r in range(42, SMALL, 2):
            s.FS[j, r : r + 2, :] = jnp.zeros((2, 128), F32)
    s.FR[m] = s.FS[m]
    for t in mp_copies(4, fin_src, fin_dst):
        t.start()

    def image_grad(zz):
        w = s.WE[zz].reshape(256, 512)
        for k in range(4):
            v = dot_cols(s.act_e[:, k * 512 : k * 512 + 512], w)
            if k == 0:
                v = v + s.sgrad[:, col(zz, 256)]
            s.taps1[:, pl.ds(pl.multiple_of(k * 1024 + zz * 256, 256), 256)] = v.astype(BF)

    loop(4, image_grad)
    for i in range(3):
        def unpermute(j, i=i):
            v = jnp.concatenate(
                [s.taps1[i * 64 : i * 64 + 64, pl.ds(pl.multiple_of(k * 1024 + j * 256, 256), 256)] for k in range(4)], axis=0
            )
            s.stage[i * 256 : i * 256 + 256, col(j, 256)] = dot_rows(s.perm[...], v).astype(BF)

        loop(4, unpermute)
    for t in mp_copies(3, img_src, img_dst):
        t.start()
    own_img = pltpu.make_async_copy(img_src(m), img_dst(m), s.loc.at[COUNT + 3])
    own_img.start()
    pumps("X")
    ag_drain("E")

    def entry_weights(zz):
        v = dot_rows(s.picT[0:Q, col(zz, 256)], s.act_e[:, 0:512])
        for k in range(1, 4):
            v = v + dot_rows(s.picT[k * Q : k * Q + Q, col(zz, 256)], s.act_e[:, k * 512 : k * 512 + 512])
        s.WE[zz] = v.astype(BF).reshape(2, 128, 512)

    loop(4, entry_weights)
    begin("E")
    pumps("Y")
    while active or waiting:
        pump()
    mp_wait(4, fin_src, fin_dst)
    s.small[...] = ((s.FR[0] + s.FR[1]) + s.FR[2]) + s.FR[3]
    own_img.wait()
    mp_wait(3, img_src, img_dst)

def fused_shards(*arrays):
    (images, image_size, entry_weight, entry_gain, entry_shift, stride_weight, stride_gain, stride_shift, expand_weight,
     expand_gain, expand_shift, project_weight, project_gain, project_shift, squeeze_weight, squeeze_bias, excite_weight,
     excite_bias, reduce_weight, reduce_gain, reduce_shift, spatial_weight, spatial_gain, spatial_shift, widen_weight,
     widen_gain, widen_shift, shrink_weight, shrink_bias, gating_weight, gating_bias, cotangent) = arrays
    weights = {
        "E": entry_weight,
        "P": project_weight,
        "S": stride_weight.reshape(576, 128),
        "X": expand_weight,
        "R": reduce_weight,
        "T": spatial_weight.reshape(576, 128),
        "V": widen_weight,
    }
    given = dict(
        entry_gain=entry_gain, entry_shift=entry_shift, stride_gain=stride_gain, stride_shift=stride_shift,
        reduce_gain=reduce_gain, reduce_shift=reduce_shift, spatial_gain=spatial_gain, spatial_shift=spatial_shift,
        expand_gain=expand_gain, expand_shift=expand_shift, project_gain=project_gain, project_shift=project_shift,
        widen_gain=widen_gain, widen_shift=widen_shift, excite_bias=excite_bias, gating_bias=gating_bias,
        squeeze_bias=squeeze_bias, shrink_bias=shrink_bias,
    )
    small = [given[n].reshape(rows, 128) for n, _, rows in VECTORS]
    hbm, vmem = pl.BlockSpec(memory_space=pl.ANY), pl.BlockSpec(memory_space=pltpu.VMEM)
    outs = [jax.ShapeDtypeStruct((4, Q, 512), BF), jax.ShapeDtypeStruct((4, 768, 256), BF)]
    outs += [jax.ShapeDtypeStruct(CLASSES[TENSORS[n][3]], F32) for n in NAMES]
    outs += [jax.ShapeDtypeStruct((SMALL, 128), F32)]
    got = pl.pallas_call(
        body,
        out_shape=outs,
        in_specs=[hbm, pl.BlockSpec(memory_space=pltpu.SMEM), hbm] + [hbm] * (len(PLAIN) + 4 + len(VECTORS)),
        out_specs=[hbm, hbm] + [vmem] * (len(NAMES) + 1),
        scratch_shapes=list(scratch_list().values()),
        compiler_params=pltpu.CompilerParams(collective_id=0, has_side_effects=True, vmem_limit_bytes=VMEM_LIMIT),
        cost_estimate=pl.CostEstimate(flops=14_000_000_000, bytes_accessed=30_000_000, transcendentals=10_000_000),
    )(
        images.reshape(4, 768, 1024), image_size, cotangent.reshape(4, Q, 512), *[weights[n] for n in PLAIN],
        squeeze_weight.T, excite_weight, shrink_weight.T, gating_weight, *small,
    )

    def held(shape):
        return pl.BlockSpec(shape, lambda i: (0, 0))

    kinds = [held(CLASSES[TENSORS[n][3]]) for n in NAMES]
    last = [jax.ShapeDtypeStruct((4, Q, 512), BF), jax.ShapeDtypeStruct((4, 768, 256), F32)]
    last += [jax.ShapeDtypeStruct(CLASSES[TENSORS[n][3]], F32) for n in PLAIN]
    last += [jax.ShapeDtypeStruct(v, F32) for v in ((16, 512),) * 4]
    last += [jax.ShapeDtypeStruct((rows, 128), F32) for _, _, rows in VECTORS]
    blocks = [pl.BlockSpec((1, Q, 512), lambda i: (i, 0, 0)), pl.BlockSpec((1, 768, 256), lambda i: (i, 0, 0))]
    final = pl.pallas_call(
        last_body,
        grid=(4,),
        out_shape=last,
        in_specs=blocks + kinds + [held((SMALL, 128))],
        out_specs=blocks + [held(CLASSES[TENSORS[n][3]]) for n in PLAIN] + [held(v) for v in ((16, 512),) * 4]
        + [held((rows, 128)) for _, _, rows in VECTORS],
        compiler_params=pltpu.CompilerParams(vmem_limit_bytes=VMEM_LIMIT),
        cost_estimate=pl.CostEstimate(flops=1_000_000, bytes_accessed=10_000_000, transcendentals=0),
    )(*got)
    f = dict(zip(LAST_OUT, final))

    def pair(n):
        return f[n + "_gain"].reshape(-1), f[n + "_shift"].reshape(-1)

    return (
        f["f_result"].reshape(cotangent.shape),
        f["f_igrad"].reshape(4, 3, 16, 16, 256),
        f["f_E"], *pair("entry"),
        f["f_S"].reshape(stride_weight.shape), *pair("stride"),
        f["f_X"], *pair("expand"),
        f["f_P"], *pair("project"),
        f["f_sqA"].T, f["squeeze_bias"].reshape(-1), f["f_exA"], f["excite_bias"].reshape(-1),
        f["f_R"], *pair("reduce"),
        f["f_T"].reshape(spatial_weight.shape), *pair("spatial"),
        f["f_V"], *pair("widen"),
        f["f_sqB"].T, f["shrink_bias"].reshape(-1), f["f_exB"], f["gating_bias"].reshape(-1),
    )


def matmul(left, right):
    return jnp.dot(left, right, preferred_element_type=jnp.float32)


def contract_rows(left, right):
    return lax.dot_general(
        left, right, (((0,), (0,)), ((), ())), preferred_element_type=jnp.float32
    )


def contract_cols(left, right):
    return lax.dot_general(
        left, right, (((1,), (1,)), ((), ())), preferred_element_type=jnp.float32
    )


def swish_slope(value):
    sigma = jax.nn.sigmoid(value)
    return sigma * (1.0 + value * (1.0 - sigma))


def pixel_masks(sizes, side):
    half = side // 2
    height = sizes[:, 0]
    breadth = sizes[:, 1]
    places = jnp.arange(side, dtype=jnp.int32)
    inside = (
        (places[None, :, None] < height[:, None, None])
        & (places[None, None, :] < breadth[:, None, None])
    ).astype(jnp.float32)
    halves = jnp.arange(half, dtype=jnp.int32)
    reduced = (
        (halves[None, :, None] < ((height + 1) // 2)[:, None, None])
        & (halves[None, None, :] < ((breadth + 1) // 2)[:, None, None])
    ).astype(jnp.float32)
    return (inside, reduced)


def spatial_taps(field, stride):
    count, side, channels = (field.shape[0], field.shape[1], field.shape[3])
    reach = stride * (side // stride - 1) + 1
    padded = jnp.pad(field, ((0, 0), (1, 1), (1, 1), (0, 0)))
    pieces = []
    for row in range(3):
        for column in range(3):
            pieces.append(
                lax.slice(
                    padded,
                    (0, row, column, 0),
                    (count, row + reach, column + reach, channels),
                    (1, stride, stride, 1),
                )
            )
    return jnp.concatenate(pieces, axis=3)


def untap(grads, stride, side):
    count, out_side = (grads.shape[0], grads.shape[1])
    channels = grads.shape[3] // 9
    reach = stride * (out_side - 1) + 1
    total = jnp.zeros((count, side + 2, side + 2, channels), jnp.float32)
    for row in range(3):
        for column in range(3):
            first = (row * 3 + column) * channels
            piece = grads[:, :, :, first : first + channels]
            total = total + lax.pad(
                piece,
                jnp.float32(0.0),
                (
                    (0, 0, 0),
                    (row, side + 2 - row - reach, stride - 1),
                    (column, side + 2 - column - reach, stride - 1),
                    (0, 0, 0),
                ),
            )
    return total[:, 1 : side + 1, 1 : side + 1, :]


def batch_statistics(fields, mask):
    weights = mask[..., None]
    terms = []
    for field in fields:
        terms.append(jnp.sum(field * weights, axis=(0, 1, 2)))
        terms.append(jnp.sum(field * field * weights, axis=(0, 1, 2)))
    packed, total_vector = lax.psum((jnp.concatenate(terms), jnp.sum(mask).reshape(1)), "dp")
    total = total_vector[0]
    result = []
    offset = 0
    for field in fields:
        breadth = field.shape[3]
        mean = packed[offset : offset + breadth] / total
        second = packed[offset + breadth : offset + 2 * breadth] / total
        result.append((mean, lax.rsqrt(second - mean * mean + eps_norm)))
        offset = offset + 2 * breadth
    return (result, total)


def standardize(raw, statistics, gain, shift):
    mean, scale = statistics
    normed = (raw - mean) * scale
    return (normed, normed * gain + shift)


def batch_backward(grads, normeds, scales, gains, mask, total, extras):
    terms = []
    for grad, normed in zip(grads, normeds):
        terms.append(jnp.sum(grad * normed, axis=(0, 1, 2)))
        terms.append(jnp.sum(grad, axis=(0, 1, 2)))
    for extra in extras:
        terms.append(extra)
    packed = lax.psum(jnp.concatenate(terms), "dp")
    results = []
    pairs = []
    offset = 0
    for grad, normed, scale, gain in zip(grads, normeds, scales, gains):
        breadth = grad.shape[3]
        gain_grad = packed[offset : offset + breadth]
        shift_grad = packed[offset + breadth : offset + 2 * breadth]
        offset = offset + 2 * breadth
        results.append(
            scale * gain * (grad - mask[..., None] * (shift_grad + normed * gain_grad) / total)
        )
        pairs.append((gain_grad, shift_grad))
    rest = []
    for extra in extras:
        rest.append(packed[offset : offset + extra.shape[0]])
        offset = offset + extra.shape[0]
    return (results, pairs, rest)


def excite_forward(field, mask, pixels, squeeze_full, squeeze_bias, excite_full, excite_bias):
    pooled = jnp.sum(field * mask[..., None], axis=(1, 2)) / pixels[:, None]
    inner_pre = (
        jnp.dot(pooled, squeeze_full.astype(jnp.float32), precision=highest) + squeeze_bias
    )
    hidden = jax.nn.silu(inner_pre)
    scale = jax.nn.sigmoid(
        jnp.dot(hidden, excite_full.astype(jnp.float32), precision=highest) + excite_bias
    )
    return (pooled, inner_pre, hidden, scale)


def excite_backward(grad_branch, field, mask, pixels, saved, squeeze_full, excite_full):
    pooled, inner_pre, hidden, scale = saved
    grad_scale = jnp.sum(grad_branch * field, axis=(1, 2))
    grad_gate = grad_scale * scale * (1.0 - scale)
    excite_grad = jnp.dot(hidden.T, grad_gate, precision=highest)
    grad_hidden = jnp.dot(grad_gate, excite_full.astype(jnp.float32).T, precision=highest)
    grad_inner = grad_hidden * swish_slope(inner_pre)
    squeeze_grad = jnp.dot(pooled.T, grad_inner, precision=highest)
    grad_pooled = jnp.dot(grad_inner, squeeze_full.astype(jnp.float32).T, precision=highest)
    grad_field = (
        grad_branch * scale[:, None, None, :]
        + grad_pooled[:, None, None, :] * mask[..., None] / pixels[:, None, None, None]
    )
    return (
        grad_field,
        squeeze_grad,
        excite_grad,
        jnp.sum(grad_inner, axis=0),
        jnp.sum(grad_gate, axis=0),
    )


def whole_vector(value):
    return lax.all_gather(value, "mp", axis=0, tiled=True)


def whole_matrix(value, dp_axis, mp_axis):
    value = lax.all_gather(value, "dp", axis=dp_axis, tiled=True)
    return lax.all_gather(value, "mp", axis=mp_axis, tiled=True)


def own_part(value, dp_axis, mp_axis):
    value = lax.psum_scatter(
        value.astype(jnp.bfloat16), "mp", scatter_dimension=mp_axis, tiled=True
    )
    return lax.psum_scatter(value, "dp", scatter_dimension=dp_axis, tiled=True).astype(
        jnp.float32
    )


def plain_shards(
    images,
    image_size,
    entry_weight,
    entry_gain,
    entry_shift,
    stride_weight,
    stride_gain,
    stride_shift,
    expand_weight,
    expand_gain,
    expand_shift,
    project_weight,
    project_gain,
    project_shift,
    squeeze_weight,
    squeeze_bias,
    excite_weight,
    excite_bias,
    reduce_weight,
    reduce_gain,
    reduce_shift,
    spatial_weight,
    spatial_gain,
    spatial_shift,
    widen_weight,
    widen_gain,
    widen_shift,
    shrink_weight,
    shrink_bias,
    gating_weight,
    gating_bias,
    cotangent,
):
    place = lax.axis_index("mp")
    count, side = (images.shape[1], images.shape[2])
    half = side // 2
    channels_in = images.shape[4]
    entry_full = whole_matrix(entry_weight, 0, 1)
    stride_full = whole_matrix(stride_weight, 2, 3)
    expand_full = whole_matrix(expand_weight, 1, 0)
    project_full = whole_matrix(project_weight, 0, 1)
    squeeze_full = whole_matrix(squeeze_weight, 1, 0)
    excite_full = whole_matrix(excite_weight, 0, 1)
    reduce_full = whole_matrix(reduce_weight, 0, 1)
    spatial_full = whole_matrix(spatial_weight, 2, 3)
    widen_full = whole_matrix(widen_weight, 1, 0)
    shrink_full = whole_matrix(shrink_weight, 1, 0)
    gating_full = whole_matrix(gating_weight, 0, 1)
    entry_gain, entry_shift = whole_vector(entry_gain), whole_vector(entry_shift)
    stride_gain, stride_shift = whole_vector(stride_gain), whole_vector(stride_shift)
    expand_gain, expand_shift = whole_vector(expand_gain), whole_vector(expand_shift)
    project_gain, project_shift = whole_vector(project_gain), whole_vector(project_shift)
    reduce_gain, reduce_shift = whole_vector(reduce_gain), whole_vector(reduce_shift)
    spatial_gain, spatial_shift = whole_vector(spatial_gain), whole_vector(spatial_shift)
    widen_gain, widen_shift = whole_vector(widen_gain), whole_vector(widen_shift)
    excite_bias, gating_bias = whole_vector(excite_bias), whole_vector(gating_bias)
    seed_grad = lax.all_to_all(cotangent, "mp", split_axis=0, concat_axis=4, tiled=True)[0]
    picture = lax.dynamic_index_in_dim(images, place, 0, keepdims=False)
    sizes = lax.dynamic_index_in_dim(image_size, place, 0, keepdims=False)
    inside, reduced = pixel_masks(sizes, side)
    pixels = jnp.sum(reduced, axis=(1, 2))
    reduced_mask = reduced[..., None]
    entry_raw = matmul(picture.reshape(-1, channels_in), entry_full).reshape(
        count, side, side, -1
    )
    stats, inside_total = batch_statistics([entry_raw], inside)
    entry_stats = stats[0]
    entry_normed, entry_pre = standardize(entry_raw, entry_stats, entry_gain, entry_shift)
    entry_act = (jax.nn.silu(entry_pre) * inside[..., None]).astype(jnp.bfloat16)
    entry_wide = entry_act
    bottleneck = entry_wide.shape[3]
    stride_taps = spatial_taps(entry_wide, 2).reshape(-1, 9 * bottleneck)
    stride_raw = matmul(stride_taps, stride_full.reshape(9 * bottleneck, -1)).reshape(
        count, half, half, -1
    )
    stats, reduced_total = batch_statistics([stride_raw], reduced)
    stride_stats = stats[0]
    stride_normed, stride_pre = standardize(stride_raw, stride_stats, stride_gain, stride_shift)
    stride_act = (jax.nn.silu(stride_pre) * reduced_mask).astype(jnp.bfloat16)
    local_bottleneck = stride_act.shape[3]
    stride_flat = stride_act.reshape(-1, local_bottleneck)
    expand_raw = matmul(stride_flat, expand_full).reshape(count, half, half, -1)
    strided_flat = picture[:, ::2, ::2, :].reshape(-1, channels_in)
    project_raw = matmul(strided_flat, project_full).reshape(count, half, half, -1)
    stats, reduced_total = batch_statistics([expand_raw, project_raw], reduced)
    expand_stats, project_stats = (stats[0], stats[1])
    expand_normed, expand_pre = standardize(expand_raw, expand_stats, expand_gain, expand_shift)
    project_normed, project_pre = standardize(
        project_raw, project_stats, project_gain, project_shift
    )
    first_saved = excite_forward(
        expand_pre, reduced, pixels, squeeze_full, squeeze_bias, excite_full, excite_bias
    )
    first_sum = expand_pre * first_saved[3][:, None, None, :] + project_pre
    first_out = (jax.nn.silu(first_sum) * reduced_mask).astype(jnp.bfloat16)
    block_wide = first_out
    block_flat = block_wide.reshape(-1, block_wide.shape[3])
    reduce_raw = matmul(block_flat, reduce_full).reshape(count, half, half, -1)
    stats, reduced_total = batch_statistics([reduce_raw], reduced)
    reduce_stats = stats[0]
    reduce_normed, reduce_pre = standardize(reduce_raw, reduce_stats, reduce_gain, reduce_shift)
    reduce_act = (jax.nn.silu(reduce_pre) * reduced_mask).astype(jnp.bfloat16)
    reduce_wide = reduce_act
    second_taps = spatial_taps(reduce_wide, 1).reshape(-1, 9 * bottleneck)
    spatial_raw = matmul(second_taps, spatial_full.reshape(9 * bottleneck, -1)).reshape(
        count, half, half, -1
    )
    stats, reduced_total = batch_statistics([spatial_raw], reduced)
    spatial_stats = stats[0]
    spatial_normed, spatial_pre = standardize(
        spatial_raw, spatial_stats, spatial_gain, spatial_shift
    )
    spatial_act = (jax.nn.silu(spatial_pre) * reduced_mask).astype(jnp.bfloat16)
    spatial_flat = spatial_act.reshape(-1, local_bottleneck)
    widen_raw = matmul(spatial_flat, widen_full).reshape(count, half, half, -1)
    stats, reduced_total = batch_statistics([widen_raw], reduced)
    widen_stats = stats[0]
    widen_normed, widen_pre = standardize(widen_raw, widen_stats, widen_gain, widen_shift)
    second_saved = excite_forward(
        widen_pre, reduced, pixels, shrink_full, shrink_bias, gating_full, gating_bias
    )
    second_sum = widen_pre * second_saved[3][:, None, None, :] + first_out.astype(jnp.float32)
    output = (jax.nn.silu(second_sum) * reduced_mask).astype(jnp.bfloat16)
    second_grad = seed_grad.astype(jnp.float32) * reduced_mask * swish_slope(second_sum)
    widen_grad, shrink_grad, gating_grad, shrink_bias_grad, gating_bias_grad = excite_backward(
        second_grad, widen_pre, reduced, pixels, second_saved, shrink_full, gating_full
    )
    grads, widen_pair, extras = batch_backward(
        [widen_grad],
        [widen_normed],
        [widen_stats[1]],
        [widen_gain],
        reduced,
        reduced_total,
        (shrink_bias_grad, gating_bias_grad),
    )
    widen_pair = widen_pair[0]
    shrink_bias_total, gating_bias_total = (extras[0], extras[1])
    widen_local = grads[0].astype(jnp.bfloat16)
    widen_low = widen_local
    widen_flat = widen_low.reshape(-1, widen_low.shape[3])
    widen_weight_grad = contract_rows(spatial_flat, widen_flat)
    spatial_act_grad = contract_cols(widen_flat, widen_full).reshape(count, half, half, -1)
    spatial_grad = spatial_act_grad * reduced_mask * swish_slope(spatial_pre)
    grads, spatial_pair, extras = batch_backward(
        [spatial_grad],
        [spatial_normed],
        [spatial_stats[1]],
        [spatial_gain],
        reduced,
        reduced_total,
        (),
    )
    spatial_pair = spatial_pair[0]
    spatial_low = grads[0].astype(jnp.bfloat16).reshape(-1, local_bottleneck)
    spatial_weight_grad = contract_rows(second_taps, spatial_low).reshape(
        3, 3, bottleneck, local_bottleneck
    )
    second_tap_grad = contract_cols(spatial_low, spatial_full.reshape(9 * bottleneck, -1))
    reduce_act_grad = untap(second_tap_grad.reshape(count, half, half, -1), 1, half)
    reduce_grad = reduce_act_grad * reduced_mask * swish_slope(reduce_pre)
    grads, reduce_pair, extras = batch_backward(
        [reduce_grad],
        [reduce_normed],
        [reduce_stats[1]],
        [reduce_gain],
        reduced,
        reduced_total,
        (),
    )
    reduce_pair = reduce_pair[0]
    reduce_low = grads[0].astype(jnp.bfloat16).reshape(-1, local_bottleneck)
    reduce_weight_grad = contract_rows(block_flat, reduce_low)
    first_partial = contract_cols(reduce_low, reduce_full).reshape(count, half, half, -1)
    first_out_grad = first_partial + second_grad
    first_grad = first_out_grad * reduced_mask * swish_slope(first_sum)
    expand_grad, squeeze_grad, excite_grad, squeeze_bias_grad, excite_bias_grad = (
        excite_backward(
            first_grad, expand_pre, reduced, pixels, first_saved, squeeze_full, excite_full
        )
    )
    grads, pairs, extras = batch_backward(
        [expand_grad, first_grad],
        [expand_normed, project_normed],
        [expand_stats[1], project_stats[1]],
        [expand_gain, project_gain],
        reduced,
        reduced_total,
        (squeeze_bias_grad, excite_bias_grad),
    )
    expand_pair, project_pair = (pairs[0], pairs[1])
    squeeze_bias_total, excite_bias_total = (extras[0], extras[1])
    expand_local = grads[0].astype(jnp.bfloat16)
    expand_low = expand_local
    expand_flat = expand_low.reshape(-1, expand_low.shape[3])
    expand_weight_grad = contract_rows(stride_flat, expand_flat)
    stride_act_grad = contract_cols(expand_flat, expand_full).reshape(count, half, half, -1)
    project_low = grads[1].astype(jnp.bfloat16).reshape(-1, grads[1].shape[3])
    project_weight_grad = contract_rows(strided_flat, project_low)
    strided_grad = contract_cols(project_low, project_full).reshape(
        count, half, half, channels_in
    )
    stride_grad = stride_act_grad * reduced_mask * swish_slope(stride_pre)
    grads, stride_pair, extras = batch_backward(
        [stride_grad],
        [stride_normed],
        [stride_stats[1]],
        [stride_gain],
        reduced,
        reduced_total,
        (),
    )
    stride_pair = stride_pair[0]
    stride_low = grads[0].astype(jnp.bfloat16).reshape(-1, local_bottleneck)
    stride_weight_grad = contract_rows(stride_taps, stride_low).reshape(
        3, 3, bottleneck, local_bottleneck
    )
    first_tap_grad = contract_cols(stride_low, stride_full.reshape(9 * bottleneck, -1))
    entry_act_grad = untap(first_tap_grad.reshape(count, half, half, -1), 2, side)
    entry_grad = entry_act_grad * inside[..., None] * swish_slope(entry_pre)
    grads, entry_pair, extras = batch_backward(
        [entry_grad], [entry_normed], [entry_stats[1]], [entry_gain], inside, inside_total, ()
    )
    entry_pair = entry_pair[0]
    entry_low = grads[0].astype(jnp.bfloat16).reshape(-1, local_bottleneck)
    entry_weight_grad = contract_rows(picture.reshape(-1, channels_in), entry_low)
    picture_partial = contract_cols(entry_low, entry_full).reshape(
        count, side, side, channels_in
    )
    picture_partial = picture_partial + lax.pad(
        strided_grad, jnp.float32(0.0), ((0, 0, 0), (0, 1, 1), (0, 1, 1), (0, 0, 0))
    )

    def own_vector(value):
        return lax.psum_scatter(value, "mp", scatter_dimension=0, tiled=True)

    picture_grad = lax.all_to_all(
        picture_partial.astype(jnp.bfloat16)[None], "mp", split_axis=4, concat_axis=0, tiled=True
    ).astype(jnp.float32)
    result = lax.all_to_all(output[None], "mp", split_axis=4, concat_axis=0, tiled=True)
    return (
        result,
        picture_grad,
        own_part(entry_weight_grad, 0, 1),
        own_vector(entry_pair[0]),
        own_vector(entry_pair[1]),
        own_part(stride_weight_grad, 2, 3),
        own_vector(stride_pair[0]),
        own_vector(stride_pair[1]),
        own_part(expand_weight_grad, 1, 0),
        own_vector(expand_pair[0]),
        own_vector(expand_pair[1]),
        own_part(project_weight_grad, 0, 1),
        own_vector(project_pair[0]),
        own_vector(project_pair[1]),
        own_part(squeeze_grad, 1, 0),
        lax.psum(squeeze_bias_total, "mp"),
        own_part(excite_grad, 0, 1),
        own_vector(excite_bias_total),
        own_part(reduce_weight_grad, 0, 1),
        own_vector(reduce_pair[0]),
        own_vector(reduce_pair[1]),
        own_part(spatial_weight_grad, 2, 3),
        own_vector(spatial_pair[0]),
        own_vector(spatial_pair[1]),
        own_part(widen_weight_grad, 1, 0),
        own_vector(widen_pair[0]),
        own_vector(widen_pair[1]),
        own_part(shrink_grad, 1, 0),
        lax.psum(shrink_bias_total, "mp"),
        own_part(gating_grad, 0, 1),
        own_vector(gating_bias_total),
    )


def solution(mesh):
    in_specs = (
        P(None, "dp", None, None, None),
        P(None, "dp", None),
        P("dp", "mp"),
        P("mp"),
        P("mp"),
        P(None, None, "dp", "mp"),
        P("mp"),
        P("mp"),
        P("mp", "dp"),
        P("mp"),
        P("mp"),
        P("dp", "mp"),
        P("mp"),
        P("mp"),
        P("mp", "dp"),
        P(),
        P("dp", "mp"),
        P("mp"),
        P("dp", "mp"),
        P("mp"),
        P("mp"),
        P(None, None, "dp", "mp"),
        P("mp"),
        P("mp"),
        P("mp", "dp"),
        P("mp"),
        P("mp"),
        P("mp", "dp"),
        P(),
        P("dp", "mp"),
        P("mp"),
        P(None, "dp", None, None, "mp"),
    )
    out_specs = (
        P(None, "dp", None, None, "mp"),
        P(None, "dp", None, None, "mp"),
        P("dp", "mp"),
        P("mp"),
        P("mp"),
        P(None, None, "dp", "mp"),
        P("mp"),
        P("mp"),
        P("mp", "dp"),
        P("mp"),
        P("mp"),
        P("dp", "mp"),
        P("mp"),
        P("mp"),
        P("mp", "dp"),
        P(),
        P("dp", "mp"),
        P("mp"),
        P("dp", "mp"),
        P("mp"),
        P("mp"),
        P(None, None, "dp", "mp"),
        P("mp"),
        P("mp"),
        P("mp", "dp"),
        P("mp"),
        P("mp"),
        P("mp", "dp"),
        P(),
        P("dp", "mp"),
        P("mp"),
    )
    shards = fused_shards if dict(mesh.shape) == {"dp": 8, "mp": 4} else plain_shards
    return jax.shard_map(shards, mesh=mesh, in_specs=in_specs, out_specs=out_specs, check_vma=False)
```

```python
import functools

import jax
import jax.numpy as jnp
from jax import lax
from jax.experimental import pallas as pl
from jax.experimental.pallas import tpu as pltpu
from jax.sharding import PartitionSpec as P

eps_norm = 1e-05
highest = lax.Precision.HIGHEST
BF = jnp.bfloat16
F32 = jnp.float32
MESH = pl.DeviceIdType.MESH

TENSORS = {
    "E": (128, 512, 1, "E"),
    "P": (128, 2048, 1, "P"),
    "S": (576, 512, 1, "S"),
    "X": (512, 256, 0, "X"),
    "A": (32, 2048, 1, "A"),
    "R": (256, 512, 1, "R"),
    "T": (576, 512, 1, "S"),
    "V": (512, 256, 0, "X"),
    "B": (32, 2048, 1, "A"),
}
NAMES = list(TENSORS)
PIECES = {
    "E": [(0, 128)],
    "P": [(0, 32), (32, 32), (64, 32), (96, 32)],
    "S": [(0, 128), (128, 128), (256, 128), (384, 192)],
    "X": [(0, 128), (128, 128)],
    "A": [(0, 32)],
    "R": [(0, 128), (128, 128)],
    "T": [(0, 128), (128, 128), (256, 128), (384, 192)],
    "V": [(0, 128), (128, 128)],
    "B": [(0, 32)],
}
ORDER = [(n, i) for n in NAMES for i in range(len(PIECES[n]))]
INDEX = {piece: i for i, piece in enumerate(ORDER)}
AG_MORE = ()
RS_MORE = (0, 5, 6, 7, 8)
AG_ROWS, RS_ROWS = 8, 12
LAST = {n: INDEX[n, len(PIECES[n]) - 1] for n in NAMES}
COUNT = len(ORDER)
LEAD, LAG, RLAG = 3, 2, 3
OPT = ()
TICKS = "bch"
STARTS = 1
ENDLAG = 2
PUMPS = "ABCDEFGHIJKLMNOPQRSUVWXY"
CLASSES = {"E": (128, 128), "P": (128, 512), "S": (576, 128), "X": (128, 256), "A": (32, 512), "R": (256, 128)}
Q = 192
VMEM_LIMIT = 64 * 2**20
WIDE = 2048
EXCHANGES = {
    "entry": (4, 512), "stride": (2, 512), "xp": (4, 2048), "reduce": (2, 512), "spatial": (2, 512), "widen": (2, 2048),
    "widen_b": (4, 2048), "spatial_b": (2, 512), "reduce_b": (2, 512), "xp_b": (4, 2048), "bias_b": (2, 2048),
    "stride_b": (2, 512), "entry_b": (2, 512),
}
EX = {n: i % 2 for i, n in enumerate(n for n in EXCHANGES if n != "bias_b")}
EX["bias_b"] = 2
ROW = {"entry": 0, "stride": 2, "reduce": 4, "spatial": 6, "expand": 8, "project": 16, "widen": 24, "excite": 32, "gating": 36,
       "squeeze": 40, "shrink": 41}
SMALL = 48
NORM512 = {"entry": 0, "stride": 1, "reduce": 2, "spatial": 3}
NORM2048 = {"expand": 0, "project": 1, "widen": 2}


def sigmoid(v):
    return 0.5 + 0.5 * jnp.tanh(0.5 * v)


def dot(a, b):
    return jnp.dot(a, b, preferred_element_type=F32)


def dot_cols(a, b):
    return lax.dot_general(a, b, (((1,), (1,)), ((), ())), preferred_element_type=F32)


def dot_rows(a, b):
    return lax.dot_general(a, b, (((0,), (0,)), ((), ())), preferred_element_type=F32)


def halves(v):
    high = v.astype(BF)
    return high, (v - high.astype(F32)).astype(BF)


def exact(fn, v, w):
    high, low = halves(v)
    return fn(high, w) + fn(low, w)


def outer(a, b):
    ah, al = halves(a)
    bh, bl = halves(b)
    af, alf, bf, blf = ah.astype(F32), al.astype(F32), bh.astype(F32), bl.astype(F32)
    left = jnp.concatenate([af, af, alf, jnp.zeros_like(af)], axis=0).astype(BF)
    right = jnp.concatenate([bf, blf, bf, jnp.zeros_like(bf)], axis=0).astype(BF)
    return dot_rows(left, right)


def lanes(v, times):
    return jnp.concatenate([v] * times, axis=1) if times > 1 else v


def scratch_list():
    s = {}
    for n, (r, c, _, _) in TENSORS.items():
        s["W" + n] = pltpu.VMEM((4, 2, r, c), BF)
    for k, (r, c) in CLASSES.items():
        s["RC" + k] = pltpu.VMEM((2, 4, 2, r, c), BF)
        s["R1" + k] = pltpu.VMEM((4, r, c), BF)
        s["R2" + k] = pltpu.VMEM((2, 4, r, c), BF)
        s["RZ" + k] = pltpu.VMEM((3, r, c), BF)
    for n, (r, c) in EXCHANGES.items():
        s["X_" + n] = pltpu.VMEM((8, r, c), F32)
    s["picT"] = pltpu.VMEM((768, 1024), BF)
    s["stage"] = pltpu.VMEM((768, 1024), BF)
    s["taps1"] = pltpu.VMEM((Q, 4608), BF)
    s["taps2"] = pltpu.VMEM((Q, 4608), BF)
    s["act_e"] = pltpu.VMEM((Q, WIDE), BF)
    s["act_s"] = pltpu.VMEM((Q, 512), BF)
    s["act_p"] = pltpu.VMEM((Q, 512), BF)
    s["first"] = pltpu.VMEM((Q, WIDE), BF)
    s["cotb"] = pltpu.VMEM((Q, WIDE), BF)
    s["g1"] = pltpu.VMEM((Q, WIDE), BF)
    s["g2"] = pltpu.VMEM((Q, WIDE), BF)
    s["gs"] = pltpu.VMEM((Q, 512), BF)
    s["shift"] = pltpu.VMEM((9, Q, Q), BF)
    s["perm"] = pltpu.VMEM((256, 256), BF)
    for n in ("e_raw", "x_raw", "j_raw", "w_raw", "sg"):
        s[n] = pltpu.VMEM((Q, WIDE), F32)
    for n in ("s_raw", "r_raw", "p_raw", "gq", "acc"):
        s[n] = pltpu.VMEM((Q, 512), F32)
    s["sgrad"] = pltpu.VMEM((Q, 1024), F32)
    s["insm"] = pltpu.VMEM((768, 128), F32)
    s["redm"] = pltpu.VMEM((Q, 128), F32)
    s["pix"] = pltpu.VMEM((8, 128), F32)
    s["cnt"] = pltpu.VMEM((8, 512), F32)
    s["gv5"] = pltpu.VMEM((8, 512), F32)
    s["gv20"] = pltpu.VMEM((8, WIDE), F32)
    s["nv5"] = pltpu.VMEM((4, 8, 512), F32)
    s["nv20"] = pltpu.VMEM((3, 8, WIDE), F32)
    for n in ("isum1", "isum2", "pool1", "pool2", "scale1", "scale2", "pg", "G0", "G1", "gate"):
        s[n] = pltpu.VMEM((8, WIDE), F32)
    for n in ("inner1", "inner2", "ing"):
        s[n] = pltpu.VMEM((8, 128), F32)
    s["params"] = pltpu.VMEM((SMALL, 128), F32)
    for n, _, rows in VECTORS:
        s["v_" + n] = pltpu.VMEM((rows, 128), F32)
    for n in ("A", "B"):
        s["in" + n] = pltpu.VMEM((32, 512), BF)
    s["PR"] = pltpu.VMEM((4, SMALL, 128), F32)
    s["FS"] = pltpu.VMEM((4, SMALL, 128), F32)
    s["FR"] = pltpu.VMEM((4, SMALL, 128), F32)
    dma = pltpu.SemaphoreType.DMA
    s["ag_s"] = dma((AG_ROWS, 9))
    s["ag_r"] = dma((AG_ROWS, 7))
    s["ag_rc"] = dma((COUNT, 2))
    s["loc"] = dma((COUNT + 4,))
    s["vec"] = dma((len(VECTORS) + 4,))
    s["rs_s"] = dma((RS_ROWS, 9))
    s["rs_r"] = dma((RS_ROWS, 9))
    s["st_s"] = dma((3, 7))
    s["st_r"] = dma((3, 8))
    s["mp_s"] = dma((5, 4))
    s["mp_r"] = dma((5, 4))
    s["free"] = pltpu.SemaphoreType.REGULAR((3,))
    return s


VECTORS = []
for _n in ("entry", "stride", "reduce", "spatial"):
    VECTORS += [(_n + "_gain", ROW[_n], 1), (_n + "_shift", ROW[_n] + 1, 1)]
for _n in ("expand", "project", "widen"):
    VECTORS += [(_n + "_gain", ROW[_n], 4), (_n + "_shift", ROW[_n] + 4, 4)]
VECTORS += [("excite_bias", ROW["excite"], 4), ("gating_bias", ROW["gating"], 4)]
VECTORS += [("squeeze_bias", ROW["squeeze"], 1), ("shrink_bias", ROW["shrink"], 1)]
PLAIN = [n for n in NAMES if n not in ("A", "B")]
IN_NAMES = ["images", "sizes", "cot_in"] + ["in" + n for n in PLAIN] + ["sqA", "exA", "sqB", "exB"] + [v[0] for v in VECTORS]
OUT_NAMES = ["result", "igrad"] + ["out" + n for n in NAMES] + ["small"]
LAST_IN = ["result", "igrad"] + ["out" + n for n in NAMES] + ["small"]
LAST_OUT = ["f_result", "f_igrad"] + ["f_" + n for n in PLAIN] + ["f_sqA", "f_exA", "f_sqB", "f_exB"] + [v[0] for v in VECTORS]


def last_body(*refs):
    g = dict(zip(LAST_IN + LAST_OUT, refs))
    step = pl.program_id(0)

    @pl.when(step == 0)
    def _():
        for n in PLAIN:
            g["f_" + n][...] = g["out" + n][...]
        for n in "AB":
            g["f_sq" + n][...] = g["out" + n][0:16, :]
            g["f_ex" + n][...] = g["out" + n][16:32, :]
        for n, row, rows in VECTORS:
            g[n][...] = g["small"][row : row + rows, :]

    g["f_igrad"][...] = g["igrad"][...].astype(F32)
    g["f_result"][...] = g["result"][...]


class Copy:
    def __init__(self, *given):
        self.given = given

    def made(self):
        src, dst, ss, rs, dev = self.given
        return pltpu.make_async_remote_copy(
            src_ref=src, dst_ref=dst, send_sem=ss, recv_sem=rs, device_id=dev, device_id_type=MESH
        )

    def start(self, priority=0):
        self.made().start(priority=priority)

    def wait_recv(self):
        self.made().wait_recv()

    def wait_send(self):
        self.made().wait_send()


def body(*refs):
    names = IN_NAMES + OUT_NAMES + list(scratch_list())
    g = dict(zip(names, refs))

    class NS:
        def __getattr__(self, k):
            return g[k]

    s = NS()
    d = lax.axis_index("dp")
    m = lax.axis_index("mp")
    z, y = d // 2, lax.rem(d, 2)
    x, c = m // 2, lax.rem(m, 2)
    mx = (1 - x) * 2 + c
    mc = x * 2 + (1 - c)
    whole = slice(None)
    xdev, ydev, cdev = (d, mx), (z * 2 + (1 - y), m), (d, mc)

    def zdev(k):
        return (lax.rem(z + k, 4) * 2 + y, m)

    def mdev(k):
        return (d, lax.rem(m + k, 4))

    def col(j, w):
        return pl.ds(pl.multiple_of(j * w, w), w)

    def rcopy(src, dst, ss, rs, dev):
        return Copy(src, dst, ss, rs, dev)

    partners = [(lax.rem(z + k // 2, 4) * 2 + lax.rem(y + k % 2, 2), m) for k in range(1, 8)]
    partners += [mdev(k) for k in range(1, 4)]
    vec = [pltpu.make_async_copy(g[v[0]], g["v_" + v[0]], s.vec.at[i]) for i, v in enumerate(VECTORS)]
    for i, n in enumerate("AB"):
        vec += [
            pltpu.make_async_copy(g["sq" + n], g["in" + n].at[pl.ds(0, 16)], s.vec.at[len(VECTORS) + 2 * i]),
            pltpu.make_async_copy(g["ex" + n], g["in" + n].at[pl.ds(16, 16)], s.vec.at[len(VECTORS) + 2 * i + 1]),
        ]
    own_pic = pltpu.make_async_copy(s.images.at[m], s.stage, s.loc.at[COUNT])
    own_pic.start()
    for t in vec:
        t.start()
    barrier = pltpu.get_barrier_semaphore()
    for dev in partners:
        pl.semaphore_signal(barrier, inc=1, device_id=dev, device_id_type=MESH)
    pl.semaphore_wait(barrier, len(partners))

    def part(piece, zs, ys, mi):
        n, i = piece
        rows, columns, dim, _ = TENSORS[n]
        start, size = PIECES[n][i]
        if dim == 1:
            return g["W" + n].at[zs, ys, pl.ds(start, size), col(mi, columns // 4)]
        return g["W" + n].at[zs, ys, col(mi, rows // 4), pl.ds(start, size)]

    def cut(piece):
        n, i = piece
        start, size = PIECES[n][i]
        return (pl.ds(start, size), whole) if TENSORS[n][2] == 1 else (whole, pl.ds(start, size))

    def shard(piece):
        return g["in" + piece[0]].at[cut(piece)]

    def ag(p, slot, region, dev, src=None):
        i = INDEX[p]
        row = i % AG_ROWS
        arrival = s.ag_r.at[row, slot] if slot < 7 else s.ag_rc.at[i, slot - 7]
        return rcopy(region if src is None else src, region, s.ag_s.at[row, slot], arrival, dev)

    def place(p):
        return pltpu.make_async_copy(shard(p), part(p, z, y, m), s.loc.at[INDEX[p]])

    def ag_copies(p):
        own = part(p, z, y, m)
        out, here = {}, {}
        share = 3 if INDEX[p] in AG_MORE else 2
        low, high = pl.ds(0, share), pl.ds(share, 4 - share)
        out[0] = [ag(p, k - 1, own, zdev(k), shard(p)) for k in range(1, 4)]
        here[0] = [(k - 1, part(p, lax.rem(z + 4 - k, 4), y, m)) for k in range(1, 4)]
        out[1] = [ag(p, 3, part(p, whole, y, m), xdev), ag(p, 4, part(p, whole, y, m), ydev)]
        here[1] = [(3, part(p, whole, y, mx)), (4, part(p, whole, 1 - y, m))]
        out[2] = [ag(p, 5, part(p, low, y, mx), ydev)]
        here[2] = [(5, part(p, low, 1 - y, mx))]
        out[2] += [ag(p, 6, part(p, high, 1 - y, m), xdev)]
        here[2] += [(6, part(p, high, 1 - y, mx))]
        out[3] = [ag(p, 7 + xx, part(p, whole, whole, xx * 2 + c), cdev) for xx in range(2)]
        here[3] = [(7 + xx, part(p, whole, whole, xx * 2 + (1 - c))) for xx in range(2)]
        return out, here

    def landed(p, here):
        for slot, region in here:
            ag(p, slot, region, cdev).wait_recv()

    def ag_z(p):
        if INDEX[p] >= AG_ROWS:
            ag_sent(ORDER[INDEX[p] - AG_ROWS])
        place(p).start()
        for t in ag_copies(p)[0][0]:
            t.start()

    def ag_1(p):
        out, here = ag_copies(p)
        place(p).wait()
        landed(p, here[0])
        for t in out[1]:
            t.start()

    def ag_2(p):
        out, here = ag_copies(p)
        landed(p, here[1])
        for t in out[2]:
            t.start()

    def ag_c(p):
        out, here = ag_copies(p)
        landed(p, here[2])
        for t in out[3]:
            t.start()

    def ag_sent(p):
        for copies in ag_copies(p)[0].values():
            for t in copies:
                t.wait_send()

    def ag_drain(n):
        if "ag" in OPT:
            return
        for i in range(len(PIECES[n])):
            if INDEX[n, i] >= COUNT - AG_ROWS:
                ag_sent((n, i))

    ticks = {"k": 0}

    def tick():
        if "ag" in OPT:
            return
        k = ticks["k"]
        ticks["k"] = k + 1
        for stage, lag in ((ag_c, 2 * LAG), (ag_2, LAG), (ag_1, 0), (ag_z, -LEAD)):
            if 0 <= k - lag < COUNT:
                stage(ORDER[k - lag])

    def mark(tag):
        for t in TICKS:
            if t == tag:
                if ticks["k"] < COUNT + 2 * LAG:
                    tick()

    def need(n):
        if "ag" in OPT:
            return
        while ticks["k"] <= LAST[n] + 2 * LAG:
            tick()
        for i in range(len(PIECES[n])):
            landed((n, i), ag_copies((n, i))[1][3])

    def loop(count, fn, unroll=1):
        def step(j, carry):
            fn(j)
            return carry

        lax.fori_loop(0, count, step, 0, unroll=unroll)

    def rs(row, slot, region, landing, dev):
        return rcopy(region, landing, s.rs_s.at[row, slot], s.rs_r.at[row, slot], dev)

    credits = {"T": 0, "V": 1, "B": 2}
    takes = {"S": ("T", 0), "X": ("V", 1), "A": ("B", 2)}
    active = []

    def pause():
        steps = 0
        while steps < state["lag"]:
            steps += 1
            yield

    def bump(region, extra):
        region[...] = region[...] + extra

    def reduce_scatter(p, row):
        n, piece = p
        k = TENSORS[n][3]
        rc, r1, r2, rz = g["RC" + k], g["R1" + k], g["R2" + k], g["RZ" + k]
        c_ = cut(p)
        swap = [
            rs(row, xx, part(p, whole, whole, xx * 2 + (1 - c)), rc.at[(xx, pl.ds(0, 4), pl.ds(0, 2)) + c_], cdev) for xx in range(2)
        ]
        share = 3 if INDEX[p] in RS_MORE else 2
        low, high = pl.ds(0, 4 - share), pl.ds(4 - share, share)
        first = [
            rs(row, 2, part(p, low, 1 - y, mx), r1.at[(low,) + c_], xdev),
            rs(row, 3, part(p, high, 1 - y, mx), r1.at[(high,) + c_], ydev),
        ]
        second = [
            rs(row, 4, part(p, whole, y, mx), r2.at[(0, pl.ds(0, 4)) + c_], xdev),
            rs(row, 5, part(p, whole, 1 - y, m), r2.at[(1, pl.ds(0, 4)) + c_], ydev),
        ]
        third = [rs(row, 5 + k, part(p, lax.rem(z + k, 4), y, m), rz.at[(k - 1,) + c_], zdev(k)) for k in range(1, 4)]
        for t in swap:
            t.start()
        yield
        for t in swap:
            t.wait_recv()

        def add_c(j):
            zz, yy = j // 2, lax.rem(j, 2)
            for xx in range(2):
                bump(part(p, zz, yy, xx * 2 + c), rc[(xx, zz, yy) + c_])

        loop(8, add_c)
        for t in first:
            t.start()
        yield from pause()
        for t in first:
            t.wait_recv()
        for h in range(4 - share):
            bump(part(p, h, 1 - y, m), r1[(h,) + c_])
        for h in range(4 - share, 4):
            bump(part(p, h, y, mx), r1[(h,) + c_])
        for t in second:
            t.start()
        yield from pause()
        for t in second:
            t.wait_recv()

        def add_2(zz):
            bump(part(p, zz, y, m), (r2[(0, zz) + c_].astype(F32) + r2[(1, zz) + c_].astype(F32)).astype(BF))

        loop(4, add_2)
        for t in third:
            t.start()
        yield from pause()
        for t in third:
            t.wait_recv()
        total = part(p, z, y, m)[...].astype(F32)
        for k in range(3):
            total = total + rz[(k,) + c_].astype(F32)
        g["out" + n][c_] = total
        if n in credits and piece == len(PIECES[n]) - 1:
            for dev in [xdev, ydev, cdev] + [zdev(k) for k in range(1, 4)]:
                pl.semaphore_signal(s.free.at[credits[n]], inc=1, device_id=dev, device_id_type=MESH)
        for t in swap + first + second + third:
            t.wait_send()

    waiting = []
    state = {"lag": RLAG, "begun": 0}

    def pump():
        for item in list(active):
            try:
                next(item[1])
            except StopIteration:
                active.remove(item)
        for _ in range(STARTS):
            if not waiting:
                return
            n, i = waiting[0]
            if n in takes and i == 0:
                if any(item[0][0] == takes[n][0] for item in active):
                    return
                pl.semaphore_wait(s.free.at[takes[n][1]], 6)
            assert len(active) < RS_ROWS
            gen = reduce_scatter(waiting.pop(0), state["begun"] % RS_ROWS)
            state["begun"] += 1
            active.append(((n, i), gen))
            next(gen)

    def pumps(tag):
        state["lag"] = RLAG
        for t in PUMPS:
            if t in "123456":
                state["lag"] = int(t)
            if t == tag:
                pump()

    def begin(n, pieces=None):
        if "rs" in OPT or "no" + n in OPT:
            return
        for i in range(len(PIECES[n])) if pieces is None else pieces:
            waiting.append((n, i))

    def st_peers():
        return [lax.rem(z + k // 2, 4) * 2 + lax.rem(y + k % 2, 2) for k in range(1, 8)]

    def send_stats(e):
        buf, i = g["X_" + e], EX[e]
        if "stats" in OPT:
            return
        for k, dd in enumerate(st_peers()):
            rcopy(buf.at[d], buf.at[d], s.st_s.at[i, k], s.st_r.at[i, d], (dd, m)).start(priority=1 if 'prio' in OPT else 0)

    def get_stats(e):
        buf, i = g["X_" + e], EX[e]
        for k, dd in enumerate([] if "stats" in OPT else st_peers()):
            rcopy(buf.at[dd], buf.at[dd], s.st_s.at[i, k], s.st_r.at[i, dd], (dd, m)).wait_recv()
        for k, dd in enumerate([] if "stats" in OPT else st_peers()):
            rcopy(buf.at[d], buf.at[d], s.st_s.at[i, k], s.st_r.at[i, d], (dd, m)).wait_send()
        total = buf[0]
        for k in range(1, 8):
            total = total + buf[k]
        return total

    def mp_copies(i, src, dst):
        return [rcopy(src(lax.rem(m + k, 4)), dst(m), s.mp_s.at[i, k], s.mp_r.at[i, k], mdev(k)) for k in range(1, 4)]

    def mp_wait(i, src, dst, recv=True, send=True):
        for k in range(1, 4):
            if recv:
                rcopy(src(m), dst(lax.rem(m + 4 - k, 4)), s.mp_s.at[i, k], s.mp_r.at[i, k], mdev(k)).wait_recv()
            if send:
                rcopy(src(lax.rem(m + k, 4)), dst(m), s.mp_s.at[i, k], s.mp_r.at[i, k], mdev(k)).wait_send()

    cot_src, cot_dst = (lambda j: s.cot_in.at[j]), (lambda j: s.cotb.at[:, col(j, 512)])
    par_src, par_dst = (lambda j: s.params), (lambda j: s.PR.at[j])
    res_src, res_dst = (lambda j: s.g2.at[:, col(j, 512)]), (lambda j: s.result.at[j])
    img_src, img_dst = (lambda j: s.stage.at[:, col(j, 256)]), (lambda j: s.igrad.at[j])
    fin_src, fin_dst = (lambda j: s.FS.at[j]), (lambda j: s.FR.at[j])

    if "ag" not in OPT:
        for p in ORDER[:LEAD]:
            ag_z(p)
    for t in vec:
        t.wait()
    for n, row, rows in VECTORS:
        s.params[row : row + rows, :] = g["v_" + n][...]
    s.params[42:SMALL, :] = jnp.zeros((SMALL - 42, 128), F32)
    for t in mp_copies(1, par_src, par_dst):
        t.start()
    s.PR[m] = s.params[...]

    if "start0" in OPT:
        mp_wait(1, par_src, par_dst)
        own_pic.wait()
        return
    r64 = lax.broadcasted_iota(jnp.int32, (64, 128), 0)
    p64, q64 = r64 >> 3, r64 & 7
    s.pix[...] = jnp.ones((8, 128), F32)
    for i in range(3):
        high, wide = s.sizes[m, i, 0], s.sizes[m, i, 1]
        for pa in range(2):
            for pb in range(2):
                ok = (2 * p64 + pa < high) & (2 * q64 + pb < wide)
                s.insm[(pa * 2 + pb) * Q + i * 64 : (pa * 2 + pb) * Q + i * 64 + 64, :] = jnp.where(ok, 1.0, 0.0).astype(F32)
        ok = (2 * p64 < high) & (2 * q64 < wide)
        mask = jnp.where(ok, 1.0, 0.0).astype(F32)
        s.redm[i * 64 : i * 64 + 64, :] = mask
        s.pix[i : i + 1, :] = jnp.sum(mask, axis=0, keepdims=True)
    r8 = lax.broadcasted_iota(jnp.int32, (8, 128), 0)
    real = jnp.where(r8 < 3, 1.0, 0.0).astype(F32)

    rr = lax.broadcasted_iota(jnp.int32, (Q, Q), 0)
    cc = lax.broadcasted_iota(jnp.int32, (Q, Q), 1)
    pp, qq = (rr >> 3) & 7, rr & 7
    for t in range(9):
        da, db = t // 3 - 1, t % 3 - 1
        ok = (cc == rr + (da * 8 + db)) & (qq + db >= 0) & (qq + db < 8) & (pp + da >= 0) & (pp + da < 8)
        s.shift[t] = jnp.where(ok, 1.0, 0.0).astype(BF)
    rp = lax.broadcasted_iota(jnp.int32, (256, 256), 0)
    cp_ = lax.broadcasted_iota(jnp.int32, (256, 256), 1)
    source = ((rp >> 3) & 7) * 32 + (rp >> 7) * 16 + (rp & 7) * 2 + ((rp >> 6) & 1)
    s.perm[...] = jnp.where(cp_ == source, 1.0, 0.0).astype(BF)

    own_pic.wait()
    if "start1" in OPT:
        mp_wait(1, par_src, par_dst)
        return
    for i in range(3):
        def permute(j, i=i):
            v = dot(s.perm[...], s.stage[i * 256 : (i + 1) * 256, col(j, 256)]).astype(BF)
            for pl_ in range(4):
                s.picT[pl_ * Q + i * 64 : pl_ * Q + i * 64 + 64, col(j, 256)] = v[pl_ * 64 : pl_ * 64 + 64]

        loop(4, permute)

    tick()
    mp_wait(1, par_src, par_dst)
    for n, r in ROW.items():
        if n in NORM512:
            for k in range(2):
                row = NORM512[n] * 2 + k
                for j in range(4):
                    s.gv5[row : row + 1, j * 128 : j * 128 + 128] = s.PR[j, r + k : r + k + 1, :]
        elif n in NORM2048 or n in ("excite", "gating"):
            first_row = NORM2048[n] * 2 if n in NORM2048 else (6 if n == "excite" else 7)
            for k in range(2 if n in NORM2048 else 1):
                for j in range(4):
                    for h in range(4):
                        b = (j * 4 + h) * 128
                        s.gv20[first_row + k : first_row + k + 1, b : b + 128] = s.PR[j, r + k * 4 + h : r + k * 4 + h + 1, :]
    tick()

    def put(e, row, columns, value):
        g["X_" + e][d, row : row + 1, columns] = value

    def colsum(v):
        return jnp.sum(v, axis=0, keepdims=True)

    def norm_vectors(nv, index, total, square, count, gv, grow):
        mean = total / count
        rstd = lax.rsqrt(square / count - mean * mean + eps_norm)
        a = gv[grow : grow + 1, :] * rstd
        nv[index, 0:1, :] = a
        nv[index, 1:2, :] = gv[grow + 1 : grow + 2, :] - mean * a
        nv[index, 2:3, :] = mean
        nv[index, 3:4, :] = rstd

    def norm_back_vectors(nv, index, gain_grad, shift_grad, count):
        a, mean, rstd = nv[index, 0:1, :], nv[index, 2:3, :], nv[index, 3:4, :]
        w = a * rstd * gain_grad / count
        nv[index, 4:5, :] = a * shift_grad / count - mean * w
        nv[index, 5:6, :] = w

    def activate(raw, index, out):
        for j in range(4):
            b = slice(j * 128, j * 128 + 128)
            pre = raw[:, b] * s.nv5[index, 0:1, b] + s.nv5[index, 1:2, b]
            out[:, b] = (pre * sigmoid(pre) * s.redm[...]).astype(BF)

    def sums_512(e, columns, value, mask, row=0):
        vm = value * mask
        put(e, row, columns, colsum(vm))
        put(e, row + 1, columns, colsum(vm * value))

    def sums_wide(e, columns, value, isum, row):
        total = 0.0
        square = 0.0
        for i in range(3):
            v = value[i * 64 : i * 64 + 64]
            vm = v * lanes(s.redm[i * 64 : i * 64 + 64, :], v.shape[1] // 128)
            si = colsum(vm)
            if isum is not None:
                isum[i : i + 1, columns] = si
            total = total + si
            square = square + colsum(vm * v)
        put(e, row, columns, total)
        put(e, row + 1, columns, square)

    if "compute" in OPT:
        for n in NAMES:
            need(n)
        for n in NAMES:
            ag_drain(n)
        for n in ["B", "V", "T", "R", "A", "X", "P", "S", "E"]:
            for i in range(len(PIECES[n])):
                begin(n, [i])
                pump()
        while active or waiting:
            pump()
        return
    need("E")

    def entry_step(n):
        b = col(n, 256)
        v = dot(s.picT[...], s.WE[:, :, :, b].reshape(1024, 256))
        total = 0.0
        square = 0.0
        for k in range(4):
            vk = v[k * Q : k * Q + Q]
            s.e_raw[:, pl.ds(pl.multiple_of(k * 512 + n * 256, 256), 256)] = vk
            vm = vk * lanes(s.insm[k * Q : k * Q + Q, :], 2)
            total = total + colsum(vm)
            square = square + colsum(vm * vk)
        put("entry", 0, b, total)
        put("entry", 1, b, square)

    loop(2, entry_step)
    put("entry", 2, slice(0, 512), lanes(colsum(s.insm[...]), 4))
    put("entry", 3, slice(0, 512), lanes(colsum(s.redm[...]), 4))
    send_stats("entry")
    mark("a")

    need("P")

    def project_step(n):
        b = col(n, 256)
        v = dot(s.picT[0:Q, :], s.WP[:, :, :, b].reshape(1024, 256))
        s.j_raw[:, b] = v
        sums_wide("xp", b, v, None, 2)

    loop(8, project_step)
    mark("b")
    tot = get_stats("entry")
    s.cnt[0:2, :] = tot[2:4]
    norm_vectors(s.nv5, 0, tot[0:1], tot[1:2], tot[2:3], s.gv5, 0)

    def entry_act_step(j):
        pcol = col(lax.rem(j, 4), 128)
        mask = s.insm[pl.ds(pl.multiple_of((j // 4) * Q, Q), Q), :]
        pre = s.e_raw[:, col(j, 128)] * s.nv5[0, 0:1, pcol] + s.nv5[0, 1:2, pcol]
        s.act_e[:, col(j, 128)] = (pre * sigmoid(pre) * mask).astype(BF)

    loop(16, entry_act_step, 2)
    mark("c")
    for a in range(3):
        for b in range(3):
            t = a * 3 + b
            plane = (2 if a != 1 else 0) + (1 if b != 1 else 0)
            which = (0 if a == 0 else 1) * 3 + (0 if b == 0 else 1)
            v = s.act_e[:, plane * 512 : plane * 512 + 512]
            if which != 4:
                v = dot(s.shift[which], v).astype(BF)
            s.taps1[:, t * 512 : t * 512 + 512] = v

    mark("d")

    def conv3(taps, w, raw, e):
        def step(n):
            b = col(n, 256)
            v = dot(taps[:, 0:512], w[:, :, 0:64, b].reshape(512, 256))
            for t in range(1, 9):
                v = v + dot(taps[:, t * 512 : t * 512 + 512], w[:, :, t * 64 : t * 64 + 64, b].reshape(512, 256))
            raw[:, b] = v
            sums_512(e, b, v, lanes(s.redm[...], 2))

        loop(2, step)

    need("S")
    conv3(s.taps1, s.WS, s.s_raw, "stride")
    send_stats("stride")
    for t in mp_copies(0, cot_src, cot_dst):
        t.start()
    own_cot = pltpu.make_async_copy(cot_src(m), cot_dst(m), s.loc.at[COUNT + 1])
    own_cot.start()
    mark("e")
    need("X")
    tot = get_stats("stride")
    count5 = s.cnt[1:2, :]
    norm_vectors(s.nv5, 1, tot[0:1], tot[1:2], count5, s.gv5, 2)
    activate(s.s_raw, 1, s.act_s)
    mark("f")

    for n in ("isum1", "isum2", "G0", "G1"):
        g[n][...] = jnp.zeros((8, WIDE), F32)

    def widening(act, w, raw, e, isum):
        def step(k):
            b = col(k, 256)
            v = dot(act[...], w[k // 2, lax.rem(k, 2)])
            raw[:, b] = v
            sums_wide(e, b, v, isum, 0)

        loop(8, step)

    widening(s.act_s, s.WX, s.x_raw, "xp", s.isum1)
    send_stats("xp")
    mark("g")
    need("A")
    count20 = lanes(s.cnt[1:2, :], 4)
    tot = get_stats("xp")
    norm_vectors(s.nv20, 0, tot[0:1], tot[1:2], count20, s.gv20, 0)
    norm_vectors(s.nv20, 1, tot[2:3], tot[3:4], count20, s.gv20, 2)

    def squeeze_excite(index, isum, w, bias, gate_row, pool, inner, scale):
        pooled = (s.nv20[index, 0:1, :] * isum[...] / lanes(s.pix[...], 16) + s.nv20[index, 1:2, :]) * lanes(real, 16)
        pool[...] = pooled
        pre = exact(dot_cols, pooled, w[:, :, 0:16, :].reshape(128, WIDE)) + bias
        inner[...] = pre
        gate = exact(dot, pre * sigmoid(pre), w[:, :, 16:32, :].reshape(128, WIDE)) + s.gv20[gate_row : gate_row + 1, :]
        scale[...] = sigmoid(gate)

    squeeze_excite(0, s.isum1, s.WA, s.PR[0, 40:41, :], 6, s.pool1, s.inner1, s.scale1)
    mark("h")

    def first_sum(j, i):
        b, rows = col(j, 128), slice(i * 64, i * 64 + 64)
        pre = s.x_raw[rows, b] * s.nv20[0, 0:1, b] + s.nv20[0, 1:2, b]
        return pre * s.scale1[i : i + 1, b] + (s.j_raw[rows, b] * s.nv20[1, 0:1, b] + s.nv20[1, 1:2, b])

    def first_step(j):
        for i in range(3):
            rows = slice(i * 64, i * 64 + 64)
            v = first_sum(j, i)
            s.first[rows, col(j, 128)] = (v * sigmoid(v) * s.redm[rows, :]).astype(BF)

    loop(16, first_step, 2)
    mark("i")

    need("R")

    def reduce_step(n):
        b = col(n, 256)
        v = dot(s.first[...], s.WR[:, :, :, b].reshape(WIDE, 256))
        s.r_raw[:, b] = v
        sums_512("reduce", b, v, lanes(s.redm[...], 2))

    loop(2, reduce_step)
    send_stats("reduce")
    mark("j")
    tot = get_stats("reduce")
    norm_vectors(s.nv5, 2, tot[0:1], tot[1:2], count5, s.gv5, 4)
    activate(s.r_raw, 2, s.act_p)
    for t in range(9):
        v = s.act_p[...]
        if t != 4:
            v = dot(s.shift[t], v).astype(BF)
        s.taps2[:, t * 512 : t * 512 + 512] = v
    mark("k")
    need("T")
    conv3(s.taps2, s.WT, s.p_raw, "spatial")
    send_stats("spatial")
    mark("l")
    need("V")
    tot = get_stats("spatial")
    norm_vectors(s.nv5, 3, tot[0:1], tot[1:2], count5, s.gv5, 6)
    activate(s.p_raw, 3, s.act_p)
    mark("m")
    widening(s.act_p, s.WV, s.w_raw, "widen", s.isum2)
    send_stats("widen")
    need("B")
    own_cot.wait()
    mp_wait(0, cot_src, cot_dst)
    tot = get_stats("widen")
    norm_vectors(s.nv20, 2, tot[0:1], tot[1:2], count20, s.gv20, 4)
    squeeze_excite(2, s.isum2, s.WB, s.PR[0, 41:42, :], 7, s.pool2, s.inner2, s.scale2)

    def result_step(j):
        b = col(j, 128)
        for i in range(3):
            rows = slice(i * 64, i * 64 + 64)
            raw = s.w_raw[rows, b]
            pre = raw * s.nv20[2, 0:1, b] + s.nv20[2, 1:2, b]
            v = pre * s.scale2[i : i + 1, b] + s.first[rows, b].astype(F32)
            sg = sigmoid(v)
            mask = s.redm[rows, :]
            s.g2[rows, b] = (v * sg * mask).astype(BF)
            grad = s.cotb[rows, b].astype(F32) * mask * (sg * (1.0 + v * (1.0 - sg)))
            s.sg[rows, b] = grad
            s.G0[i : i + 1, b] = colsum(grad)
            s.G1[i : i + 1, b] = colsum(grad * ((raw - s.nv20[2, 2:3, b]) * s.nv20[2, 3:4, b]))

    loop(16, result_step, 2)
    for t in mp_copies(2, res_src, res_dst):
        t.start()
    own_res = pltpu.make_async_copy(res_src(m), res_dst(m), s.loc.at[COUNT + 2])
    own_res.start()

    if "fwd" in OPT:
        for n in NAMES:
            ag_drain(n)
        own_res.wait()
        mp_wait(2, res_src, res_dst)
        return
    def keep512(n, k, v):
        for j in range(4):
            s.FS[j, ROW[n] + k : ROW[n] + k + 1, :] = v[:, j * 128 : j * 128 + 128]

    def keep2048(row, v):
        for j in range(4):
            for h in range(4):
                b = (j * 4 + h) * 128
                s.FS[j, row + h : row + h + 1, :] = v[:, b : b + 128]

    def excite_back(index, isum, w, inner, scale):
        scl = scale[...]
        gate_grad = (s.gv20[index * 2 : index * 2 + 1, :] * s.G1[...] + s.gv20[index * 2 + 1 : index * 2 + 2, :] * s.G0[...]) * (
            scl * (1.0 - scl)
        )
        s.gate[...] = gate_grad
        pre = inner[...]
        sg = sigmoid(pre)
        ing = exact(dot_cols, gate_grad, w[:, :, 16:32, :].reshape(128, WIDE)) * (sg * (1.0 + pre * (1.0 - sg)))
        s.ing[...] = ing
        pix = lanes(s.pix[...], 16)
        pg = exact(dot, ing, w[:, :, 0:16, :].reshape(128, WIDE)) / pix
        s.pg[...] = pg
        spread = (isum[...] - s.nv20[index, 2:3, :] * pix) * s.nv20[index, 3:4, :]
        return (colsum(scl * s.G1[...] + pg * spread), colsum(scl * s.G0[...] + pg * pix), colsum(gate_grad), colsum(ing))

    def excite_weights(n, pool, inner):
        pre = inner[...]
        hidden = pre * sigmoid(pre)
        w = g["W" + n]

        def step(j):
            b = col(j, 512)
            w[:, :, 0:16, b] = outer(s.ing[...], pool[:, b]).astype(BF).reshape(4, 2, 16, 512)
            w[:, :, 16:32, b] = outer(hidden, s.gate[:, b]).astype(BF).reshape(4, 2, 16, 512)

        loop(4, step)

    def wide_grad(index, raw, out, scale):
        def step(j):
            b = col(j, 128)
            for i in range(3):
                rows = slice(i * 64, i * 64 + 64)
                grad, mask = s.sg[rows, b], s.redm[rows, :]
                if scale is not None:
                    grad = grad * scale[i : i + 1, b] + mask * s.pg[i : i + 1, b]
                v = s.nv20[index, 0:1, b] * grad - mask * (s.nv20[index, 4:5, b] + s.nv20[index, 5:6, b] * raw[rows, b])
                out[rows, b] = v.astype(BF)

        loop(16, step, 2)

    def back_sums(e, index, b, grad, raw, mask):
        out = []
        pre = raw * s.nv5[index, 0:1, b] + s.nv5[index, 1:2, b]
        sg = sigmoid(pre)
        grad = grad * mask * (sg * (1.0 + pre * (1.0 - sg)))
        put(e, 0, b, colsum(grad * ((raw - s.nv5[index, 2:3, b]) * s.nv5[index, 3:4, b])))
        put(e, 1, b, colsum(grad))
        return grad

    def narrow_back(e, index, acc, raw):
        for j in range(4):
            b = slice(j * 128, j * 128 + 128)
            s.gq[:, b] = back_sums(e, index, b, acc[:, b], raw[:, b], s.redm[...])

    def narrow_grad(index, raw):
        for j in range(4):
            b = slice(j * 128, j * 128 + 128)
            v = s.nv5[index, 0:1, b] * s.gq[:, b] - s.redm[...] * (s.nv5[index, 4:5, b] + s.nv5[index, 5:6, b] * raw[:, b])
            s.gs[:, b] = v.astype(BF)

    def narrow_stats(e, n):
        tot = get_stats(e)
        keep512(n, 0, tot[0:1])
        keep512(n, 1, tot[1:2])
        norm_back_vectors(s.nv5, NORM512[n], tot[0:1], tot[1:2], s.cnt[0:1, :] if n == "entry" else count5)

    def widening_back(grads, w):
        def step(n):
            rows = col(n, 256)
            v = dot_cols(grads[:, 0:256], w[0, 0, rows, :])
            for k in range(1, 8):
                v = v + dot_cols(grads[:, k * 256 : k * 256 + 256], w[k // 2, k % 2, rows, :])
            s.acc[:, rows] = v

        loop(2, step)

    def widening_weights(n, act, grads):
        ag_drain(n)
        w = g["W" + n]

        def step(k):
            w[k // 2, lax.rem(k, 2)] = dot_rows(act[...], grads[:, col(k, 256)]).astype(BF)

        loop(8, step)
        begin(n)

    def conv3_weights(n, taps):
        ag_drain(n)
        w = g["W" + n]

        def step(t):
            for h in range(2):
                b = slice(h * 256, h * 256 + 256)
                v = dot_rows(taps[:, col(t, 512)], s.gs[:, b]).astype(BF)
                w[:, :, col(t, 64), b] = v.reshape(4, 2, 64, 256)

        loop(9, step)
        begin(n)

    sums = excite_back(2, s.isum2, s.WB, s.inner2, s.scale2)
    for k in range(3):
        put("widen_b", k, slice(0, WIDE), sums[k])
    put("widen_b", 3, slice(0, WIDE), lanes(sums[3], 16))
    send_stats("widen_b")
    ag_drain("B")
    excite_weights("B", s.pool2, s.inner2)
    begin("B")
    tot = get_stats("widen_b")
    pumps("A")
    keep2048(ROW["widen"], tot[0:1])
    keep2048(ROW["widen"] + 4, tot[1:2])
    keep2048(ROW["gating"], tot[2:3])
    for j in range(4):
        s.FS[j, ROW["shrink"] : ROW["shrink"] + 1, :] = tot[3:4, 0:128]
    norm_back_vectors(s.nv20, 2, tot[0:1], tot[1:2], count20)
    wide_grad(2, s.w_raw, s.g1, s.scale2)
    pumps("B")
    widening_back(s.g1, s.WV)
    narrow_back("spatial_b", 3, s.acc, s.p_raw)
    send_stats("spatial_b")
    pumps("C")
    widening_weights("V", s.act_p, s.g1)
    pumps("D")
    narrow_stats("spatial_b", "spatial")
    narrow_grad(3, s.p_raw)
    pumps("E")
    s.acc[...] = jnp.zeros((Q, 512), F32)

    def spatial_back(t):
        v = dot(s.shift[8 - t], s.gs[...]).astype(BF)
        s.acc[...] += dot_cols(v, s.WT[:, :, col(t, 64), :].reshape(512, 512))

    loop(9, spatial_back)
    pumps("F")
    narrow_back("reduce_b", 2, s.acc, s.r_raw)
    send_stats("reduce_b")
    pumps("G")
    conv3_weights("T", s.taps2)
    pumps("H")
    narrow_stats("reduce_b", "reduce")
    narrow_grad(2, s.r_raw)
    pumps("I")

    def reduce_back(k):
        v = dot_cols(s.gs[...], s.WR[k // 2, lax.rem(k, 2)])
        for h in range(2):
            j = k * 2 + h
            b = col(j, 128)
            project_sum = 0.0
            shift_sum = 0.0
            for i in range(3):
                rows = slice(i * 64, i * 64 + 64)
                fs = first_sum(j, i)
                sg = sigmoid(fs)
                grad = (v[rows, h * 128 : h * 128 + 128] + s.sg[rows, b]) * s.redm[rows, :] * (sg * (1.0 + fs * (1.0 - sg)))
                s.sg[rows, b] = grad
                total = colsum(grad)
                s.G0[i : i + 1, b] = total
                s.G1[i : i + 1, b] = colsum(grad * ((s.x_raw[rows, b] - s.nv20[0, 2:3, b]) * s.nv20[0, 3:4, b]))
                shift_sum = shift_sum + total
                project_sum = project_sum + colsum(grad * ((s.j_raw[rows, b] - s.nv20[1, 2:3, b]) * s.nv20[1, 3:4, b]))
            put("xp_b", 2, b, project_sum)
            put("xp_b", 3, b, shift_sum)

    loop(8, reduce_back)
    pumps("J")
    sums = excite_back(0, s.isum1, s.WA, s.inner1, s.scale1)
    put("xp_b", 0, slice(0, WIDE), sums[0])
    put("xp_b", 1, slice(0, WIDE), sums[1])
    send_stats("xp_b")
    put("bias_b", 0, slice(0, WIDE), sums[2])
    put("bias_b", 1, slice(0, WIDE), lanes(sums[3], 16))
    send_stats("bias_b")
    pumps("K")
    ag_drain("R")

    def reduce_weights(k):
        s.WR[k // 2, lax.rem(k, 2)] = dot_rows(s.first[:, col(k, 256)], s.gs[...]).astype(BF)

    loop(8, reduce_weights)
    begin("R")
    pumps("L")
    ag_drain("A")
    excite_weights("A", s.pool1, s.inner1)
    begin("A")
    pumps("M")
    tot = get_stats("xp_b")
    for k, n in enumerate(("expand", "project")):
        keep2048(ROW[n], tot[2 * k : 2 * k + 1])
        keep2048(ROW[n] + 4, tot[2 * k + 1 : 2 * k + 2])
        norm_back_vectors(s.nv20, k, tot[2 * k : 2 * k + 1], tot[2 * k + 1 : 2 * k + 2], count20)
    wide_grad(0, s.x_raw, s.g1, s.scale1)
    pumps("N")
    widening_back(s.g1, s.WX)
    narrow_back("stride_b", 1, s.acc, s.s_raw)
    send_stats("stride_b")
    pumps("O")
    own_res.wait()
    mp_wait(2, res_src, res_dst)
    wide_grad(1, s.j_raw, s.g2, None)

    def project_back(zz):
        w = s.WP[zz].reshape(256, WIDE)
        s.sgrad[:, col(zz, 256)] = dot_cols(s.g2[...], w)

    loop(4, project_back)
    pumps("P")
    widening_weights("X", s.act_s, s.g1)
    pumps("Q")
    ag_drain("P")

    def project_weights(n):
        b = col(n, 256)
        for h in range(2):
            v = dot_rows(s.picT[0:Q, h * 512 : h * 512 + 512], s.g2[:, b]).astype(BF)
            s.WP[2 * h : 2 * h + 2, :, :, b] = v.reshape(2, 2, 128, 256)

    loop(8, project_weights)
    begin("P")
    pumps("R")
    narrow_stats("stride_b", "stride")
    narrow_grad(1, s.s_raw)
    pumps("S")

    for k in range(4):
        pa, pb = k // 2, k % 2
        columns = slice(k * 512, k * 512 + 512)
        first_tap = True
        for a in (0, 2) if pa else (1,):
            for b in (0, 2) if pb else (1,):
                t = a * 3 + b
                which = (0 if a == 0 else 1) * 3 + (0 if b == 0 else 1)
                v = s.gs[...]
                if which != 4:
                    v = dot(s.shift[8 - which], v).astype(BF)
                v = dot_cols(v, s.WS[:, :, t * 64 : t * 64 + 64, :].reshape(512, 512))
                if first_tap:
                    s.w_raw[:, columns] = v
                else:
                    s.w_raw[:, columns] += v
                first_tap = False

    def entry_back(n):
        b = col(n, 128)
        gain_sum = 0.0
        shift_sum = 0.0
        for k in range(4):
            kb = pl.ds(pl.multiple_of(k * 512 + n * 128, 128), 128)
            raw = s.e_raw[:, kb]
            pre = raw * s.nv5[0, 0:1, b] + s.nv5[0, 1:2, b]
            sg = sigmoid(pre)
            grad = s.w_raw[:, kb] * s.insm[k * Q : k * Q + Q, :] * (sg * (1.0 + pre * (1.0 - sg)))
            s.w_raw[:, kb] = grad
            gain_sum = gain_sum + colsum(grad * ((raw - s.nv5[0, 2:3, b]) * s.nv5[0, 3:4, b]))
            shift_sum = shift_sum + colsum(grad)
        put("entry_b", 0, b, gain_sum)
        put("entry_b", 1, b, shift_sum)

    loop(4, entry_back)
    send_stats("entry_b")
    pumps("U")
    conv3_weights("S", s.taps1)
    pumps("V")
    narrow_stats("entry_b", "entry")

    def entry_grad(j):
        pcol = col(lax.rem(j, 4), 128)
        mask = s.insm[pl.ds(pl.multiple_of((j // 4) * Q, Q), Q), :]
        b = col(j, 128)
        v = s.nv5[0, 0:1, pcol] * s.w_raw[:, b] - mask * (s.nv5[0, 4:5, pcol] + s.nv5[0, 5:6, pcol] * s.e_raw[:, b])
        s.act_e[:, b] = v.astype(BF)

    loop(16, entry_grad, 2)
    pumps("W")
    tot = get_stats("bias_b")
    keep2048(ROW["excite"], tot[0:1])
    for j in range(4):
        s.FS[j, ROW["squeeze"] : ROW["squeeze"] + 1, :] = tot[1:2, 0:128]
        for r in range(42, SMALL, 2):
            s.FS[j, r : r + 2, :] = jnp.zeros((2, 128), F32)
    s.FR[m] = s.FS[m]
    for t in mp_copies(4, fin_src, fin_dst):
        t.start()

    def image_grad(zz):
        w = s.WE[zz].reshape(256, 512)
        for k in range(4):
            v = dot_cols(s.act_e[:, k * 512 : k * 512 + 512], w)
            if k == 0:
                v = v + s.sgrad[:, col(zz, 256)]
            s.taps1[:, pl.ds(pl.multiple_of(k * 1024 + zz * 256, 256), 256)] = v.astype(BF)

    loop(4, image_grad)
    for i in range(3):
        def unpermute(j, i=i):
            v = jnp.concatenate(
                [s.taps1[i * 64 : i * 64 + 64, pl.ds(pl.multiple_of(k * 1024 + j * 256, 256), 256)] for k in range(4)], axis=0
            )
            s.stage[i * 256 : i * 256 + 256, col(j, 256)] = dot_rows(s.perm[...], v).astype(BF)

        loop(4, unpermute)
    for t in mp_copies(3, img_src, img_dst):
        t.start()
    own_img = pltpu.make_async_copy(img_src(m), img_dst(m), s.loc.at[COUNT + 3])
    own_img.start()
    pumps("X")
    ag_drain("E")

    def entry_weights(zz):
        v = dot_rows(s.picT[0:Q, col(zz, 256)], s.act_e[:, 0:512])
        for k in range(1, 4):
            v = v + dot_rows(s.picT[k * Q : k * Q + Q, col(zz, 256)], s.act_e[:, k * 512 : k * 512 + 512])
        s.WE[zz] = v.astype(BF).reshape(2, 128, 512)

    loop(4, entry_weights)
    begin("E")
    pumps("Y")
    state["lag"] = ENDLAG
    while active or waiting:
        pump()
    mp_wait(4, fin_src, fin_dst)
    s.small[...] = ((s.FR[0] + s.FR[1]) + s.FR[2]) + s.FR[3]
    own_img.wait()
    mp_wait(3, img_src, img_dst)

def fused_shards(*arrays):
    (images, image_size, entry_weight, entry_gain, entry_shift, stride_weight, stride_gain, stride_shift, expand_weight,
     expand_gain, expand_shift, project_weight, project_gain, project_shift, squeeze_weight, squeeze_bias, excite_weight,
     excite_bias, reduce_weight, reduce_gain, reduce_shift, spatial_weight, spatial_gain, spatial_shift, widen_weight,
     widen_gain, widen_shift, shrink_weight, shrink_bias, gating_weight, gating_bias, cotangent) = arrays
    weights = {
        "E": entry_weight,
        "P": project_weight,
        "S": stride_weight.reshape(576, 128),
        "X": expand_weight,
        "R": reduce_weight,
        "T": spatial_weight.reshape(576, 128),
        "V": widen_weight,
    }
    given = dict(
        entry_gain=entry_gain, entry_shift=entry_shift, stride_gain=stride_gain, stride_shift=stride_shift,
        reduce_gain=reduce_gain, reduce_shift=reduce_shift, spatial_gain=spatial_gain, spatial_shift=spatial_shift,
        expand_gain=expand_gain, expand_shift=expand_shift, project_gain=project_gain, project_shift=project_shift,
        widen_gain=widen_gain, widen_shift=widen_shift, excite_bias=excite_bias, gating_bias=gating_bias,
        squeeze_bias=squeeze_bias, shrink_bias=shrink_bias,
    )
    small = [given[n].reshape(rows, 128) for n, _, rows in VECTORS]
    hbm, vmem = pl.BlockSpec(memory_space=pl.ANY), pl.BlockSpec(memory_space=pltpu.VMEM)
    outs = [jax.ShapeDtypeStruct((4, Q, 512), BF), jax.ShapeDtypeStruct((4, 768, 256), BF)]
    outs += [jax.ShapeDtypeStruct(CLASSES[TENSORS[n][3]], F32) for n in NAMES]
    outs += [jax.ShapeDtypeStruct((SMALL, 128), F32)]
    got = pl.pallas_call(
        body,
        out_shape=outs,
        in_specs=[hbm, pl.BlockSpec(memory_space=pltpu.SMEM), hbm] + [hbm] * (len(PLAIN) + 4 + len(VECTORS)),
        out_specs=[hbm, hbm] + [vmem] * (len(NAMES) + 1),
        scratch_shapes=list(scratch_list().values()),
        compiler_params=pltpu.CompilerParams(collective_id=0, has_side_effects=True, vmem_limit_bytes=VMEM_LIMIT),
        cost_estimate=pl.CostEstimate(flops=14_000_000_000, bytes_accessed=30_000_000, transcendentals=10_000_000),
    )(
        images.reshape(4, 768, 1024), image_size, cotangent.reshape(4, Q, 512), *[weights[n] for n in PLAIN],
        squeeze_weight.T, excite_weight, shrink_weight.T, gating_weight, *small,
    )

    def held(shape):
        return pl.BlockSpec(shape, lambda i: (0, 0))

    kinds = [held(CLASSES[TENSORS[n][3]]) for n in NAMES]
    last = [jax.ShapeDtypeStruct((4, Q, 512), BF), jax.ShapeDtypeStruct((4, 768, 256), F32)]
    last += [jax.ShapeDtypeStruct(CLASSES[TENSORS[n][3]], F32) for n in PLAIN]
    last += [jax.ShapeDtypeStruct(v, F32) for v in ((16, 512),) * 4]
    last += [jax.ShapeDtypeStruct((rows, 128), F32) for _, _, rows in VECTORS]
    blocks = [pl.BlockSpec((1, Q, 512), lambda i: (i, 0, 0)), pl.BlockSpec((1, 768, 256), lambda i: (i, 0, 0))]
    final = pl.pallas_call(
        last_body,
        grid=(4,),
        out_shape=last,
        in_specs=blocks + kinds + [held((SMALL, 128))],
        out_specs=blocks + [held(CLASSES[TENSORS[n][3]]) for n in PLAIN] + [held(v) for v in ((16, 512),) * 4]
        + [held((rows, 128)) for _, _, rows in VECTORS],
        compiler_params=pltpu.CompilerParams(vmem_limit_bytes=VMEM_LIMIT),
        cost_estimate=pl.CostEstimate(flops=1_000_000, bytes_accessed=10_000_000, transcendentals=0),
    )(*got)
    f = dict(zip(LAST_OUT, final))

    def pair(n):
        return f[n + "_gain"].reshape(-1), f[n + "_shift"].reshape(-1)

    return (
        f["f_result"].reshape(cotangent.shape),
        f["f_igrad"].reshape(4, 3, 16, 16, 256),
        f["f_E"], *pair("entry"),
        f["f_S"].reshape(stride_weight.shape), *pair("stride"),
        f["f_X"], *pair("expand"),
        f["f_P"], *pair("project"),
        f["f_sqA"].T, f["squeeze_bias"].reshape(-1), f["f_exA"], f["excite_bias"].reshape(-1),
        f["f_R"], *pair("reduce"),
        f["f_T"].reshape(spatial_weight.shape), *pair("spatial"),
        f["f_V"], *pair("widen"),
        f["f_sqB"].T, f["shrink_bias"].reshape(-1), f["f_exB"], f["gating_bias"].reshape(-1),
    )


def matmul(left, right):
    return jnp.dot(left, right, preferred_element_type=jnp.float32)


def contract_rows(left, right):
    return lax.dot_general(
        left, right, (((0,), (0,)), ((), ())), preferred_element_type=jnp.float32
    )


def contract_cols(left, right):
    return lax.dot_general(
        left, right, (((1,), (1,)), ((), ())), preferred_element_type=jnp.float32
    )


def swish_slope(value):
    sigma = jax.nn.sigmoid(value)
    return sigma * (1.0 + value * (1.0 - sigma))


def pixel_masks(sizes, side):
    half = side // 2
    height = sizes[:, 0]
    breadth = sizes[:, 1]
    places = jnp.arange(side, dtype=jnp.int32)
    inside = (
        (places[None, :, None] < height[:, None, None])
        & (places[None, None, :] < breadth[:, None, None])
    ).astype(jnp.float32)
    halves = jnp.arange(half, dtype=jnp.int32)
    reduced = (
        (halves[None, :, None] < ((height + 1) // 2)[:, None, None])
        & (halves[None, None, :] < ((breadth + 1) // 2)[:, None, None])
    ).astype(jnp.float32)
    return (inside, reduced)


def spatial_taps(field, stride):
    count, side, channels = (field.shape[0], field.shape[1], field.shape[3])
    reach = stride * (side // stride - 1) + 1
    padded = jnp.pad(field, ((0, 0), (1, 1), (1, 1), (0, 0)))
    pieces = []
    for row in range(3):
        for column in range(3):
            pieces.append(
                lax.slice(
                    padded,
                    (0, row, column, 0),
                    (count, row + reach, column + reach, channels),
                    (1, stride, stride, 1),
                )
            )
    return jnp.concatenate(pieces, axis=3)


def untap(grads, stride, side):
    count, out_side = (grads.shape[0], grads.shape[1])
    channels = grads.shape[3] // 9
    reach = stride * (out_side - 1) + 1
    total = jnp.zeros((count, side + 2, side + 2, channels), jnp.float32)
    for row in range(3):
        for column in range(3):
            first = (row * 3 + column) * channels
            piece = grads[:, :, :, first : first + channels]
            total = total + lax.pad(
                piece,
                jnp.float32(0.0),
                (
                    (0, 0, 0),
                    (row, side + 2 - row - reach, stride - 1),
                    (column, side + 2 - column - reach, stride - 1),
                    (0, 0, 0),
                ),
            )
    return total[:, 1 : side + 1, 1 : side + 1, :]


def batch_statistics(fields, mask):
    weights = mask[..., None]
    terms = []
    for field in fields:
        terms.append(jnp.sum(field * weights, axis=(0, 1, 2)))
        terms.append(jnp.sum(field * field * weights, axis=(0, 1, 2)))
    packed, total_vector = lax.psum((jnp.concatenate(terms), jnp.sum(mask).reshape(1)), "dp")
    total = total_vector[0]
    result = []
    offset = 0
    for field in fields:
        breadth = field.shape[3]
        mean = packed[offset : offset + breadth] / total
        second = packed[offset + breadth : offset + 2 * breadth] / total
        result.append((mean, lax.rsqrt(second - mean * mean + eps_norm)))
        offset = offset + 2 * breadth
    return (result, total)


def standardize(raw, statistics, gain, shift):
    mean, scale = statistics
    normed = (raw - mean) * scale
    return (normed, normed * gain + shift)


def batch_backward(grads, normeds, scales, gains, mask, total, extras):
    terms = []
    for grad, normed in zip(grads, normeds):
        terms.append(jnp.sum(grad * normed, axis=(0, 1, 2)))
        terms.append(jnp.sum(grad, axis=(0, 1, 2)))
    for extra in extras:
        terms.append(extra)
    packed = lax.psum(jnp.concatenate(terms), "dp")
    results = []
    pairs = []
    offset = 0
    for grad, normed, scale, gain in zip(grads, normeds, scales, gains):
        breadth = grad.shape[3]
        gain_grad = packed[offset : offset + breadth]
        shift_grad = packed[offset + breadth : offset + 2 * breadth]
        offset = offset + 2 * breadth
        results.append(
            scale * gain * (grad - mask[..., None] * (shift_grad + normed * gain_grad) / total)
        )
        pairs.append((gain_grad, shift_grad))
    rest = []
    for extra in extras:
        rest.append(packed[offset : offset + extra.shape[0]])
        offset = offset + extra.shape[0]
    return (results, pairs, rest)


def excite_forward(field, mask, pixels, squeeze_full, squeeze_bias, excite_full, excite_bias):
    pooled = jnp.sum(field * mask[..., None], axis=(1, 2)) / pixels[:, None]
    inner_pre = (
        jnp.dot(pooled, squeeze_full.astype(jnp.float32), precision=highest) + squeeze_bias
    )
    hidden = jax.nn.silu(inner_pre)
    scale = jax.nn.sigmoid(
        jnp.dot(hidden, excite_full.astype(jnp.float32), precision=highest) + excite_bias
    )
    return (pooled, inner_pre, hidden, scale)


def excite_backward(grad_branch, field, mask, pixels, saved, squeeze_full, excite_full):
    pooled, inner_pre, hidden, scale = saved
    grad_scale = jnp.sum(grad_branch * field, axis=(1, 2))
    grad_gate = grad_scale * scale * (1.0 - scale)
    excite_grad = jnp.dot(hidden.T, grad_gate, precision=highest)
    grad_hidden = jnp.dot(grad_gate, excite_full.astype(jnp.float32).T, precision=highest)
    grad_inner = grad_hidden * swish_slope(inner_pre)
    squeeze_grad = jnp.dot(pooled.T, grad_inner, precision=highest)
    grad_pooled = jnp.dot(grad_inner, squeeze_full.astype(jnp.float32).T, precision=highest)
    grad_field = (
        grad_branch * scale[:, None, None, :]
        + grad_pooled[:, None, None, :] * mask[..., None] / pixels[:, None, None, None]
    )
    return (
        grad_field,
        squeeze_grad,
        excite_grad,
        jnp.sum(grad_inner, axis=0),
        jnp.sum(grad_gate, axis=0),
    )


def whole_vector(value):
    return lax.all_gather(value, "mp", axis=0, tiled=True)


def whole_matrix(value, dp_axis, mp_axis):
    value = lax.all_gather(value, "dp", axis=dp_axis, tiled=True)
    return lax.all_gather(value, "mp", axis=mp_axis, tiled=True)


def own_part(value, dp_axis, mp_axis):
    value = lax.psum_scatter(
        value.astype(jnp.bfloat16), "mp", scatter_dimension=mp_axis, tiled=True
    )
    return lax.psum_scatter(value, "dp", scatter_dimension=dp_axis, tiled=True).astype(
        jnp.float32
    )


def plain_shards(
    images,
    image_size,
    entry_weight,
    entry_gain,
    entry_shift,
    stride_weight,
    stride_gain,
    stride_shift,
    expand_weight,
    expand_gain,
    expand_shift,
    project_weight,
    project_gain,
    project_shift,
    squeeze_weight,
    squeeze_bias,
    excite_weight,
    excite_bias,
    reduce_weight,
    reduce_gain,
    reduce_shift,
    spatial_weight,
    spatial_gain,
    spatial_shift,
    widen_weight,
    widen_gain,
    widen_shift,
    shrink_weight,
    shrink_bias,
    gating_weight,
    gating_bias,
    cotangent,
):
    place = lax.axis_index("mp")
    count, side = (images.shape[1], images.shape[2])
    half = side // 2
    channels_in = images.shape[4]
    entry_full = whole_matrix(entry_weight, 0, 1)
    stride_full = whole_matrix(stride_weight, 2, 3)
    expand_full = whole_matrix(expand_weight, 1, 0)
    project_full = whole_matrix(project_weight, 0, 1)
    squeeze_full = whole_matrix(squeeze_weight, 1, 0)
    excite_full = whole_matrix(excite_weight, 0, 1)
    reduce_full = whole_matrix(reduce_weight, 0, 1)
    spatial_full = whole_matrix(spatial_weight, 2, 3)
    widen_full = whole_matrix(widen_weight, 1, 0)
    shrink_full = whole_matrix(shrink_weight, 1, 0)
    gating_full = whole_matrix(gating_weight, 0, 1)
    entry_gain, entry_shift = whole_vector(entry_gain), whole_vector(entry_shift)
    stride_gain, stride_shift = whole_vector(stride_gain), whole_vector(stride_shift)
    expand_gain, expand_shift = whole_vector(expand_gain), whole_vector(expand_shift)
    project_gain, project_shift = whole_vector(project_gain), whole_vector(project_shift)
    reduce_gain, reduce_shift = whole_vector(reduce_gain), whole_vector(reduce_shift)
    spatial_gain, spatial_shift = whole_vector(spatial_gain), whole_vector(spatial_shift)
    widen_gain, widen_shift = whole_vector(widen_gain), whole_vector(widen_shift)
    excite_bias, gating_bias = whole_vector(excite_bias), whole_vector(gating_bias)
    seed_grad = lax.all_to_all(cotangent, "mp", split_axis=0, concat_axis=4, tiled=True)[0]
    picture = lax.dynamic_index_in_dim(images, place, 0, keepdims=False)
    sizes = lax.dynamic_index_in_dim(image_size, place, 0, keepdims=False)
    inside, reduced = pixel_masks(sizes, side)
    pixels = jnp.sum(reduced, axis=(1, 2))
    reduced_mask = reduced[..., None]
    entry_raw = matmul(picture.reshape(-1, channels_in), entry_full).reshape(
        count, side, side, -1
    )
    stats, inside_total = batch_statistics([entry_raw], inside)
    entry_stats = stats[0]
    entry_normed, entry_pre = standardize(entry_raw, entry_stats, entry_gain, entry_shift)
    entry_act = (jax.nn.silu(entry_pre) * inside[..., None]).astype(jnp.bfloat16)
    entry_wide = entry_act
    bottleneck = entry_wide.shape[3]
    stride_taps = spatial_taps(entry_wide, 2).reshape(-1, 9 * bottleneck)
    stride_raw = matmul(stride_taps, stride_full.reshape(9 * bottleneck, -1)).reshape(
        count, half, half, -1
    )
    stats, reduced_total = batch_statistics([stride_raw], reduced)
    stride_stats = stats[0]
    stride_normed, stride_pre = standardize(stride_raw, stride_stats, stride_gain, stride_shift)
    stride_act = (jax.nn.silu(stride_pre) * reduced_mask).astype(jnp.bfloat16)
    local_bottleneck = stride_act.shape[3]
    stride_flat = stride_act.reshape(-1, local_bottleneck)
    expand_raw = matmul(stride_flat, expand_full).reshape(count, half, half, -1)
    strided_flat = picture[:, ::2, ::2, :].reshape(-1, channels_in)
    project_raw = matmul(strided_flat, project_full).reshape(count, half, half, -1)
    stats, reduced_total = batch_statistics([expand_raw, project_raw], reduced)
    expand_stats, project_stats = (stats[0], stats[1])
    expand_normed, expand_pre = standardize(expand_raw, expand_stats, expand_gain, expand_shift)
    project_normed, project_pre = standardize(
        project_raw, project_stats, project_gain, project_shift
    )
    first_saved = excite_forward(
        expand_pre, reduced, pixels, squeeze_full, squeeze_bias, excite_full, excite_bias
    )
    first_sum = expand_pre * first_saved[3][:, None, None, :] + project_pre
    first_out = (jax.nn.silu(first_sum) * reduced_mask).astype(jnp.bfloat16)
    block_wide = first_out
    block_flat = block_wide.reshape(-1, block_wide.shape[3])
    reduce_raw = matmul(block_flat, reduce_full).reshape(count, half, half, -1)
    stats, reduced_total = batch_statistics([reduce_raw], reduced)
    reduce_stats = stats[0]
    reduce_normed, reduce_pre = standardize(reduce_raw, reduce_stats, reduce_gain, reduce_shift)
    reduce_act = (jax.nn.silu(reduce_pre) * reduced_mask).astype(jnp.bfloat16)
    reduce_wide = reduce_act
    second_taps = spatial_taps(reduce_wide, 1).reshape(-1, 9 * bottleneck)
    spatial_raw = matmul(second_taps, spatial_full.reshape(9 * bottleneck, -1)).reshape(
        count, half, half, -1
    )
    stats, reduced_total = batch_statistics([spatial_raw], reduced)
    spatial_stats = stats[0]
    spatial_normed, spatial_pre = standardize(
        spatial_raw, spatial_stats, spatial_gain, spatial_shift
    )
    spatial_act = (jax.nn.silu(spatial_pre) * reduced_mask).astype(jnp.bfloat16)
    spatial_flat = spatial_act.reshape(-1, local_bottleneck)
    widen_raw = matmul(spatial_flat, widen_full).reshape(count, half, half, -1)
    stats, reduced_total = batch_statistics([widen_raw], reduced)
    widen_stats = stats[0]
    widen_normed, widen_pre = standardize(widen_raw, widen_stats, widen_gain, widen_shift)
    second_saved = excite_forward(
        widen_pre, reduced, pixels, shrink_full, shrink_bias, gating_full, gating_bias
    )
    second_sum = widen_pre * second_saved[3][:, None, None, :] + first_out.astype(jnp.float32)
    output = (jax.nn.silu(second_sum) * reduced_mask).astype(jnp.bfloat16)
    second_grad = seed_grad.astype(jnp.float32) * reduced_mask * swish_slope(second_sum)
    widen_grad, shrink_grad, gating_grad, shrink_bias_grad, gating_bias_grad = excite_backward(
        second_grad, widen_pre, reduced, pixels, second_saved, shrink_full, gating_full
    )
    grads, widen_pair, extras = batch_backward(
        [widen_grad],
        [widen_normed],
        [widen_stats[1]],
        [widen_gain],
        reduced,
        reduced_total,
        (shrink_bias_grad, gating_bias_grad),
    )
    widen_pair = widen_pair[0]
    shrink_bias_total, gating_bias_total = (extras[0], extras[1])
    widen_local = grads[0].astype(jnp.bfloat16)
    widen_low = widen_local
    widen_flat = widen_low.reshape(-1, widen_low.shape[3])
    widen_weight_grad = contract_rows(spatial_flat, widen_flat)
    spatial_act_grad = contract_cols(widen_flat, widen_full).reshape(count, half, half, -1)
    spatial_grad = spatial_act_grad * reduced_mask * swish_slope(spatial_pre)
    grads, spatial_pair, extras = batch_backward(
        [spatial_grad],
        [spatial_normed],
        [spatial_stats[1]],
        [spatial_gain],
        reduced,
        reduced_total,
        (),
    )
    spatial_pair = spatial_pair[0]
    spatial_low = grads[0].astype(jnp.bfloat16).reshape(-1, local_bottleneck)
    spatial_weight_grad = contract_rows(second_taps, spatial_low).reshape(
        3, 3, bottleneck, local_bottleneck
    )
    second_tap_grad = contract_cols(spatial_low, spatial_full.reshape(9 * bottleneck, -1))
    reduce_act_grad = untap(second_tap_grad.reshape(count, half, half, -1), 1, half)
    reduce_grad = reduce_act_grad * reduced_mask * swish_slope(reduce_pre)
    grads, reduce_pair, extras = batch_backward(
        [reduce_grad],
        [reduce_normed],
        [reduce_stats[1]],
        [reduce_gain],
        reduced,
        reduced_total,
        (),
    )
    reduce_pair = reduce_pair[0]
    reduce_low = grads[0].astype(jnp.bfloat16).reshape(-1, local_bottleneck)
    reduce_weight_grad = contract_rows(block_flat, reduce_low)
    first_partial = contract_cols(reduce_low, reduce_full).reshape(count, half, half, -1)
    first_out_grad = first_partial + second_grad
    first_grad = first_out_grad * reduced_mask * swish_slope(first_sum)
    expand_grad, squeeze_grad, excite_grad, squeeze_bias_grad, excite_bias_grad = (
        excite_backward(
            first_grad, expand_pre, reduced, pixels, first_saved, squeeze_full, excite_full
        )
    )
    grads, pairs, extras = batch_backward(
        [expand_grad, first_grad],
        [expand_normed, project_normed],
        [expand_stats[1], project_stats[1]],
        [expand_gain, project_gain],
        reduced,
        reduced_total,
        (squeeze_bias_grad, excite_bias_grad),
    )
    expand_pair, project_pair = (pairs[0], pairs[1])
    squeeze_bias_total, excite_bias_total = (extras[0], extras[1])
    expand_local = grads[0].astype(jnp.bfloat16)
    expand_low = expand_local
    expand_flat = expand_low.reshape(-1, expand_low.shape[3])
    expand_weight_grad = contract_rows(stride_flat, expand_flat)
    stride_act_grad = contract_cols(expand_flat, expand_full).reshape(count, half, half, -1)
    project_low = grads[1].astype(jnp.bfloat16).reshape(-1, grads[1].shape[3])
    project_weight_grad = contract_rows(strided_flat, project_low)
    strided_grad = contract_cols(project_low, project_full).reshape(
        count, half, half, channels_in
    )
    stride_grad = stride_act_grad * reduced_mask * swish_slope(stride_pre)
    grads, stride_pair, extras = batch_backward(
        [stride_grad],
        [stride_normed],
        [stride_stats[1]],
        [stride_gain],
        reduced,
        reduced_total,
        (),
    )
    stride_pair = stride_pair[0]
    stride_low = grads[0].astype(jnp.bfloat16).reshape(-1, local_bottleneck)
    stride_weight_grad = contract_rows(stride_taps, stride_low).reshape(
        3, 3, bottleneck, local_bottleneck
    )
    first_tap_grad = contract_cols(stride_low, stride_full.reshape(9 * bottleneck, -1))
    entry_act_grad = untap(first_tap_grad.reshape(count, half, half, -1), 2, side)
    entry_grad = entry_act_grad * inside[..., None] * swish_slope(entry_pre)
    grads, entry_pair, extras = batch_backward(
        [entry_grad], [entry_normed], [entry_stats[1]], [entry_gain], inside, inside_total, ()
    )
    entry_pair = entry_pair[0]
    entry_low = grads[0].astype(jnp.bfloat16).reshape(-1, local_bottleneck)
    entry_weight_grad = contract_rows(picture.reshape(-1, channels_in), entry_low)
    picture_partial = contract_cols(entry_low, entry_full).reshape(
        count, side, side, channels_in
    )
    picture_partial = picture_partial + lax.pad(
        strided_grad, jnp.float32(0.0), ((0, 0, 0), (0, 1, 1), (0, 1, 1), (0, 0, 0))
    )

    def own_vector(value):
        return lax.psum_scatter(value, "mp", scatter_dimension=0, tiled=True)

    picture_grad = lax.all_to_all(
        picture_partial.astype(jnp.bfloat16)[None], "mp", split_axis=4, concat_axis=0, tiled=True
    ).astype(jnp.float32)
    result = lax.all_to_all(output[None], "mp", split_axis=4, concat_axis=0, tiled=True)
    return (
        result,
        picture_grad,
        own_part(entry_weight_grad, 0, 1),
        own_vector(entry_pair[0]),
        own_vector(entry_pair[1]),
        own_part(stride_weight_grad, 2, 3),
        own_vector(stride_pair[0]),
        own_vector(stride_pair[1]),
        own_part(expand_weight_grad, 1, 0),
        own_vector(expand_pair[0]),
        own_vector(expand_pair[1]),
        own_part(project_weight_grad, 0, 1),
        own_vector(project_pair[0]),
        own_vector(project_pair[1]),
        own_part(squeeze_grad, 1, 0),
        lax.psum(squeeze_bias_total, "mp"),
        own_part(excite_grad, 0, 1),
        own_vector(excite_bias_total),
        own_part(reduce_weight_grad, 0, 1),
        own_vector(reduce_pair[0]),
        own_vector(reduce_pair[1]),
        own_part(spatial_weight_grad, 2, 3),
        own_vector(spatial_pair[0]),
        own_vector(spatial_pair[1]),
        own_part(widen_weight_grad, 1, 0),
        own_vector(widen_pair[0]),
        own_vector(widen_pair[1]),
        own_part(shrink_grad, 1, 0),
        lax.psum(shrink_bias_total, "mp"),
        own_part(gating_grad, 0, 1),
        own_vector(gating_bias_total),
    )


def solution(mesh):
    in_specs = (
        P(None, "dp", None, None, None),
        P(None, "dp", None),
        P("dp", "mp"),
        P("mp"),
        P("mp"),
        P(None, None, "dp", "mp"),
        P("mp"),
        P("mp"),
        P("mp", "dp"),
        P("mp"),
        P("mp"),
        P("dp", "mp"),
        P("mp"),
        P("mp"),
        P("mp", "dp"),
        P(),
        P("dp", "mp"),
        P("mp"),
        P("dp", "mp"),
        P("mp"),
        P("mp"),
        P(None, None, "dp", "mp"),
        P("mp"),
        P("mp"),
        P("mp", "dp"),
        P("mp"),
        P("mp"),
        P("mp", "dp"),
        P(),
        P("dp", "mp"),
        P("mp"),
        P(None, "dp", None, None, "mp"),
    )
    out_specs = (
        P(None, "dp", None, None, "mp"),
        P(None, "dp", None, None, "mp"),
        P("dp", "mp"),
        P("mp"),
        P("mp"),
        P(None, None, "dp", "mp"),
        P("mp"),
        P("mp"),
        P("mp", "dp"),
        P("mp"),
        P("mp"),
        P("dp", "mp"),
        P("mp"),
        P("mp"),
        P("mp", "dp"),
        P(),
        P("dp", "mp"),
        P("mp"),
        P("dp", "mp"),
        P("mp"),
        P("mp"),
        P(None, None, "dp", "mp"),
        P("mp"),
        P("mp"),
        P("mp", "dp"),
        P("mp"),
        P("mp"),
        P("mp", "dp"),
        P(),
        P("dp", "mp"),
        P("mp"),
    )
    shards = fused_shards if dict(mesh.shape) == {"dp": 8, "mp": 4} else plain_shards
    return jax.shard_map(shards, mesh=mesh, in_specs=in_specs, out_specs=out_specs, check_vma=False)
```

```python
import functools

import jax
import jax.numpy as jnp
from jax import lax
from jax.experimental import pallas as pl
from jax.experimental.pallas import tpu as pltpu
from jax.sharding import PartitionSpec as P

eps_norm = 1e-05
highest = lax.Precision.HIGHEST
BF = jnp.bfloat16
F32 = jnp.float32
MESH = pl.DeviceIdType.MESH

TENSORS = {
    "E": (128, 512, 1, "E"),
    "P": (128, 2048, 1, "P"),
    "S": (576, 512, 1, "S"),
    "X": (512, 256, 0, "X"),
    "A": (32, 2048, 1, "A"),
    "R": (256, 512, 1, "R"),
    "T": (576, 512, 1, "S"),
    "V": (512, 256, 0, "X"),
    "B": (32, 2048, 1, "A"),
}
NAMES = list(TENSORS)
PIECES = {
    "E": [(0, 128)],
    "P": [(0, 32), (32, 32), (64, 32), (96, 32)],
    "S": [(0, 128), (128, 128), (256, 128), (384, 192)],
    "X": [(0, 128), (128, 128)],
    "A": [(0, 32)],
    "R": [(0, 128), (128, 128)],
    "T": [(0, 128), (128, 128), (256, 128), (384, 192)],
    "V": [(0, 128), (128, 128)],
    "B": [(0, 32)],
}
ORDER = [(n, i) for n in NAMES for i in range(len(PIECES[n]))]
INDEX = {piece: i for i, piece in enumerate(ORDER)}
AG_MORE = ()
RS_MORE = (0, 2, 4, 5, 6, 7, 8)
AG_ROWS, RS_ROWS = 8, 12
LAST = {n: INDEX[n, len(PIECES[n]) - 1] for n in NAMES}
COUNT = len(ORDER)
LEAD, LAG, RLAG = 3, 2, 3
OPT = ()
TICKS = "bch"
STARTS = 1
ENDLAG = 2
PUMPS = "ABCDEFGHIJKLMNOPQRSUVWXY"
CLASSES = {"E": (128, 128), "P": (128, 512), "S": (576, 128), "X": (128, 256), "A": (32, 512), "R": (256, 128)}
Q = 192
VMEM_LIMIT = 64 * 2**20
WIDE = 2048
EXCHANGES = {
    "entry": (4, 512), "stride": (2, 512), "xp": (4, 2048), "reduce": (2, 512), "spatial": (2, 512), "widen": (2, 2048),
    "widen_b": (4, 2048), "spatial_b": (2, 512), "reduce_b": (2, 512), "xp_b": (4, 2048), "bias_b": (2, 2048),
    "stride_b": (2, 512), "entry_b": (2, 512),
}
EX = {n: i % 2 for i, n in enumerate(n for n in EXCHANGES if n != "bias_b")}
EX["bias_b"] = 2
ROW = {"entry": 0, "stride": 2, "reduce": 4, "spatial": 6, "expand": 8, "project": 16, "widen": 24, "excite": 32, "gating": 36,
       "squeeze": 40, "shrink": 41}
SMALL = 48
NORM512 = {"entry": 0, "stride": 1, "reduce": 2, "spatial": 3}
NORM2048 = {"expand": 0, "project": 1, "widen": 2}


def sigmoid(v):
    return 0.5 + 0.5 * jnp.tanh(0.5 * v)


def dot(a, b):
    return jnp.dot(a, b, preferred_element_type=F32)


def dot_cols(a, b):
    return lax.dot_general(a, b, (((1,), (1,)), ((), ())), preferred_element_type=F32)


def dot_rows(a, b):
    return lax.dot_general(a, b, (((0,), (0,)), ((), ())), preferred_element_type=F32)


def halves(v):
    high = v.astype(BF)
    return high, (v - high.astype(F32)).astype(BF)


def exact(fn, v, w):
    high, low = halves(v)
    return fn(high, w) + fn(low, w)


def outer(a, b):
    ah, al = halves(a)
    bh, bl = halves(b)
    af, alf, bf, blf = ah.astype(F32), al.astype(F32), bh.astype(F32), bl.astype(F32)
    left = jnp.concatenate([af, af, alf, jnp.zeros_like(af)], axis=0).astype(BF)
    right = jnp.concatenate([bf, blf, bf, jnp.zeros_like(bf)], axis=0).astype(BF)
    return dot_rows(left, right)


def lanes(v, times):
    return jnp.concatenate([v] * times, axis=1) if times > 1 else v


def scratch_list():
    s = {}
    for n, (r, c, _, _) in TENSORS.items():
        s["W" + n] = pltpu.VMEM((4, 2, r, c), BF)
    for k, (r, c) in CLASSES.items():
        s["RC" + k] = pltpu.VMEM((2, 4, 2, r, c), BF)
        s["R1" + k] = pltpu.VMEM((4, r, c), BF)
        s["R2" + k] = pltpu.VMEM((2, 4, r, c), BF)
        s["RZ" + k] = pltpu.VMEM((3, r, c), BF)
    for n, (r, c) in EXCHANGES.items():
        s["X_" + n] = pltpu.VMEM((8, r, c), F32)
    s["picT"] = pltpu.VMEM((768, 1024), BF)
    s["stage"] = pltpu.VMEM((768, 1024), BF)
    s["taps1"] = pltpu.VMEM((Q, 4608), BF)
    s["taps2"] = pltpu.VMEM((Q, 4608), BF)
    s["act_e"] = pltpu.VMEM((Q, WIDE), BF)
    s["act_s"] = pltpu.VMEM((Q, 512), BF)
    s["act_p"] = pltpu.VMEM((Q, 512), BF)
    s["first"] = pltpu.VMEM((Q, WIDE), BF)
    s["cotb"] = pltpu.VMEM((Q, WIDE), BF)
    s["g1"] = pltpu.VMEM((Q, WIDE), BF)
    s["g2"] = pltpu.VMEM((Q, WIDE), BF)
    s["gs"] = pltpu.VMEM((Q, 512), BF)
    s["shift"] = pltpu.VMEM((9, Q, Q), BF)
    s["perm"] = pltpu.VMEM((256, 256), BF)
    for n in ("e_raw", "x_raw", "j_raw", "w_raw", "sg"):
        s[n] = pltpu.VMEM((Q, WIDE), F32)
    for n in ("s_raw", "r_raw", "p_raw", "gq", "acc"):
        s[n] = pltpu.VMEM((Q, 512), F32)
    s["sgrad"] = pltpu.VMEM((Q, 1024), F32)
    s["insm"] = pltpu.VMEM((768, 128), F32)
    s["redm"] = pltpu.VMEM((Q, 128), F32)
    s["pix"] = pltpu.VMEM((8, 128), F32)
    s["cnt"] = pltpu.VMEM((8, 512), F32)
    s["gv5"] = pltpu.VMEM((8, 512), F32)
    s["gv20"] = pltpu.VMEM((8, WIDE), F32)
    s["nv5"] = pltpu.VMEM((4, 8, 512), F32)
    s["nv20"] = pltpu.VMEM((3, 8, WIDE), F32)
    for n in ("isum1", "isum2", "pool1", "pool2", "scale1", "scale2", "pg", "G0", "G1", "gate"):
        s[n] = pltpu.VMEM((8, WIDE), F32)
    for n in ("inner1", "inner2", "ing"):
        s[n] = pltpu.VMEM((8, 128), F32)
    s["params"] = pltpu.VMEM((SMALL, 128), F32)
    for n, _, rows in VECTORS:
        s["v_" + n] = pltpu.VMEM((rows, 128), F32)
    for n in ("A", "B"):
        s["in" + n] = pltpu.VMEM((32, 512), BF)
    s["PR"] = pltpu.VMEM((4, SMALL, 128), F32)
    s["FS"] = pltpu.VMEM((4, SMALL, 128), F32)
    s["FR"] = pltpu.VMEM((4, SMALL, 128), F32)
    dma = pltpu.SemaphoreType.DMA
    s["ag_s"] = dma((AG_ROWS, 9))
    s["ag_r"] = dma((AG_ROWS, 7))
    s["ag_rc"] = dma((COUNT, 2))
    s["loc"] = dma((COUNT + 4,))
    s["vec"] = dma((len(VECTORS) + 4,))
    s["rs_s"] = dma((RS_ROWS, 9))
    s["rs_r"] = dma((RS_ROWS, 9))
    s["st_s"] = dma((3, 7))
    s["st_r"] = dma((3, 8))
    s["mp_s"] = dma((5, 4))
    s["mp_r"] = dma((5, 4))
    s["free"] = pltpu.SemaphoreType.REGULAR((3,))
    return s


VECTORS = []
for _n in ("entry", "stride", "reduce", "spatial"):
    VECTORS += [(_n + "_gain", ROW[_n], 1), (_n + "_shift", ROW[_n] + 1, 1)]
for _n in ("expand", "project", "widen"):
    VECTORS += [(_n + "_gain", ROW[_n], 4), (_n + "_shift", ROW[_n] + 4, 4)]
VECTORS += [("excite_bias", ROW["excite"], 4), ("gating_bias", ROW["gating"], 4)]
VECTORS += [("squeeze_bias", ROW["squeeze"], 1), ("shrink_bias", ROW["shrink"], 1)]
PLAIN = [n for n in NAMES if n not in ("A", "B")]
IN_NAMES = ["images", "sizes", "cot_in"] + ["in" + n for n in PLAIN] + ["sqA", "exA", "sqB", "exB"] + [v[0] for v in VECTORS]
OUT_NAMES = ["result", "igrad"] + ["out" + n for n in NAMES] + ["small"]
LAST_IN = ["result", "igrad"] + ["out" + n for n in NAMES] + ["small"]
LAST_OUT = ["f_result", "f_igrad"] + ["f_" + n for n in PLAIN] + ["f_sqA", "f_exA", "f_sqB", "f_exB"] + [v[0] for v in VECTORS]


def last_body(*refs):
    g = dict(zip(LAST_IN + LAST_OUT, refs))
    step = pl.program_id(0)

    @pl.when(step == 0)
    def _():
        for n in PLAIN:
            g["f_" + n][...] = g["out" + n][...]
        for n in "AB":
            g["f_sq" + n][...] = g["out" + n][0:16, :]
            g["f_ex" + n][...] = g["out" + n][16:32, :]
        for n, row, rows in VECTORS:
            g[n][...] = g["small"][row : row + rows, :]

    g["f_igrad"][...] = g["igrad"][...].astype(F32)
    g["f_result"][...] = g["result"][...]


class Copy:
    def __init__(self, *given):
        self.given = given

    def made(self):
        src, dst, ss, rs, dev = self.given
        return pltpu.make_async_remote_copy(
            src_ref=src, dst_ref=dst, send_sem=ss, recv_sem=rs, device_id=dev, device_id_type=MESH
        )

    def start(self, priority=0):
        self.made().start(priority=priority)

    def wait_recv(self):
        self.made().wait_recv()

    def wait_send(self):
        self.made().wait_send()


def body(*refs):
    names = IN_NAMES + OUT_NAMES + list(scratch_list())
    g = dict(zip(names, refs))

    class NS:
        def __getattr__(self, k):
            return g[k]

    s = NS()
    d = lax.axis_index("dp")
    m = lax.axis_index("mp")
    z, y = d // 2, lax.rem(d, 2)
    x, c = m // 2, lax.rem(m, 2)
    mx = (1 - x) * 2 + c
    mc = x * 2 + (1 - c)
    whole = slice(None)
    xdev, ydev, cdev = (d, mx), (z * 2 + (1 - y), m), (d, mc)

    def zdev(k):
        return (lax.rem(z + k, 4) * 2 + y, m)

    def mdev(k):
        return (d, lax.rem(m + k, 4))

    def col(j, w):
        return pl.ds(pl.multiple_of(j * w, w), w)

    def rcopy(src, dst, ss, rs, dev):
        return Copy(src, dst, ss, rs, dev)

    partners = [(lax.rem(z + k // 2, 4) * 2 + lax.rem(y + k % 2, 2), m) for k in range(1, 8)]
    partners += [mdev(k) for k in range(1, 4)]
    vec = [pltpu.make_async_copy(g[v[0]], g["v_" + v[0]], s.vec.at[i]) for i, v in enumerate(VECTORS)]
    for i, n in enumerate("AB"):
        vec += [
            pltpu.make_async_copy(g["sq" + n], g["in" + n].at[pl.ds(0, 16)], s.vec.at[len(VECTORS) + 2 * i]),
            pltpu.make_async_copy(g["ex" + n], g["in" + n].at[pl.ds(16, 16)], s.vec.at[len(VECTORS) + 2 * i + 1]),
        ]
    own_pic = pltpu.make_async_copy(s.images.at[m], s.stage, s.loc.at[COUNT])
    own_pic.start()
    for t in vec:
        t.start()
    barrier = pltpu.get_barrier_semaphore()
    for dev in partners:
        pl.semaphore_signal(barrier, inc=1, device_id=dev, device_id_type=MESH)
    pl.semaphore_wait(barrier, len(partners))

    def part(piece, zs, ys, mi):
        n, i = piece
        rows, columns, dim, _ = TENSORS[n]
        start, size = PIECES[n][i]
        if dim == 1:
            return g["W" + n].at[zs, ys, pl.ds(start, size), col(mi, columns // 4)]
        return g["W" + n].at[zs, ys, col(mi, rows // 4), pl.ds(start, size)]

    def cut(piece):
        n, i = piece
        start, size = PIECES[n][i]
        return (pl.ds(start, size), whole) if TENSORS[n][2] == 1 else (whole, pl.ds(start, size))

    def shard(piece):
        return g["in" + piece[0]].at[cut(piece)]

    def ag(p, slot, region, dev, src=None):
        i = INDEX[p]
        row = i % AG_ROWS
        arrival = s.ag_r.at[row, slot] if slot < 7 else s.ag_rc.at[i, slot - 7]
        return rcopy(region if src is None else src, region, s.ag_s.at[row, slot], arrival, dev)

    def place(p):
        return pltpu.make_async_copy(shard(p), part(p, z, y, m), s.loc.at[INDEX[p]])

    def ag_copies(p):
        own = part(p, z, y, m)
        out, here = {}, {}
        share = 3 if INDEX[p] in AG_MORE else 2
        low, high = pl.ds(0, share), pl.ds(share, 4 - share)
        out[0] = [ag(p, k - 1, own, zdev(k), shard(p)) for k in range(1, 4)]
        here[0] = [(k - 1, part(p, lax.rem(z + 4 - k, 4), y, m)) for k in range(1, 4)]
        out[1] = [ag(p, 3, part(p, whole, y, m), xdev), ag(p, 4, part(p, whole, y, m), ydev)]
        here[1] = [(3, part(p, whole, y, mx)), (4, part(p, whole, 1 - y, m))]
        out[2] = [ag(p, 5, part(p, low, y, mx), ydev)]
        here[2] = [(5, part(p, low, 1 - y, mx))]
        out[2] += [ag(p, 6, part(p, high, 1 - y, m), xdev)]
        here[2] += [(6, part(p, high, 1 - y, mx))]
        out[3] = [ag(p, 7 + xx, part(p, whole, whole, xx * 2 + c), cdev) for xx in range(2)]
        here[3] = [(7 + xx, part(p, whole, whole, xx * 2 + (1 - c))) for xx in range(2)]
        return out, here

    def landed(p, here):
        for slot, region in here:
            ag(p, slot, region, cdev).wait_recv()

    def ag_z(p):
        if INDEX[p] >= AG_ROWS:
            ag_sent(ORDER[INDEX[p] - AG_ROWS])
        place(p).start()
        for t in ag_copies(p)[0][0]:
            t.start()

    def ag_1(p):
        out, here = ag_copies(p)
        place(p).wait()
        landed(p, here[0])
        for t in out[1]:
            t.start()

    def ag_2(p):
        out, here = ag_copies(p)
        landed(p, here[1])
        for t in out[2]:
            t.start()

    def ag_c(p):
        out, here = ag_copies(p)
        landed(p, here[2])
        for t in out[3]:
            t.start()

    def ag_sent(p):
        for copies in ag_copies(p)[0].values():
            for t in copies:
                t.wait_send()

    def ag_drain(n):
        if "ag" in OPT:
            return
        for i in range(len(PIECES[n])):
            if INDEX[n, i] >= COUNT - AG_ROWS:
                ag_sent((n, i))

    ticks = {"k": 0}

    def tick():
        if "ag" in OPT:
            return
        k = ticks["k"]
        ticks["k"] = k + 1
        for stage, lag in ((ag_c, 2 * LAG), (ag_2, LAG), (ag_1, 0), (ag_z, -LEAD)):
            if 0 <= k - lag < COUNT:
                stage(ORDER[k - lag])

    def mark(tag):
        for t in TICKS:
            if t == tag:
                if ticks["k"] < COUNT + 2 * LAG:
                    tick()

    def need(n):
        if "ag" in OPT:
            return
        while ticks["k"] <= LAST[n] + 2 * LAG:
            tick()
        for i in range(len(PIECES[n])):
            landed((n, i), ag_copies((n, i))[1][3])

    def loop(count, fn, unroll=1):
        def step(j, carry):
            fn(j)
            return carry

        lax.fori_loop(0, count, step, 0, unroll=unroll)

    def rs(row, slot, region, landing, dev):
        return rcopy(region, landing, s.rs_s.at[row, slot], s.rs_r.at[row, slot], dev)

    credits = {"T": 0, "V": 1, "B": 2}
    takes = {"S": ("T", 0), "X": ("V", 1), "A": ("B", 2)}
    active = []

    def pause():
        steps = 0
        while steps < state["lag"]:
            steps += 1
            yield

    def bump(region, extra):
        region[...] = region[...] + extra

    def reduce_scatter(p, row):
        n, piece = p
        k = TENSORS[n][3]
        rc, r1, r2, rz = g["RC" + k], g["R1" + k], g["R2" + k], g["RZ" + k]
        c_ = cut(p)
        swap = [
            rs(row, xx, part(p, whole, whole, xx * 2 + (1 - c)), rc.at[(xx, pl.ds(0, 4), pl.ds(0, 2)) + c_], cdev) for xx in range(2)
        ]
        share = 3 if INDEX[p] in RS_MORE else 2
        low, high = pl.ds(0, 4 - share), pl.ds(4 - share, share)
        first = [
            rs(row, 2, part(p, low, 1 - y, mx), r1.at[(low,) + c_], xdev),
            rs(row, 3, part(p, high, 1 - y, mx), r1.at[(high,) + c_], ydev),
        ]
        second = [
            rs(row, 4, part(p, whole, y, mx), r2.at[(0, pl.ds(0, 4)) + c_], xdev),
            rs(row, 5, part(p, whole, 1 - y, m), r2.at[(1, pl.ds(0, 4)) + c_], ydev),
        ]
        third = [rs(row, 5 + k, part(p, lax.rem(z + k, 4), y, m), rz.at[(k - 1,) + c_], zdev(k)) for k in range(1, 4)]
        for t in swap:
            t.start()
        yield
        for t in swap:
            t.wait_recv()

        def add_c(j):
            zz, yy = j // 2, lax.rem(j, 2)
            for xx in range(2):
                bump(part(p, zz, yy, xx * 2 + c), rc[(xx, zz, yy) + c_])

        loop(8, add_c)
        for t in first:
            t.start()
        yield from pause()
        for t in first:
            t.wait_recv()
        for h in range(4 - share):
            bump(part(p, h, 1 - y, m), r1[(h,) + c_])
        for h in range(4 - share, 4):
            bump(part(p, h, y, mx), r1[(h,) + c_])
        for t in second:
            t.start()
        yield from pause()
        for t in second:
            t.wait_recv()

        def add_2(zz):
            bump(part(p, zz, y, m), (r2[(0, zz) + c_].astype(F32) + r2[(1, zz) + c_].astype(F32)).astype(BF))

        loop(4, add_2)
        for t in third:
            t.start()
        yield from pause()
        for t in third:
            t.wait_recv()
        total = part(p, z, y, m)[...].astype(F32)
        for k in range(3):
            total = total + rz[(k,) + c_].astype(F32)
        g["out" + n][c_] = total
        if n in credits and piece == len(PIECES[n]) - 1:
            for dev in [xdev, ydev, cdev] + [zdev(k) for k in range(1, 4)]:
                pl.semaphore_signal(s.free.at[credits[n]], inc=1, device_id=dev, device_id_type=MESH)
        for t in swap + first + second + third:
            t.wait_send()

    waiting = []
    state = {"lag": RLAG, "begun": 0}

    def pump():
        for item in list(active):
            try:
                next(item[1])
            except StopIteration:
                active.remove(item)
        for _ in range(STARTS):
            if not waiting:
                return
            n, i = waiting[0]
            if n in takes and i == 0:
                if any(item[0][0] == takes[n][0] for item in active):
                    return
                pl.semaphore_wait(s.free.at[takes[n][1]], 6)
            assert len(active) < RS_ROWS
            gen = reduce_scatter(waiting.pop(0), state["begun"] % RS_ROWS)
            state["begun"] += 1
            active.append(((n, i), gen))
            next(gen)

    def pumps(tag):
        state["lag"] = RLAG
        for t in PUMPS:
            if t in "123456":
                state["lag"] = int(t)
            if t == tag:
                pump()

    def begin(n, pieces=None):
        if "rs" in OPT or "no" + n in OPT:
            return
        for i in range(len(PIECES[n])) if pieces is None else pieces:
            waiting.append((n, i))

    def st_peers():
        return [lax.rem(z + k // 2, 4) * 2 + lax.rem(y + k % 2, 2) for k in range(1, 8)]

    def send_stats(e):
        buf, i = g["X_" + e], EX[e]
        if "stats" in OPT:
            return
        for k, dd in enumerate(st_peers()):
            rcopy(buf.at[d], buf.at[d], s.st_s.at[i, k], s.st_r.at[i, d], (dd, m)).start(priority=1 if 'prio' in OPT else 0)

    def get_stats(e):
        buf, i = g["X_" + e], EX[e]
        for k, dd in enumerate([] if "stats" in OPT else st_peers()):
            rcopy(buf.at[dd], buf.at[dd], s.st_s.at[i, k], s.st_r.at[i, dd], (dd, m)).wait_recv()
        for k, dd in enumerate([] if "stats" in OPT else st_peers()):
            rcopy(buf.at[d], buf.at[d], s.st_s.at[i, k], s.st_r.at[i, d], (dd, m)).wait_send()
        total = buf[0]
        for k in range(1, 8):
            total = total + buf[k]
        return total

    def mp_copies(i, src, dst):
        return [rcopy(src(lax.rem(m + k, 4)), dst(m), s.mp_s.at[i, k], s.mp_r.at[i, k], mdev(k)) for k in range(1, 4)]

    def mp_wait(i, src, dst, recv=True, send=True):
        for k in range(1, 4):
            if recv:
                rcopy(src(m), dst(lax.rem(m + 4 - k, 4)), s.mp_s.at[i, k], s.mp_r.at[i, k], mdev(k)).wait_recv()
            if send:
                rcopy(src(lax.rem(m + k, 4)), dst(m), s.mp_s.at[i, k], s.mp_r.at[i, k], mdev(k)).wait_send()

    cot_src, cot_dst = (lambda j: s.cot_in.at[j]), (lambda j: s.cotb.at[:, col(j, 512)])
    par_src, par_dst = (lambda j: s.params), (lambda j: s.PR.at[j])
    res_src, res_dst = (lambda j: s.g2.at[:, col(j, 512)]), (lambda j: s.result.at[j])
    img_src, img_dst = (lambda j: s.stage.at[:, col(j, 256)]), (lambda j: s.igrad.at[j])
    fin_src, fin_dst = (lambda j: s.FS.at[j]), (lambda j: s.FR.at[j])

    if "ag" not in OPT:
        for p in ORDER[:LEAD]:
            ag_z(p)
    for t in vec:
        t.wait()
    for n, row, rows in VECTORS:
        s.params[row : row + rows, :] = g["v_" + n][...]
    s.params[42:SMALL, :] = jnp.zeros((SMALL - 42, 128), F32)
    for t in mp_copies(1, par_src, par_dst):
        t.start()
    s.PR[m] = s.params[...]

    if "start0" in OPT:
        mp_wait(1, par_src, par_dst)
        own_pic.wait()
        return
    r64 = lax.broadcasted_iota(jnp.int32, (64, 128), 0)
    p64, q64 = r64 >> 3, r64 & 7
    s.pix[...] = jnp.ones((8, 128), F32)
    for i in range(3):
        high, wide = s.sizes[m, i, 0], s.sizes[m, i, 1]
        for pa in range(2):
            for pb in range(2):
                ok = (2 * p64 + pa < high) & (2 * q64 + pb < wide)
                s.insm[(pa * 2 + pb) * Q + i * 64 : (pa * 2 + pb) * Q + i * 64 + 64, :] = jnp.where(ok, 1.0, 0.0).astype(F32)
        ok = (2 * p64 < high) & (2 * q64 < wide)
        mask = jnp.where(ok, 1.0, 0.0).astype(F32)
        s.redm[i * 64 : i * 64 + 64, :] = mask
        s.pix[i : i + 1, :] = jnp.sum(mask, axis=0, keepdims=True)
    r8 = lax.broadcasted_iota(jnp.int32, (8, 128), 0)
    real = jnp.where(r8 < 3, 1.0, 0.0).astype(F32)

    rr = lax.broadcasted_iota(jnp.int32, (Q, Q), 0)
    cc = lax.broadcasted_iota(jnp.int32, (Q, Q), 1)
    pp, qq = (rr >> 3) & 7, rr & 7
    for t in range(9):
        da, db = t // 3 - 1, t % 3 - 1
        ok = (cc == rr + (da * 8 + db)) & (qq + db >= 0) & (qq + db < 8) & (pp + da >= 0) & (pp + da < 8)
        s.shift[t] = jnp.where(ok, 1.0, 0.0).astype(BF)
    rp = lax.broadcasted_iota(jnp.int32, (256, 256), 0)
    cp_ = lax.broadcasted_iota(jnp.int32, (256, 256), 1)
    source = ((rp >> 3) & 7) * 32 + (rp >> 7) * 16 + (rp & 7) * 2 + ((rp >> 6) & 1)
    s.perm[...] = jnp.where(cp_ == source, 1.0, 0.0).astype(BF)

    own_pic.wait()
    if "start1" in OPT:
        mp_wait(1, par_src, par_dst)
        return
    for i in range(3):
        def permute(j, i=i):
            v = dot(s.perm[...], s.stage[i * 256 : (i + 1) * 256, col(j, 256)]).astype(BF)
            for pl_ in range(4):
                s.picT[pl_ * Q + i * 64 : pl_ * Q + i * 64 + 64, col(j, 256)] = v[pl_ * 64 : pl_ * 64 + 64]

        loop(4, permute)

    tick()
    mp_wait(1, par_src, par_dst)
    for n, r in ROW.items():
        if n in NORM512:
            for k in range(2):
                row = NORM512[n] * 2 + k
                for j in range(4):
                    s.gv5[row : row + 1, j * 128 : j * 128 + 128] = s.PR[j, r + k : r + k + 1, :]
        elif n in NORM2048 or n in ("excite", "gating"):
            first_row = NORM2048[n] * 2 if n in NORM2048 else (6 if n == "excite" else 7)
            for k in range(2 if n in NORM2048 else 1):
                for j in range(4):
                    for h in range(4):
                        b = (j * 4 + h) * 128
                        s.gv20[first_row + k : first_row + k + 1, b : b + 128] = s.PR[j, r + k * 4 + h : r + k * 4 + h + 1, :]
    tick()

    def put(e, row, columns, value):
        g["X_" + e][d, row : row + 1, columns] = value

    def colsum(v):
        return jnp.sum(v, axis=0, keepdims=True)

    def norm_vectors(nv, index, total, square, count, gv, grow):
        mean = total / count
        rstd = lax.rsqrt(square / count - mean * mean + eps_norm)
        a = gv[grow : grow + 1, :] * rstd
        nv[index, 0:1, :] = a
        nv[index, 1:2, :] = gv[grow + 1 : grow + 2, :] - mean * a
        nv[index, 2:3, :] = mean
        nv[index, 3:4, :] = rstd

    def norm_back_vectors(nv, index, gain_grad, shift_grad, count):
        a, mean, rstd = nv[index, 0:1, :], nv[index, 2:3, :], nv[index, 3:4, :]
        w = a * rstd * gain_grad / count
        nv[index, 4:5, :] = a * shift_grad / count - mean * w
        nv[index, 5:6, :] = w

    def activate(raw, index, out):
        for j in range(4):
            b = slice(j * 128, j * 128 + 128)
            pre = raw[:, b] * s.nv5[index, 0:1, b] + s.nv5[index, 1:2, b]
            out[:, b] = (pre * sigmoid(pre) * s.redm[...]).astype(BF)

    def sums_512(e, columns, value, mask, row=0):
        vm = value * mask
        put(e, row, columns, colsum(vm))
        put(e, row + 1, columns, colsum(vm * value))

    def sums_wide(e, columns, value, isum, row):
        total = 0.0
        square = 0.0
        for i in range(3):
            v = value[i * 64 : i * 64 + 64]
            vm = v * lanes(s.redm[i * 64 : i * 64 + 64, :], v.shape[1] // 128)
            si = colsum(vm)
            if isum is not None:
                isum[i : i + 1, columns] = si
            total = total + si
            square = square + colsum(vm * v)
        put(e, row, columns, total)
        put(e, row + 1, columns, square)

    if "compute" in OPT:
        for n in NAMES:
            need(n)
        for n in NAMES:
            ag_drain(n)
        for n in ["B", "V", "T", "R", "A", "X", "P", "S", "E"]:
            for i in range(len(PIECES[n])):
                begin(n, [i])
                pump()
        while active or waiting:
            pump()
        return
    need("E")

    def entry_step(n):
        b = col(n, 256)
        v = dot(s.picT[...], s.WE[:, :, :, b].reshape(1024, 256))
        total = 0.0
        square = 0.0
        for k in range(4):
            vk = v[k * Q : k * Q + Q]
            s.e_raw[:, pl.ds(pl.multiple_of(k * 512 + n * 256, 256), 256)] = vk
            vm = vk * lanes(s.insm[k * Q : k * Q + Q, :], 2)
            total = total + colsum(vm)
            square = square + colsum(vm * vk)
        put("entry", 0, b, total)
        put("entry", 1, b, square)

    loop(2, entry_step)
    put("entry", 2, slice(0, 512), lanes(colsum(s.insm[...]), 4))
    put("entry", 3, slice(0, 512), lanes(colsum(s.redm[...]), 4))
    send_stats("entry")
    mark("a")

    need("P")

    def project_step(n):
        b = col(n, 256)
        v = dot(s.picT[0:Q, :], s.WP[:, :, :, b].reshape(1024, 256))
        s.j_raw[:, b] = v
        sums_wide("xp", b, v, None, 2)

    loop(8, project_step)
    mark("b")
    tot = get_stats("entry")
    s.cnt[0:2, :] = tot[2:4]
    norm_vectors(s.nv5, 0, tot[0:1], tot[1:2], tot[2:3], s.gv5, 0)

    def entry_act_step(j):
        pcol = col(lax.rem(j, 4), 128)
        mask = s.insm[pl.ds(pl.multiple_of((j // 4) * Q, Q), Q), :]
        pre = s.e_raw[:, col(j, 128)] * s.nv5[0, 0:1, pcol] + s.nv5[0, 1:2, pcol]
        s.act_e[:, col(j, 128)] = (pre * sigmoid(pre) * mask).astype(BF)

    loop(16, entry_act_step, 2)
    mark("c")
    for a in range(3):
        for b in range(3):
            t = a * 3 + b
            plane = (2 if a != 1 else 0) + (1 if b != 1 else 0)
            which = (0 if a == 0 else 1) * 3 + (0 if b == 0 else 1)
            v = s.act_e[:, plane * 512 : plane * 512 + 512]
            if which != 4:
                v = dot(s.shift[which], v).astype(BF)
            s.taps1[:, t * 512 : t * 512 + 512] = v

    mark("d")

    def conv3(taps, w, raw, e):
        def step(n):
            b = col(n, 256)
            v = dot(taps[:, 0:512], w[:, :, 0:64, b].reshape(512, 256))
            for t in range(1, 9):
                v = v + dot(taps[:, t * 512 : t * 512 + 512], w[:, :, t * 64 : t * 64 + 64, b].reshape(512, 256))
            raw[:, b] = v
            sums_512(e, b, v, lanes(s.redm[...], 2))

        loop(2, step)

    need("S")
    conv3(s.taps1, s.WS, s.s_raw, "stride")
    send_stats("stride")
    for t in mp_copies(0, cot_src, cot_dst):
        t.start()
    own_cot = pltpu.make_async_copy(cot_src(m), cot_dst(m), s.loc.at[COUNT + 1])
    own_cot.start()
    mark("e")
    need("X")
    tot = get_stats("stride")
    count5 = s.cnt[1:2, :]
    norm_vectors(s.nv5, 1, tot[0:1], tot[1:2], count5, s.gv5, 2)
    activate(s.s_raw, 1, s.act_s)
    mark("f")

    for n in ("isum1", "isum2", "G0", "G1"):
        g[n][...] = jnp.zeros((8, WIDE), F32)

    def widening(act, w, raw, e, isum):
        def step(k):
            b = col(k, 256)
            v = dot(act[...], w[k // 2, lax.rem(k, 2)])
            raw[:, b] = v
            sums_wide(e, b, v, isum, 0)

        loop(8, step)

    widening(s.act_s, s.WX, s.x_raw, "xp", s.isum1)
    send_stats("xp")
    mark("g")
    need("A")
    count20 = lanes(s.cnt[1:2, :], 4)
    tot = get_stats("xp")
    norm_vectors(s.nv20, 0, tot[0:1], tot[1:2], count20, s.gv20, 0)
    norm_vectors(s.nv20, 1, tot[2:3], tot[3:4], count20, s.gv20, 2)

    def squeeze_excite(index, isum, w, bias, gate_row, pool, inner, scale):
        pooled = (s.nv20[index, 0:1, :] * isum[...] / lanes(s.pix[...], 16) + s.nv20[index, 1:2, :]) * lanes(real, 16)
        pool[...] = pooled
        pre = exact(dot_cols, pooled, w[:, :, 0:16, :].reshape(128, WIDE)) + bias
        inner[...] = pre
        gate = exact(dot, pre * sigmoid(pre), w[:, :, 16:32, :].reshape(128, WIDE)) + s.gv20[gate_row : gate_row + 1, :]
        scale[...] = sigmoid(gate)

    squeeze_excite(0, s.isum1, s.WA, s.PR[0, 40:41, :], 6, s.pool1, s.inner1, s.scale1)
    mark("h")

    def first_sum(j, i):
        b, rows = col(j, 128), slice(i * 64, i * 64 + 64)
        pre = s.x_raw[rows, b] * s.nv20[0, 0:1, b] + s.nv20[0, 1:2, b]
        return pre * s.scale1[i : i + 1, b] + (s.j_raw[rows, b] * s.nv20[1, 0:1, b] + s.nv20[1, 1:2, b])

    def first_step(j):
        for i in range(3):
            rows = slice(i * 64, i * 64 + 64)
            v = first_sum(j, i)
            s.first[rows, col(j, 128)] = (v * sigmoid(v) * s.redm[rows, :]).astype(BF)

    loop(16, first_step, 2)
    mark("i")

    need("R")

    def reduce_step(n):
        b = col(n, 256)
        v = dot(s.first[...], s.WR[:, :, :, b].reshape(WIDE, 256))
        s.r_raw[:, b] = v
        sums_512("reduce", b, v, lanes(s.redm[...], 2))

    loop(2, reduce_step)
    send_stats("reduce")
    mark("j")
    tot = get_stats("reduce")
    norm_vectors(s.nv5, 2, tot[0:1], tot[1:2], count5, s.gv5, 4)
    activate(s.r_raw, 2, s.act_p)
    for t in range(9):
        v = s.act_p[...]
        if t != 4:
            v = dot(s.shift[t], v).astype(BF)
        s.taps2[:, t * 512 : t * 512 + 512] = v
    mark("k")
    need("T")
    conv3(s.taps2, s.WT, s.p_raw, "spatial")
    send_stats("spatial")
    mark("l")
    need("V")
    tot = get_stats("spatial")
    norm_vectors(s.nv5, 3, tot[0:1], tot[1:2], count5, s.gv5, 6)
    activate(s.p_raw, 3, s.act_p)
    mark("m")
    widening(s.act_p, s.WV, s.w_raw, "widen", s.isum2)
    send_stats("widen")
    need("B")
    own_cot.wait()
    mp_wait(0, cot_src, cot_dst)
    tot = get_stats("widen")
    norm_vectors(s.nv20, 2, tot[0:1], tot[1:2], count20, s.gv20, 4)
    squeeze_excite(2, s.isum2, s.WB, s.PR[0, 41:42, :], 7, s.pool2, s.inner2, s.scale2)

    def result_step(j):
        b = col(j, 128)
        for i in range(3):
            rows = slice(i * 64, i * 64 + 64)
            raw = s.w_raw[rows, b]
            pre = raw * s.nv20[2, 0:1, b] + s.nv20[2, 1:2, b]
            v = pre * s.scale2[i : i + 1, b] + s.first[rows, b].astype(F32)
            sg = sigmoid(v)
            mask = s.redm[rows, :]
            s.g2[rows, b] = (v * sg * mask).astype(BF)
            grad = s.cotb[rows, b].astype(F32) * mask * (sg * (1.0 + v * (1.0 - sg)))
            s.sg[rows, b] = grad
            s.G0[i : i + 1, b] = colsum(grad)
            s.G1[i : i + 1, b] = colsum(grad * ((raw - s.nv20[2, 2:3, b]) * s.nv20[2, 3:4, b]))

    loop(16, result_step, 2)
    for t in mp_copies(2, res_src, res_dst):
        t.start()
    own_res = pltpu.make_async_copy(res_src(m), res_dst(m), s.loc.at[COUNT + 2])
    own_res.start()

    if "fwd" in OPT:
        for n in NAMES:
            ag_drain(n)
        own_res.wait()
        mp_wait(2, res_src, res_dst)
        return
    def keep512(n, k, v):
        for j in range(4):
            s.FS[j, ROW[n] + k : ROW[n] + k + 1, :] = v[:, j * 128 : j * 128 + 128]

    def keep2048(row, v):
        for j in range(4):
            for h in range(4):
                b = (j * 4 + h) * 128
                s.FS[j, row + h : row + h + 1, :] = v[:, b : b + 128]

    def excite_back(index, isum, w, inner, scale):
        scl = scale[...]
        gate_grad = (s.gv20[index * 2 : index * 2 + 1, :] * s.G1[...] + s.gv20[index * 2 + 1 : index * 2 + 2, :] * s.G0[...]) * (
            scl * (1.0 - scl)
        )
        s.gate[...] = gate_grad
        pre = inner[...]
        sg = sigmoid(pre)
        ing = exact(dot_cols, gate_grad, w[:, :, 16:32, :].reshape(128, WIDE)) * (sg * (1.0 + pre * (1.0 - sg)))
        s.ing[...] = ing
        pix = lanes(s.pix[...], 16)
        pg = exact(dot, ing, w[:, :, 0:16, :].reshape(128, WIDE)) / pix
        s.pg[...] = pg
        spread = (isum[...] - s.nv20[index, 2:3, :] * pix) * s.nv20[index, 3:4, :]
        return (colsum(scl * s.G1[...] + pg * spread), colsum(scl * s.G0[...] + pg * pix), colsum(gate_grad), colsum(ing))

    def excite_weights(n, pool, inner):
        pre = inner[...]
        hidden = pre * sigmoid(pre)
        w = g["W" + n]

        def step(j):
            b = col(j, 512)
            w[:, :, 0:16, b] = outer(s.ing[...], pool[:, b]).astype(BF).reshape(4, 2, 16, 512)
            w[:, :, 16:32, b] = outer(hidden, s.gate[:, b]).astype(BF).reshape(4, 2, 16, 512)

        loop(4, step)

    def wide_grad(index, raw, out, scale):
        def step(j):
            b = col(j, 128)
            for i in range(3):
                rows = slice(i * 64, i * 64 + 64)
                grad, mask = s.sg[rows, b], s.redm[rows, :]
                if scale is not None:
                    grad = grad * scale[i : i + 1, b] + mask * s.pg[i : i + 1, b]
                v = s.nv20[index, 0:1, b] * grad - mask * (s.nv20[index, 4:5, b] + s.nv20[index, 5:6, b] * raw[rows, b])
                out[rows, b] = v.astype(BF)

        loop(16, step, 2)

    def back_sums(e, index, b, grad, raw, mask):
        out = []
        pre = raw * s.nv5[index, 0:1, b] + s.nv5[index, 1:2, b]
        sg = sigmoid(pre)
        grad = grad * mask * (sg * (1.0 + pre * (1.0 - sg)))
        put(e, 0, b, colsum(grad * ((raw - s.nv5[index, 2:3, b]) * s.nv5[index, 3:4, b])))
        put(e, 1, b, colsum(grad))
        return grad

    def narrow_back(e, index, acc, raw):
        for j in range(4):
            b = slice(j * 128, j * 128 + 128)
            s.gq[:, b] = back_sums(e, index, b, acc[:, b], raw[:, b], s.redm[...])

    def narrow_grad(index, raw):
        for j in range(4):
            b = slice(j * 128, j * 128 + 128)
            v = s.nv5[index, 0:1, b] * s.gq[:, b] - s.redm[...] * (s.nv5[index, 4:5, b] + s.nv5[index, 5:6, b] * raw[:, b])
            s.gs[:, b] = v.astype(BF)

    def narrow_stats(e, n):
        tot = get_stats(e)
        keep512(n, 0, tot[0:1])
        keep512(n, 1, tot[1:2])
        norm_back_vectors(s.nv5, NORM512[n], tot[0:1], tot[1:2], s.cnt[0:1, :] if n == "entry" else count5)

    def widening_back(grads, w):
        def step(n):
            rows = col(n, 256)
            v = dot_cols(grads[:, 0:256], w[0, 0, rows, :])
            for k in range(1, 8):
                v = v + dot_cols(grads[:, k * 256 : k * 256 + 256], w[k // 2, k % 2, rows, :])
            s.acc[:, rows] = v

        loop(2, step)

    def widening_weights(n, act, grads):
        ag_drain(n)
        w = g["W" + n]

        def step(k):
            w[k // 2, lax.rem(k, 2)] = dot_rows(act[...], grads[:, col(k, 256)]).astype(BF)

        loop(8, step)
        begin(n)

    def conv3_weights(n, taps):
        ag_drain(n)
        w = g["W" + n]

        def step(t):
            for h in range(2):
                b = slice(h * 256, h * 256 + 256)
                v = dot_rows(taps[:, col(t, 512)], s.gs[:, b]).astype(BF)
                w[:, :, col(t, 64), b] = v.reshape(4, 2, 64, 256)

        loop(9, step)
        begin(n)

    sums = excite_back(2, s.isum2, s.WB, s.inner2, s.scale2)
    for k in range(3):
        put("widen_b", k, slice(0, WIDE), sums[k])
    put("widen_b", 3, slice(0, WIDE), lanes(sums[3], 16))
    send_stats("widen_b")
    ag_drain("B")
    excite_weights("B", s.pool2, s.inner2)
    begin("B")
    tot = get_stats("widen_b")
    pumps("A")
    keep2048(ROW["widen"], tot[0:1])
    keep2048(ROW["widen"] + 4, tot[1:2])
    keep2048(ROW["gating"], tot[2:3])
    for j in range(4):
        s.FS[j, ROW["shrink"] : ROW["shrink"] + 1, :] = tot[3:4, 0:128]
    norm_back_vectors(s.nv20, 2, tot[0:1], tot[1:2], count20)
    wide_grad(2, s.w_raw, s.g1, s.scale2)
    pumps("B")
    widening_back(s.g1, s.WV)
    narrow_back("spatial_b", 3, s.acc, s.p_raw)
    send_stats("spatial_b")
    pumps("C")
    widening_weights("V", s.act_p, s.g1)
    pumps("D")
    narrow_stats("spatial_b", "spatial")
    narrow_grad(3, s.p_raw)
    pumps("E")
    s.acc[...] = jnp.zeros((Q, 512), F32)

    def spatial_back(t):
        v = dot(s.shift[8 - t], s.gs[...]).astype(BF)
        s.acc[...] += dot_cols(v, s.WT[:, :, col(t, 64), :].reshape(512, 512))

    loop(9, spatial_back)
    pumps("F")
    narrow_back("reduce_b", 2, s.acc, s.r_raw)
    send_stats("reduce_b")
    pumps("G")
    conv3_weights("T", s.taps2)
    pumps("H")
    narrow_stats("reduce_b", "reduce")
    narrow_grad(2, s.r_raw)
    pumps("I")

    def reduce_back(k):
        v = dot_cols(s.gs[...], s.WR[k // 2, lax.rem(k, 2)])
        for h in range(2):
            j = k * 2 + h
            b = col(j, 128)
            project_sum = 0.0
            shift_sum = 0.0
            for i in range(3):
                rows = slice(i * 64, i * 64 + 64)
                fs = first_sum(j, i)
                sg = sigmoid(fs)
                grad = (v[rows, h * 128 : h * 128 + 128] + s.sg[rows, b]) * s.redm[rows, :] * (sg * (1.0 + fs * (1.0 - sg)))
                s.sg[rows, b] = grad
                total = colsum(grad)
                s.G0[i : i + 1, b] = total
                s.G1[i : i + 1, b] = colsum(grad * ((s.x_raw[rows, b] - s.nv20[0, 2:3, b]) * s.nv20[0, 3:4, b]))
                shift_sum = shift_sum + total
                project_sum = project_sum + colsum(grad * ((s.j_raw[rows, b] - s.nv20[1, 2:3, b]) * s.nv20[1, 3:4, b]))
            put("xp_b", 2, b, project_sum)
            put("xp_b", 3, b, shift_sum)

    loop(8, reduce_back)
    pumps("J")
    sums = excite_back(0, s.isum1, s.WA, s.inner1, s.scale1)
    put("xp_b", 0, slice(0, WIDE), sums[0])
    put("xp_b", 1, slice(0, WIDE), sums[1])
    send_stats("xp_b")
    put("bias_b", 0, slice(0, WIDE), sums[2])
    put("bias_b", 1, slice(0, WIDE), lanes(sums[3], 16))
    send_stats("bias_b")
    pumps("K")
    ag_drain("R")

    def reduce_weights(k):
        s.WR[k // 2, lax.rem(k, 2)] = dot_rows(s.first[:, col(k, 256)], s.gs[...]).astype(BF)

    loop(8, reduce_weights)
    begin("R")
    pumps("L")
    ag_drain("A")
    excite_weights("A", s.pool1, s.inner1)
    begin("A")
    pumps("M")
    tot = get_stats("xp_b")
    for k, n in enumerate(("expand", "project")):
        keep2048(ROW[n], tot[2 * k : 2 * k + 1])
        keep2048(ROW[n] + 4, tot[2 * k + 1 : 2 * k + 2])
        norm_back_vectors(s.nv20, k, tot[2 * k : 2 * k + 1], tot[2 * k + 1 : 2 * k + 2], count20)
    own_res.wait()
    mp_wait(2, res_src, res_dst)
    wide_grad(1, s.j_raw, s.g2, None)

    def project_back(zz):
        w = s.WP[zz].reshape(256, WIDE)
        s.sgrad[:, col(zz, 256)] = dot_cols(s.g2[...], w)

    loop(4, project_back)
    pumps("P")
    ag_drain("P")

    def project_weights(n):
        b = col(n, 256)
        for h in range(2):
            v = dot_rows(s.picT[0:Q, h * 512 : h * 512 + 512], s.g2[:, b]).astype(BF)
            s.WP[2 * h : 2 * h + 2, :, :, b] = v.reshape(2, 2, 128, 256)

    loop(8, project_weights)
    begin("P")
    pumps("R")
    wide_grad(0, s.x_raw, s.g1, s.scale1)
    pumps("N")
    widening_back(s.g1, s.WX)
    narrow_back("stride_b", 1, s.acc, s.s_raw)
    send_stats("stride_b")
    pumps("O")
    widening_weights("X", s.act_s, s.g1)
    pumps("Q")
    narrow_stats("stride_b", "stride")
    narrow_grad(1, s.s_raw)
    pumps("S")

    for k in range(4):
        pa, pb = k // 2, k % 2
        columns = slice(k * 512, k * 512 + 512)
        first_tap = True
        for a in (0, 2) if pa else (1,):
            for b in (0, 2) if pb else (1,):
                t = a * 3 + b
                which = (0 if a == 0 else 1) * 3 + (0 if b == 0 else 1)
                v = s.gs[...]
                if which != 4:
                    v = dot(s.shift[8 - which], v).astype(BF)
                v = dot_cols(v, s.WS[:, :, t * 64 : t * 64 + 64, :].reshape(512, 512))
                if first_tap:
                    s.w_raw[:, columns] = v
                else:
                    s.w_raw[:, columns] += v
                first_tap = False

    def entry_back(n):
        b = col(n, 128)
        gain_sum = 0.0
        shift_sum = 0.0
        for k in range(4):
            kb = pl.ds(pl.multiple_of(k * 512 + n * 128, 128), 128)
            raw = s.e_raw[:, kb]
            pre = raw * s.nv5[0, 0:1, b] + s.nv5[0, 1:2, b]
            sg = sigmoid(pre)
            grad = s.w_raw[:, kb] * s.insm[k * Q : k * Q + Q, :] * (sg * (1.0 + pre * (1.0 - sg)))
            s.w_raw[:, kb] = grad
            gain_sum = gain_sum + colsum(grad * ((raw - s.nv5[0, 2:3, b]) * s.nv5[0, 3:4, b]))
            shift_sum = shift_sum + colsum(grad)
        put("entry_b", 0, b, gain_sum)
        put("entry_b", 1, b, shift_sum)

    loop(4, entry_back)
    send_stats("entry_b")
    pumps("U")
    conv3_weights("S", s.taps1)
    pumps("V")
    narrow_stats("entry_b", "entry")

    def entry_grad(j):
        pcol = col(lax.rem(j, 4), 128)
        mask = s.insm[pl.ds(pl.multiple_of((j // 4) * Q, Q), Q), :]
        b = col(j, 128)
        v = s.nv5[0, 0:1, pcol] * s.w_raw[:, b] - mask * (s.nv5[0, 4:5, pcol] + s.nv5[0, 5:6, pcol] * s.e_raw[:, b])
        s.act_e[:, b] = v.astype(BF)

    loop(16, entry_grad, 2)
    pumps("W")
    tot = get_stats("bias_b")
    keep2048(ROW["excite"], tot[0:1])
    for j in range(4):
        s.FS[j, ROW["squeeze"] : ROW["squeeze"] + 1, :] = tot[1:2, 0:128]
        for r in range(42, SMALL, 2):
            s.FS[j, r : r + 2, :] = jnp.zeros((2, 128), F32)
    s.FR[m] = s.FS[m]
    for t in mp_copies(4, fin_src, fin_dst):
        t.start()

    def image_grad(zz):
        w = s.WE[zz].reshape(256, 512)
        for k in range(4):
            v = dot_cols(s.act_e[:, k * 512 : k * 512 + 512], w)
            if k == 0:
                v = v + s.sgrad[:, col(zz, 256)]
            s.taps1[:, pl.ds(pl.multiple_of(k * 1024 + zz * 256, 256), 256)] = v.astype(BF)

    loop(4, image_grad)
    for i in range(3):
        def unpermute(j, i=i):
            v = jnp.concatenate(
                [s.taps1[i * 64 : i * 64 + 64, pl.ds(pl.multiple_of(k * 1024 + j * 256, 256), 256)] for k in range(4)], axis=0
            )
            s.stage[i * 256 : i * 256 + 256, col(j, 256)] = dot_rows(s.perm[...], v).astype(BF)

        loop(4, unpermute)
    for t in mp_copies(3, img_src, img_dst):
        t.start()
    own_img = pltpu.make_async_copy(img_src(m), img_dst(m), s.loc.at[COUNT + 3])
    own_img.start()
    pumps("X")
    ag_drain("E")

    def entry_weights(zz):
        v = dot_rows(s.picT[0:Q, col(zz, 256)], s.act_e[:, 0:512])
        for k in range(1, 4):
            v = v + dot_rows(s.picT[k * Q : k * Q + Q, col(zz, 256)], s.act_e[:, k * 512 : k * 512 + 512])
        s.WE[zz] = v.astype(BF).reshape(2, 128, 512)

    loop(4, entry_weights)
    begin("E")
    pumps("Y")
    state["lag"] = ENDLAG
    while active or waiting:
        pump()
    mp_wait(4, fin_src, fin_dst)
    s.small[...] = ((s.FR[0] + s.FR[1]) + s.FR[2]) + s.FR[3]
    own_img.wait()
    mp_wait(3, img_src, img_dst)

def fused_shards(*arrays):
    (images, image_size, entry_weight, entry_gain, entry_shift, stride_weight, stride_gain, stride_shift, expand_weight,
     expand_gain, expand_shift, project_weight, project_gain, project_shift, squeeze_weight, squeeze_bias, excite_weight,
     excite_bias, reduce_weight, reduce_gain, reduce_shift, spatial_weight, spatial_gain, spatial_shift, widen_weight,
     widen_gain, widen_shift, shrink_weight, shrink_bias, gating_weight, gating_bias, cotangent) = arrays
    weights = {
        "E": entry_weight,
        "P": project_weight,
        "S": stride_weight.reshape(576, 128),
        "X": expand_weight,
        "R": reduce_weight,
        "T": spatial_weight.reshape(576, 128),
        "V": widen_weight,
    }
    given = dict(
        entry_gain=entry_gain, entry_shift=entry_shift, stride_gain=stride_gain, stride_shift=stride_shift,
        reduce_gain=reduce_gain, reduce_shift=reduce_shift, spatial_gain=spatial_gain, spatial_shift=spatial_shift,
        expand_gain=expand_gain, expand_shift=expand_shift, project_gain=project_gain, project_shift=project_shift,
        widen_gain=widen_gain, widen_shift=widen_shift, excite_bias=excite_bias, gating_bias=gating_bias,
        squeeze_bias=squeeze_bias, shrink_bias=shrink_bias,
    )
    small = [given[n].reshape(rows, 128) for n, _, rows in VECTORS]
    hbm, vmem = pl.BlockSpec(memory_space=pl.ANY), pl.BlockSpec(memory_space=pltpu.VMEM)
    outs = [jax.ShapeDtypeStruct((4, Q, 512), BF), jax.ShapeDtypeStruct((4, 768, 256), BF)]
    outs += [jax.ShapeDtypeStruct(CLASSES[TENSORS[n][3]], F32) for n in NAMES]
    outs += [jax.ShapeDtypeStruct((SMALL, 128), F32)]
    got = pl.pallas_call(
        body,
        out_shape=outs,
        in_specs=[hbm, pl.BlockSpec(memory_space=pltpu.SMEM), hbm] + [hbm] * (len(PLAIN) + 4 + len(VECTORS)),
        out_specs=[hbm, hbm] + [vmem] * (len(NAMES) + 1),
        scratch_shapes=list(scratch_list().values()),
        compiler_params=pltpu.CompilerParams(collective_id=0, has_side_effects=True, vmem_limit_bytes=VMEM_LIMIT),
        cost_estimate=pl.CostEstimate(flops=14_000_000_000, bytes_accessed=30_000_000, transcendentals=10_000_000),
    )(
        images.reshape(4, 768, 1024), image_size, cotangent.reshape(4, Q, 512), *[weights[n] for n in PLAIN],
        squeeze_weight.T, excite_weight, shrink_weight.T, gating_weight, *small,
    )

    def held(shape):
        return pl.BlockSpec(shape, lambda i: (0, 0))

    kinds = [held(CLASSES[TENSORS[n][3]]) for n in NAMES]
    last = [jax.ShapeDtypeStruct((4, Q, 512), BF), jax.ShapeDtypeStruct((4, 768, 256), F32)]
    last += [jax.ShapeDtypeStruct(CLASSES[TENSORS[n][3]], F32) for n in PLAIN]
    last += [jax.ShapeDtypeStruct(v, F32) for v in ((16, 512),) * 4]
    last += [jax.ShapeDtypeStruct((rows, 128), F32) for _, _, rows in VECTORS]
    blocks = [pl.BlockSpec((2, Q, 512), lambda i: (i, 0, 0)), pl.BlockSpec((2, 768, 256), lambda i: (i, 0, 0))]
    final = pl.pallas_call(
        last_body,
        grid=(2,),
        out_shape=last,
        in_specs=blocks + kinds + [held((SMALL, 128))],
        out_specs=blocks + [held(CLASSES[TENSORS[n][3]]) for n in PLAIN] + [held(v) for v in ((16, 512),) * 4]
        + [held((rows, 128)) for _, _, rows in VECTORS],
        compiler_params=pltpu.CompilerParams(vmem_limit_bytes=VMEM_LIMIT),
        cost_estimate=pl.CostEstimate(flops=1_000_000, bytes_accessed=10_000_000, transcendentals=0),
    )(*got)
    f = dict(zip(LAST_OUT, final))

    def pair(n):
        return f[n + "_gain"].reshape(-1), f[n + "_shift"].reshape(-1)

    return (
        f["f_result"].reshape(cotangent.shape),
        f["f_igrad"].reshape(4, 3, 16, 16, 256),
        f["f_E"], *pair("entry"),
        f["f_S"].reshape(stride_weight.shape), *pair("stride"),
        f["f_X"], *pair("expand"),
        f["f_P"], *pair("project"),
        f["f_sqA"].T, f["squeeze_bias"].reshape(-1), f["f_exA"], f["excite_bias"].reshape(-1),
        f["f_R"], *pair("reduce"),
        f["f_T"].reshape(spatial_weight.shape), *pair("spatial"),
        f["f_V"], *pair("widen"),
        f["f_sqB"].T, f["shrink_bias"].reshape(-1), f["f_exB"], f["gating_bias"].reshape(-1),
    )


def matmul(left, right):
    return jnp.dot(left, right, preferred_element_type=jnp.float32)


def contract_rows(left, right):
    return lax.dot_general(
        left, right, (((0,), (0,)), ((), ())), preferred_element_type=jnp.float32
    )


def contract_cols(left, right):
    return lax.dot_general(
        left, right, (((1,), (1,)), ((), ())), preferred_element_type=jnp.float32
    )


def swish_slope(value):
    sigma = jax.nn.sigmoid(value)
    return sigma * (1.0 + value * (1.0 - sigma))


def pixel_masks(sizes, side):
    half = side // 2
    height = sizes[:, 0]
    breadth = sizes[:, 1]
    places = jnp.arange(side, dtype=jnp.int32)
    inside = (
        (places[None, :, None] < height[:, None, None])
        & (places[None, None, :] < breadth[:, None, None])
    ).astype(jnp.float32)
    halves = jnp.arange(half, dtype=jnp.int32)
    reduced = (
        (halves[None, :, None] < ((height + 1) // 2)[:, None, None])
        & (halves[None, None, :] < ((breadth + 1) // 2)[:, None, None])
    ).astype(jnp.float32)
    return (inside, reduced)


def spatial_taps(field, stride):
    count, side, channels = (field.shape[0], field.shape[1], field.shape[3])
    reach = stride * (side // stride - 1) + 1
    padded = jnp.pad(field, ((0, 0), (1, 1), (1, 1), (0, 0)))
    pieces = []
    for row in range(3):
        for column in range(3):
            pieces.append(
                lax.slice(
                    padded,
                    (0, row, column, 0),
                    (count, row + reach, column + reach, channels),
                    (1, stride, stride, 1),
                )
            )
    return jnp.concatenate(pieces, axis=3)


def untap(grads, stride, side):
    count, out_side = (grads.shape[0], grads.shape[1])
    channels = grads.shape[3] // 9
    reach = stride * (out_side - 1) + 1
    total = jnp.zeros((count, side + 2, side + 2, channels), jnp.float32)
    for row in range(3):
        for column in range(3):
            first = (row * 3 + column) * channels
            piece = grads[:, :, :, first : first + channels]
            total = total + lax.pad(
                piece,
                jnp.float32(0.0),
                (
                    (0, 0, 0),
                    (row, side + 2 - row - reach, stride - 1),
                    (column, side + 2 - column - reach, stride - 1),
                    (0, 0, 0),
                ),
            )
    return total[:, 1 : side + 1, 1 : side + 1, :]


def batch_statistics(fields, mask):
    weights = mask[..., None]
    terms = []
    for field in fields:
        terms.append(jnp.sum(field * weights, axis=(0, 1, 2)))
        terms.append(jnp.sum(field * field * weights, axis=(0, 1, 2)))
    packed, total_vector = lax.psum((jnp.concatenate(terms), jnp.sum(mask).reshape(1)), "dp")
    total = total_vector[0]
    result = []
    offset = 0
    for field in fields:
        breadth = field.shape[3]
        mean = packed[offset : offset + breadth] / total
        second = packed[offset + breadth : offset + 2 * breadth] / total
        result.append((mean, lax.rsqrt(second - mean * mean + eps_norm)))
        offset = offset + 2 * breadth
    return (result, total)


def standardize(raw, statistics, gain, shift):
    mean, scale = statistics
    normed = (raw - mean) * scale
    return (normed, normed * gain + shift)


def batch_backward(grads, normeds, scales, gains, mask, total, extras):
    terms = []
    for grad, normed in zip(grads, normeds):
        terms.append(jnp.sum(grad * normed, axis=(0, 1, 2)))
        terms.append(jnp.sum(grad, axis=(0, 1, 2)))
    for extra in extras:
        terms.append(extra)
    packed = lax.psum(jnp.concatenate(terms), "dp")
    results = []
    pairs = []
    offset = 0
    for grad, normed, scale, gain in zip(grads, normeds, scales, gains):
        breadth = grad.shape[3]
        gain_grad = packed[offset : offset + breadth]
        shift_grad = packed[offset + breadth : offset + 2 * breadth]
        offset = offset + 2 * breadth
        results.append(
            scale * gain * (grad - mask[..., None] * (shift_grad + normed * gain_grad) / total)
        )
        pairs.append((gain_grad, shift_grad))
    rest = []
    for extra in extras:
        rest.append(packed[offset : offset + extra.shape[0]])
        offset = offset + extra.shape[0]
    return (results, pairs, rest)


def excite_forward(field, mask, pixels, squeeze_full, squeeze_bias, excite_full, excite_bias):
    pooled = jnp.sum(field * mask[..., None], axis=(1, 2)) / pixels[:, None]
    inner_pre = (
        jnp.dot(pooled, squeeze_full.astype(jnp.float32), precision=highest) + squeeze_bias
    )
    hidden = jax.nn.silu(inner_pre)
    scale = jax.nn.sigmoid(
        jnp.dot(hidden, excite_full.astype(jnp.float32), precision=highest) + excite_bias
    )
    return (pooled, inner_pre, hidden, scale)


def excite_backward(grad_branch, field, mask, pixels, saved, squeeze_full, excite_full):
    pooled, inner_pre, hidden, scale = saved
    grad_scale = jnp.sum(grad_branch * field, axis=(1, 2))
    grad_gate = grad_scale * scale * (1.0 - scale)
    excite_grad = jnp.dot(hidden.T, grad_gate, precision=highest)
    grad_hidden = jnp.dot(grad_gate, excite_full.astype(jnp.float32).T, precision=highest)
    grad_inner = grad_hidden * swish_slope(inner_pre)
    squeeze_grad = jnp.dot(pooled.T, grad_inner, precision=highest)
    grad_pooled = jnp.dot(grad_inner, squeeze_full.astype(jnp.float32).T, precision=highest)
    grad_field = (
        grad_branch * scale[:, None, None, :]
        + grad_pooled[:, None, None, :] * mask[..., None] / pixels[:, None, None, None]
    )
    return (
        grad_field,
        squeeze_grad,
        excite_grad,
        jnp.sum(grad_inner, axis=0),
        jnp.sum(grad_gate, axis=0),
    )


def whole_vector(value):
    return lax.all_gather(value, "mp", axis=0, tiled=True)


def whole_matrix(value, dp_axis, mp_axis):
    value = lax.all_gather(value, "dp", axis=dp_axis, tiled=True)
    return lax.all_gather(value, "mp", axis=mp_axis, tiled=True)


def own_part(value, dp_axis, mp_axis):
    value = lax.psum_scatter(
        value.astype(jnp.bfloat16), "mp", scatter_dimension=mp_axis, tiled=True
    )
    return lax.psum_scatter(value, "dp", scatter_dimension=dp_axis, tiled=True).astype(
        jnp.float32
    )


def plain_shards(
    images,
    image_size,
    entry_weight,
    entry_gain,
    entry_shift,
    stride_weight,
    stride_gain,
    stride_shift,
    expand_weight,
    expand_gain,
    expand_shift,
    project_weight,
    project_gain,
    project_shift,
    squeeze_weight,
    squeeze_bias,
    excite_weight,
    excite_bias,
    reduce_weight,
    reduce_gain,
    reduce_shift,
    spatial_weight,
    spatial_gain,
    spatial_shift,
    widen_weight,
    widen_gain,
    widen_shift,
    shrink_weight,
    shrink_bias,
    gating_weight,
    gating_bias,
    cotangent,
):
    place = lax.axis_index("mp")
    count, side = (images.shape[1], images.shape[2])
    half = side // 2
    channels_in = images.shape[4]
    entry_full = whole_matrix(entry_weight, 0, 1)
    stride_full = whole_matrix(stride_weight, 2, 3)
    expand_full = whole_matrix(expand_weight, 1, 0)
    project_full = whole_matrix(project_weight, 0, 1)
    squeeze_full = whole_matrix(squeeze_weight, 1, 0)
    excite_full = whole_matrix(excite_weight, 0, 1)
    reduce_full = whole_matrix(reduce_weight, 0, 1)
    spatial_full = whole_matrix(spatial_weight, 2, 3)
    widen_full = whole_matrix(widen_weight, 1, 0)
    shrink_full = whole_matrix(shrink_weight, 1, 0)
    gating_full = whole_matrix(gating_weight, 0, 1)
    entry_gain, entry_shift = whole_vector(entry_gain), whole_vector(entry_shift)
    stride_gain, stride_shift = whole_vector(stride_gain), whole_vector(stride_shift)
    expand_gain, expand_shift = whole_vector(expand_gain), whole_vector(expand_shift)
    project_gain, project_shift = whole_vector(project_gain), whole_vector(project_shift)
    reduce_gain, reduce_shift = whole_vector(reduce_gain), whole_vector(reduce_shift)
    spatial_gain, spatial_shift = whole_vector(spatial_gain), whole_vector(spatial_shift)
    widen_gain, widen_shift = whole_vector(widen_gain), whole_vector(widen_shift)
    excite_bias, gating_bias = whole_vector(excite_bias), whole_vector(gating_bias)
    seed_grad = lax.all_to_all(cotangent, "mp", split_axis=0, concat_axis=4, tiled=True)[0]
    picture = lax.dynamic_index_in_dim(images, place, 0, keepdims=False)
    sizes = lax.dynamic_index_in_dim(image_size, place, 0, keepdims=False)
    inside, reduced = pixel_masks(sizes, side)
    pixels = jnp.sum(reduced, axis=(1, 2))
    reduced_mask = reduced[..., None]
    entry_raw = matmul(picture.reshape(-1, channels_in), entry_full).reshape(
        count, side, side, -1
    )
    stats, inside_total = batch_statistics([entry_raw], inside)
    entry_stats = stats[0]
    entry_normed, entry_pre = standardize(entry_raw, entry_stats, entry_gain, entry_shift)
    entry_act = (jax.nn.silu(entry_pre) * inside[..., None]).astype(jnp.bfloat16)
    entry_wide = entry_act
    bottleneck = entry_wide.shape[3]
    stride_taps = spatial_taps(entry_wide, 2).reshape(-1, 9 * bottleneck)
    stride_raw = matmul(stride_taps, stride_full.reshape(9 * bottleneck, -1)).reshape(
        count, half, half, -1
    )
    stats, reduced_total = batch_statistics([stride_raw], reduced)
    stride_stats = stats[0]
    stride_normed, stride_pre = standardize(stride_raw, stride_stats, stride_gain, stride_shift)
    stride_act = (jax.nn.silu(stride_pre) * reduced_mask).astype(jnp.bfloat16)
    local_bottleneck = stride_act.shape[3]
    stride_flat = stride_act.reshape(-1, local_bottleneck)
    expand_raw = matmul(stride_flat, expand_full).reshape(count, half, half, -1)
    strided_flat = picture[:, ::2, ::2, :].reshape(-1, channels_in)
    project_raw = matmul(strided_flat, project_full).reshape(count, half, half, -1)
    stats, reduced_total = batch_statistics([expand_raw, project_raw], reduced)
    expand_stats, project_stats = (stats[0], stats[1])
    expand_normed, expand_pre = standardize(expand_raw, expand_stats, expand_gain, expand_shift)
    project_normed, project_pre = standardize(
        project_raw, project_stats, project_gain, project_shift
    )
    first_saved = excite_forward(
        expand_pre, reduced, pixels, squeeze_full, squeeze_bias, excite_full, excite_bias
    )
    first_sum = expand_pre * first_saved[3][:, None, None, :] + project_pre
    first_out = (jax.nn.silu(first_sum) * reduced_mask).astype(jnp.bfloat16)
    block_wide = first_out
    block_flat = block_wide.reshape(-1, block_wide.shape[3])
    reduce_raw = matmul(block_flat, reduce_full).reshape(count, half, half, -1)
    stats, reduced_total = batch_statistics([reduce_raw], reduced)
    reduce_stats = stats[0]
    reduce_normed, reduce_pre = standardize(reduce_raw, reduce_stats, reduce_gain, reduce_shift)
    reduce_act = (jax.nn.silu(reduce_pre) * reduced_mask).astype(jnp.bfloat16)
    reduce_wide = reduce_act
    second_taps = spatial_taps(reduce_wide, 1).reshape(-1, 9 * bottleneck)
    spatial_raw = matmul(second_taps, spatial_full.reshape(9 * bottleneck, -1)).reshape(
        count, half, half, -1
    )
    stats, reduced_total = batch_statistics([spatial_raw], reduced)
    spatial_stats = stats[0]
    spatial_normed, spatial_pre = standardize(
        spatial_raw, spatial_stats, spatial_gain, spatial_shift
    )
    spatial_act = (jax.nn.silu(spatial_pre) * reduced_mask).astype(jnp.bfloat16)
    spatial_flat = spatial_act.reshape(-1, local_bottleneck)
    widen_raw = matmul(spatial_flat, widen_full).reshape(count, half, half, -1)
    stats, reduced_total = batch_statistics([widen_raw], reduced)
    widen_stats = stats[0]
    widen_normed, widen_pre = standardize(widen_raw, widen_stats, widen_gain, widen_shift)
    second_saved = excite_forward(
        widen_pre, reduced, pixels, shrink_full, shrink_bias, gating_full, gating_bias
    )
    second_sum = widen_pre * second_saved[3][:, None, None, :] + first_out.astype(jnp.float32)
    output = (jax.nn.silu(second_sum) * reduced_mask).astype(jnp.bfloat16)
    second_grad = seed_grad.astype(jnp.float32) * reduced_mask * swish_slope(second_sum)
    widen_grad, shrink_grad, gating_grad, shrink_bias_grad, gating_bias_grad = excite_backward(
        second_grad, widen_pre, reduced, pixels, second_saved, shrink_full, gating_full
    )
    grads, widen_pair, extras = batch_backward(
        [widen_grad],
        [widen_normed],
        [widen_stats[1]],
        [widen_gain],
        reduced,
        reduced_total,
        (shrink_bias_grad, gating_bias_grad),
    )
    widen_pair = widen_pair[0]
    shrink_bias_total, gating_bias_total = (extras[0], extras[1])
    widen_local = grads[0].astype(jnp.bfloat16)
    widen_low = widen_local
    widen_flat = widen_low.reshape(-1, widen_low.shape[3])
    widen_weight_grad = contract_rows(spatial_flat, widen_flat)
    spatial_act_grad = contract_cols(widen_flat, widen_full).reshape(count, half, half, -1)
    spatial_grad = spatial_act_grad * reduced_mask * swish_slope(spatial_pre)
    grads, spatial_pair, extras = batch_backward(
        [spatial_grad],
        [spatial_normed],
        [spatial_stats[1]],
        [spatial_gain],
        reduced,
        reduced_total,
        (),
    )
    spatial_pair = spatial_pair[0]
    spatial_low = grads[0].astype(jnp.bfloat16).reshape(-1, local_bottleneck)
    spatial_weight_grad = contract_rows(second_taps, spatial_low).reshape(
        3, 3, bottleneck, local_bottleneck
    )
    second_tap_grad = contract_cols(spatial_low, spatial_full.reshape(9 * bottleneck, -1))
    reduce_act_grad = untap(second_tap_grad.reshape(count, half, half, -1), 1, half)
    reduce_grad = reduce_act_grad * reduced_mask * swish_slope(reduce_pre)
    grads, reduce_pair, extras = batch_backward(
        [reduce_grad],
        [reduce_normed],
        [reduce_stats[1]],
        [reduce_gain],
        reduced,
        reduced_total,
        (),
    )
    reduce_pair = reduce_pair[0]
    reduce_low = grads[0].astype(jnp.bfloat16).reshape(-1, local_bottleneck)
    reduce_weight_grad = contract_rows(block_flat, reduce_low)
    first_partial = contract_cols(reduce_low, reduce_full).reshape(count, half, half, -1)
    first_out_grad = first_partial + second_grad
    first_grad = first_out_grad * reduced_mask * swish_slope(first_sum)
    expand_grad, squeeze_grad, excite_grad, squeeze_bias_grad, excite_bias_grad = (
        excite_backward(
            first_grad, expand_pre, reduced, pixels, first_saved, squeeze_full, excite_full
        )
    )
    grads, pairs, extras = batch_backward(
        [expand_grad, first_grad],
        [expand_normed, project_normed],
        [expand_stats[1], project_stats[1]],
        [expand_gain, project_gain],
        reduced,
        reduced_total,
        (squeeze_bias_grad, excite_bias_grad),
    )
    expand_pair, project_pair = (pairs[0], pairs[1])
    squeeze_bias_total, excite_bias_total = (extras[0], extras[1])
    expand_local = grads[0].astype(jnp.bfloat16)
    expand_low = expand_local
    expand_flat = expand_low.reshape(-1, expand_low.shape[3])
    expand_weight_grad = contract_rows(stride_flat, expand_flat)
    stride_act_grad = contract_cols(expand_flat, expand_full).reshape(count, half, half, -1)
    project_low = grads[1].astype(jnp.bfloat16).reshape(-1, grads[1].shape[3])
    project_weight_grad = contract_rows(strided_flat, project_low)
    strided_grad = contract_cols(project_low, project_full).reshape(
        count, half, half, channels_in
    )
    stride_grad = stride_act_grad * reduced_mask * swish_slope(stride_pre)
    grads, stride_pair, extras = batch_backward(
        [stride_grad],
        [stride_normed],
        [stride_stats[1]],
        [stride_gain],
        reduced,
        reduced_total,
        (),
    )
    stride_pair = stride_pair[0]
    stride_low = grads[0].astype(jnp.bfloat16).reshape(-1, local_bottleneck)
    stride_weight_grad = contract_rows(stride_taps, stride_low).reshape(
        3, 3, bottleneck, local_bottleneck
    )
    first_tap_grad = contract_cols(stride_low, stride_full.reshape(9 * bottleneck, -1))
    entry_act_grad = untap(first_tap_grad.reshape(count, half, half, -1), 2, side)
    entry_grad = entry_act_grad * inside[..., None] * swish_slope(entry_pre)
    grads, entry_pair, extras = batch_backward(
        [entry_grad], [entry_normed], [entry_stats[1]], [entry_gain], inside, inside_total, ()
    )
    entry_pair = entry_pair[0]
    entry_low = grads[0].astype(jnp.bfloat16).reshape(-1, local_bottleneck)
    entry_weight_grad = contract_rows(picture.reshape(-1, channels_in), entry_low)
    picture_partial = contract_cols(entry_low, entry_full).reshape(
        count, side, side, channels_in
    )
    picture_partial = picture_partial + lax.pad(
        strided_grad, jnp.float32(0.0), ((0, 0, 0), (0, 1, 1), (0, 1, 1), (0, 0, 0))
    )

    def own_vector(value):
        return lax.psum_scatter(value, "mp", scatter_dimension=0, tiled=True)

    picture_grad = lax.all_to_all(
        picture_partial.astype(jnp.bfloat16)[None], "mp", split_axis=4, concat_axis=0, tiled=True
    ).astype(jnp.float32)
    result = lax.all_to_all(output[None], "mp", split_axis=4, concat_axis=0, tiled=True)
    return (
        result,
        picture_grad,
        own_part(entry_weight_grad, 0, 1),
        own_vector(entry_pair[0]),
        own_vector(entry_pair[1]),
        own_part(stride_weight_grad, 2, 3),
        own_vector(stride_pair[0]),
        own_vector(stride_pair[1]),
        own_part(expand_weight_grad, 1, 0),
        own_vector(expand_pair[0]),
        own_vector(expand_pair[1]),
        own_part(project_weight_grad, 0, 1),
        own_vector(project_pair[0]),
        own_vector(project_pair[1]),
        own_part(squeeze_grad, 1, 0),
        lax.psum(squeeze_bias_total, "mp"),
        own_part(excite_grad, 0, 1),
        own_vector(excite_bias_total),
        own_part(reduce_weight_grad, 0, 1),
        own_vector(reduce_pair[0]),
        own_vector(reduce_pair[1]),
        own_part(spatial_weight_grad, 2, 3),
        own_vector(spatial_pair[0]),
        own_vector(spatial_pair[1]),
        own_part(widen_weight_grad, 1, 0),
        own_vector(widen_pair[0]),
        own_vector(widen_pair[1]),
        own_part(shrink_grad, 1, 0),
        lax.psum(shrink_bias_total, "mp"),
        own_part(gating_grad, 0, 1),
        own_vector(gating_bias_total),
    )


def solution(mesh):
    in_specs = (
        P(None, "dp", None, None, None),
        P(None, "dp", None),
        P("dp", "mp"),
        P("mp"),
        P("mp"),
        P(None, None, "dp", "mp"),
        P("mp"),
        P("mp"),
        P("mp", "dp"),
        P("mp"),
        P("mp"),
        P("dp", "mp"),
        P("mp"),
        P("mp"),
        P("mp", "dp"),
        P(),
        P("dp", "mp"),
        P("mp"),
        P("dp", "mp"),
        P("mp"),
        P("mp"),
        P(None, None, "dp", "mp"),
        P("mp"),
        P("mp"),
        P("mp", "dp"),
        P("mp"),
        P("mp"),
        P("mp", "dp"),
        P(),
        P("dp", "mp"),
        P("mp"),
        P(None, "dp", None, None, "mp"),
    )
    out_specs = (
        P(None, "dp", None, None, "mp"),
        P(None, "dp", None, None, "mp"),
        P("dp", "mp"),
        P("mp"),
        P("mp"),
        P(None, None, "dp", "mp"),
        P("mp"),
        P("mp"),
        P("mp", "dp"),
        P("mp"),
        P("mp"),
        P("dp", "mp"),
        P("mp"),
        P("mp"),
        P("mp", "dp"),
        P(),
        P("dp", "mp"),
        P("mp"),
        P("dp", "mp"),
        P("mp"),
        P("mp"),
        P(None, None, "dp", "mp"),
        P("mp"),
        P("mp"),
        P("mp", "dp"),
        P("mp"),
        P("mp"),
        P("mp", "dp"),
        P(),
        P("dp", "mp"),
        P("mp"),
    )
    shards = fused_shards if dict(mesh.shape) == {"dp": 8, "mp": 4} else plain_shards
    return jax.shard_map(shards, mesh=mesh, in_specs=in_specs, out_specs=out_specs, check_vma=False)
```
